32 devices in a mesh: dp: 16 (over z, y, x), tensor: 2 (over core).
Axes of the slice: x: 2, y: 2, z: 4, core: 2. Of those that a mesh axis runs over, the one named last changes fastest.
Arguments:
- tokens: bfloat16 [1024, 4096], P(('dp', 'tensor')), may hold values from -6 to 6
- out_grad: bfloat16 [1024, 4096], P(('dp', 'tensor')), may hold values from -6 to 6
- weight_tiles: bfloat16 [128, 3, 112, 3, 128], P('dp', None, 'tensor'), may hold values from -0.3125 to 0.3125
- tile_counts: int32 [3, 112], P(None, 'tensor'), may hold values from 1 to 3, as said below
- tile_rows: int32 [3, 112, 3], P(None, 'tensor'), may hold values from 0 to 31, as said below
Outputs:
- ffn_out: bfloat16 [1024, 4096], P(('dp', 'tensor'))
- input_grad: bfloat16 [1024, 4096], P(('dp', 'tensor'))
- tile_grad: bfloat16 [128, 3, 112, 3, 128], P('dp', None, 'tensor')
The draws below stay inside these ranges and needn't reach their ends.
Inputs may be any that keep to these rules, and one draw needn't show every extreme that they name: `tile_counts`: for each matrix and each q, the live slots of hidden blocks q * 56 to (q + 1) * 56 - 1 number at most 112 together, and for each matrix some q reaches 112. `tile_rows`: within one hidden block of one matrix the 3 feature blocks are distinct.
All inputs are finite; a program needn't handle non-finite values.
Results may differ from the reference program's by a relative error of at most 0.018.
Values may be sent and summed in bfloat16 or wider, within the bound.
No kernel may reach another device: no remote copies, remote signals or barrier semaphores. Data moves between devices by JAX's collectives and lax.ppermute only.
A program may use at most 128 MiB of HBM per device.

```python
import math
import jax
import jax.numpy as jnp
from jax import lax

D = 4096
TILE = 128
KMAX = 3
DB = 32
FB = 112
FB_DEV = 56
GROUP_ROWS = 64
TOKENS = 1024
N_DP = 16


def draw_tile_counts(key, part):

    def count_row(matrix_key):
        base_key, pick_key = jax.random.split(matrix_key)
        base_count = jax.random.randint(base_key, (FB,), 1, KMAX, dtype=jnp.int32)
        busiest = jax.random.randint(pick_key, (), 0, FB // FB_DEV, dtype=jnp.int32)
        block_ids = jnp.arange(FB, dtype=jnp.int32)
        busy_count = jnp.where(block_ids % 2 == 0, KMAX, KMAX - 2).astype(jnp.int32)
        return jnp.where(block_ids // FB_DEV == busiest, busy_count, base_count).astype(jnp.int32)
    return jnp.stack([count_row(jax.random.fold_in(key, 11 + matrix)) for matrix in range(3)])


def draw_tile_rows(key, part):
    key_list = jax.random.split(jax.random.fold_in(key, 29), 3 * FB)
    picked = jax.vmap(lambda one_key: jax.random.permutation(one_key, DB)[:KMAX])(key_list)
    return picked.reshape(3, FB, KMAX).astype(jnp.int32)


def level_of(key, dims, cuts, low, top_value):
    def one(axis_at, parts):
        heights = jax.random.uniform(jax.random.fold_in(jax.random.fold_in(key, 6), axis_at), (parts,), jnp.float32, low / len(cuts), top_value / len(cuts))
        return jnp.repeat(jnp.exp(heights), dims[axis_at] // parts).reshape((-1,) + (1,) * (len(dims) - axis_at - 1))

    factor_of = one(*cuts[0])
    for cut in cuts[1:]:
        factor_of = factor_of * one(*cut)
    return factor_of


def gaussian(rng, extent, scale, reach, cuts=(), kind=jnp.bfloat16):
    entries = jax.random.normal(rng, extent, jnp.float32) * scale
    if len(cuts) > 0:
        entries = level_of(rng, extent, cuts, -0.22, 0.18) * entries
    return jnp.clip(entries, min=-reach, max=reach).astype(kind)


def setup_inputs(seed: int = 0) -> dict:
    seeds = jax.random.split(jax.random.key(seed), 6)
    tokens = gaussian(seeds[0], (TOKENS, D), 1.0, 6.0, ((0, 32),))
    out_grad = gaussian(seeds[1], (TOKENS, D), 1.0, 6.0, ((0, 32),))
    weight_tiles = gaussian(seeds[2], (TILE, 3, FB, KMAX, TILE), (KMAX * TILE) ** -0.5, 0.3125, ((0, 16), (2, 2)))
    tile_counts = draw_tile_counts(jax.random.fold_in(seeds[5], 71), 0)
    tile_rows = draw_tile_rows(jax.random.fold_in(seeds[5], 71), 0)
    return dict(tokens=tokens, out_grad=out_grad, weight_tiles=weight_tiles, tile_counts=tile_counts, tile_rows=tile_rows)


def reference(tokens, out_grad, weight_tiles, tile_counts, tile_rows):
    highest = lax.Precision.HIGHEST
    slot_total = FB * KMAX
    tile_values = weight_tiles.reshape(TILE, 3, slot_total, TILE).astype(jnp.float32)
    live_mask = (jnp.arange(KMAX, dtype=jnp.int32)[None, None, :] < tile_counts[:, :, None]).astype(jnp.float32).reshape(3, slot_total)
    row_ids = tile_rows.reshape(3, slot_total).astype(jnp.int32)
    row_onehot = (row_ids[:, :, None] == jnp.arange(DB, dtype=jnp.int32)[None, None, :]).astype(jnp.float32) * live_mask[:, :, None]
    grad_scale = 1.0 / math.sqrt(TOKENS)

    def to_blocks(products, matrix):
        masked = products * live_mask[matrix][None, :, None]
        return lax.optimization_barrier(jnp.sum(masked.reshape(GROUP_ROWS, FB, KMAX, TILE), axis=2))

    def from_blocks(values):
        return jnp.repeat(values.astype(jnp.float32), KMAX, axis=1)

    def to_rows(products, matrix):
        return jnp.einsum('tsb,sr->trb', products, row_onehot[matrix], precision=highest)

    def group(running, group_data):
        input_rows, grad_rows = group_data
        input_blocks = input_rows.astype(jnp.float32).reshape(GROUP_ROWS, DB, TILE)
        grad_blocks = grad_rows.astype(jnp.float32).reshape(GROUP_ROWS, DB, TILE)
        gate_sel = jnp.take(input_blocks, row_ids[0], axis=1)
        up_sel = jnp.take(input_blocks, row_ids[1], axis=1)
        gate_pre = to_blocks(jnp.einsum('tsa,asb->tsb', gate_sel, tile_values[:, 0], precision=highest), 0)
        up_pre = to_blocks(jnp.einsum('tsa,asb->tsb', up_sel, tile_values[:, 1], precision=highest), 1)
        gate_sig = jax.nn.sigmoid(gate_pre)
        gate_act = gate_pre * gate_sig
        hidden = (gate_act * up_pre).astype(jnp.bfloat16)
        hidden_sel = from_blocks(hidden)
        ffn_rows = to_rows(jnp.einsum('tsa,asb->tsb', hidden_sel, tile_values[:, 2], precision=highest), 2)
        grad_sel = jnp.take(grad_blocks, row_ids[2], axis=1)
        dh_blocks = to_blocks(jnp.einsum('tsb,asb->tsa', grad_sel, tile_values[:, 2], precision=highest), 2)
        grad_gate = (dh_blocks * up_pre * gate_sig * (1.0 + gate_pre * (1.0 - gate_sig))).astype(jnp.bfloat16)
        grad_up = (dh_blocks * gate_act).astype(jnp.bfloat16)
        dgate_sel = from_blocks(grad_gate)
        dup_sel = from_blocks(grad_up)
        from_gate = to_rows(jnp.einsum('tsb,asb->tsa', dgate_sel, tile_values[:, 0], precision=highest), 0)
        from_up = to_rows(jnp.einsum('tsb,asb->tsa', dup_sel, tile_values[:, 1], precision=highest), 1)
        input_rows_grad = from_gate + from_up
        tile_terms = jnp.stack([jnp.einsum('tsa,tsb->asb', gate_sel, dgate_sel, precision=highest), jnp.einsum('tsa,tsb->asb', up_sel, dup_sel, precision=highest), jnp.einsum('tsa,tsb->asb', hidden_sel, grad_sel, precision=highest)], axis=1)
        tile_terms = tile_terms * (live_mask * grad_scale)[None, :, :, None]
        rounded = lax.optimization_barrier(tile_terms.astype(jnp.bfloat16))
        running = running + rounded.astype(jnp.float32)
        return (running, (ffn_rows.reshape(GROUP_ROWS, D).astype(jnp.bfloat16), input_rows_grad.reshape(GROUP_ROWS, D).astype(jnp.bfloat16)))
    start_sum = jnp.zeros((TILE, 3, slot_total, TILE), jnp.float32)
    group_inputs = (tokens.reshape(N_DP, GROUP_ROWS, D), out_grad.reshape(N_DP, GROUP_ROWS, D))
    total, (ffn_all, input_all) = lax.scan(group, start_sum, group_inputs)
    tile_grad = total.astype(jnp.bfloat16).reshape(TILE, 3, FB, KMAX, TILE)
    return (ffn_all.reshape(TOKENS, D), input_all.reshape(TOKENS, D), tile_grad)
```

```python
import functools
import math

import jax
import jax.numpy as jnp
from jax import lax
from jax.experimental import pallas as pl
from jax.experimental.pallas import tpu as pltpu
from jax.sharding import PartitionSpec as P

F32 = jnp.float32
BF16 = jnp.bfloat16


def swap(value, axis, stride):
    size = lax.axis_size(axis)
    return lax.ppermute(value, axis, [(at, at ^ stride) for at in range(size)])


def add(first, *others):
    total = first.astype(F32)
    for other in others:
        total = total + other.astype(F32)
    return total.astype(BF16)


def strides_of(size, unit=1):
    found = []
    step = size // 2
    while step >= 1:
        found.append(step * unit)
        step //= 2
    return found


def gather(items, axis, strides):
    for stride in strides:
        items = {**items, **{at ^ stride: swap(one, axis, stride) for at, one in items.items()}}
    return items


def scatter(items, axis, strides):
    for stride in reversed(strides):
        kept = {}
        for at, one in items.items():
            if not at & stride:
                kept[at] = add(one, swap(items[at ^ stride], axis, stride))
        items = kept
    return items


def layer(
    offsets, counts, rows, *refs, token_parts, weight_parts, slot_count, grad_scale, own_parts
):
    part_count = len(token_parts)
    token_refs, refs = refs[:part_count], refs[part_count:]
    weight_refs, refs = refs[: len(weight_parts)], refs[len(weight_parts) :]
    own_out, other_out, refs = refs[0], refs[1], refs[2:]
    grad_refs, refs = refs[: len(weight_parts)], refs[len(weight_parts) :]
    x_all, g_all, x_turned, ffn_sum, input_sum, tiles, tile_out = refs
    block = pl.program_id(0)
    own_rows = token_refs[0].shape[0] // 2
    tile = tiles.shape[1]
    features = x_all.shape[1]

    @pl.when(block == 0)
    def _():
        for at, ref in enumerate(token_refs):
            x_all[at * own_rows : (at + 1) * own_rows, :] = ref[:own_rows, :]
            g_all[at * own_rows : (at + 1) * own_rows, :] = ref[own_rows:, :]
        ffn_sum[...] = jnp.zeros_like(ffn_sum)
        input_sum[...] = jnp.zeros_like(input_sum)
        for at in range(features // tile):
            x_turned[at * tile : (at + 1) * tile, :] = x_all[:, at * tile : (at + 1) * tile].T

    for ref, (group_at, first, length) in zip(weight_refs, weight_parts):
        for at in range(length):
            offset = pl.multiple_of(offsets[group_at, first + at], ref.shape[3])
            tiles[:, pl.ds(offset, ref.shape[3]), :] = ref[at, 0].astype(F32)

    def columns(matrix, slot):
        return pl.ds(pl.multiple_of(rows[matrix, block, slot] * tile, tile), tile)

    slots = range(slot_count)
    live = [[(slot < counts[matrix, block]).astype(F32) for slot in slots] for matrix in range(3)]

    def tile_of(matrix, slot):
        return (tiles[matrix * slot_count + slot] * live[matrix][slot]).astype(BF16)

    gate_tiles = jnp.concatenate([tile_of(0, slot) for slot in slots], axis=0)
    up_tiles = jnp.concatenate([tile_of(1, slot) for slot in slots], axis=0)
    down_tiles = jnp.concatenate([tile_of(2, slot) for slot in slots], axis=1)
    gate_in = jnp.concatenate([x_all[:, columns(0, slot)] for slot in slots], axis=1)
    up_in = jnp.concatenate([x_all[:, columns(1, slot)] for slot in slots], axis=1)
    grad_in = jnp.concatenate([g_all[:, columns(2, slot)] for slot in slots], axis=1)
    dot = functools.partial(lax.dot_general, preferred_element_type=F32)
    plain = (((1,), (0,)), ((), ()))
    turned = (((1,), (1,)), ((), ()))
    gate_pre = dot(gate_in, gate_tiles, plain)
    up_pre = dot(up_in, up_tiles, plain)
    gate_sig = jax.nn.sigmoid(gate_pre)
    gate_act = gate_pre * gate_sig
    hidden = (gate_act * up_pre).astype(BF16)
    ffn = dot(hidden, down_tiles, plain)
    hidden_grad = dot(grad_in, down_tiles, turned)
    gate_grad = (hidden_grad * up_pre * gate_sig * (1.0 + gate_pre * (1.0 - gate_sig))).astype(BF16)
    up_grad = (hidden_grad * gate_act).astype(BF16)
    from_gate = dot(gate_grad, gate_tiles, turned)
    from_up = dot(up_grad, up_tiles, turned)
    for slot in slots:
        here = slice(slot * tile, (slot + 1) * tile)
        ffn_sum[:, columns(2, slot)] += ffn[:, here]
        input_sum[:, columns(0, slot)] += from_gate[:, here]
        input_sum[:, columns(1, slot)] += from_up[:, here]
    down_terms = dot(hidden.T, grad_in, plain)
    for slot in slots:
        here = slice(slot * tile, (slot + 1) * tile)
        tile_out[slot] = dot(x_turned[columns(0, slot), :], gate_grad, plain) * (
            live[0][slot] * grad_scale
        )
        tile_out[slot_count + slot] = dot(x_turned[columns(1, slot), :], up_grad, plain) * (
            live[1][slot] * grad_scale
        )
        tile_out[2 * slot_count + slot] = down_terms[:, here] * (live[2][slot] * grad_scale)
    for ref, (group_at, first, length) in zip(grad_refs, weight_parts):
        for at in range(length):
            offset = pl.multiple_of(offsets[group_at, first + at], ref.shape[3])
            ref[at, 0] = tile_out[:, pl.ds(offset, ref.shape[3]), :].astype(BF16)

    @pl.when(block == pl.num_programs(0) - 1)
    def _():
        own_at, other_at = 0, 0
        for at in range(part_count):
            source = slice(at * own_rows, (at + 1) * own_rows)
            if at in own_parts:
                ref, place = own_out, own_at
                own_at += 1
            else:
                ref, place = other_out, other_at
                other_at += 1
            ref[place, :own_rows, :] = ffn_sum[source, :].astype(BF16)
            ref[place, own_rows:, :] = input_sum[source, :].astype(BF16)


def shards(tokens, out_grad, weight_tiles, tile_counts, tile_rows):
    row_share, _, blocks_dev, slot_count, tile = weight_tiles.shape
    own_rows, features = tokens.shape
    dp_size, tensor_size = lax.axis_size("dp"), lax.axis_size("tensor")
    far = math.gcd(4, math.gcd(dp_size, blocks_dev))
    near = dp_size // far
    blocks = blocks_dev // far
    terms = 3 * slot_count
    grad_scale = 1.0 / math.sqrt(own_rows * tensor_size * dp_size)
    me = lax.axis_index("dp")
    far_at, near_at = me // near, me % near
    far_strides, near_strides = strides_of(far, near), strides_of(near)
    tensor_strides = strides_of(tensor_size)

    quarters = (
        jnp.transpose(weight_tiles, (2, 1, 3, 0, 4))
        .reshape(far, blocks, terms, row_share, tile)
    )
    held = [lax.dynamic_index_in_dim(quarters, far_at, 0, keepdims=False)]
    for at in range(1, far):
        part = lax.dynamic_index_in_dim(quarters, far_at ^ at, 0, keepdims=False)
        held.append(swap(part, "dp", at * near))
    held = jnp.stack(held)

    both = jnp.concatenate([tokens, out_grad], axis=0)
    token_items = gather({0: both}, "dp", far_strides)
    token_list, token_parts = [], []
    for at in sorted(token_items):
        spread = gather({0: token_items[at]}, "tensor", tensor_strides)
        for other in sorted(spread):
            token_parts.append((at, other))
            token_list.append(spread[other])
    half = far // 2
    split = near == 4 and far % 2 == 0
    if split:
        from_1, from_2 = swap(held, "dp", 1), swap(held, "dp", 2)
        weight_list = [
            held, from_1, from_2, swap(from_1[:half], "dp", 2), swap(from_2[half:], "dp", 1)
        ]
        weight_parts = [(0, 0, far), (1, 0, far), (2, 0, far), (3, 0, half), (3, half, half)]
    else:
        items = gather({0: held}, "dp", near_strides)
        weight_list = [items[at] for at in range(near)]
        weight_parts = [(at, 0, far) for at in range(near)]

    counts = lax.dynamic_slice_in_dim(tile_counts, far_at * blocks, blocks, 1)
    rows = lax.dynamic_slice_in_dim(tile_rows, far_at * blocks, blocks, 1)
    offsets = (
        (jnp.arange(far, dtype=jnp.int32)[None, :] ^ far_at) * near
        + (jnp.arange(near, dtype=jnp.int32)[:, None] ^ near_at)
    ) * row_share

    part_count = len(token_parts)
    group_rows = part_count * own_rows
    own_parts = tuple(at for at, (_, other) in enumerate(token_parts) if other == 0)
    other_count = part_count - len(own_parts)
    whole = lambda shape: pl.BlockSpec(shape, lambda block, *_: (0,) * len(shape))
    weight_specs = [
        pl.BlockSpec(
            (length, 1, terms, row_share, tile), lambda block, *_: (0, block, 0, 0, 0)
        )
        for _, _, length in weight_parts
    ]
    token_specs = [whole((2 * own_rows, features))] * part_count
    flops = 18 * blocks * slot_count * group_rows * tile * tile
    outs = pl.pallas_call(
        functools.partial(
            layer,
            token_parts=token_parts,
            weight_parts=weight_parts,
            slot_count=slot_count,
            grad_scale=grad_scale,
            own_parts=own_parts,
        ),
        grid_spec=pltpu.PrefetchScalarGridSpec(
            num_scalar_prefetch=3,
            grid=(blocks,),
            in_specs=token_specs + weight_specs,
            out_specs=[
                whole((len(own_parts), 2 * own_rows, features)),
                whole((other_count, 2 * own_rows, features)),
            ]
            + weight_specs,
            scratch_shapes=[
                pltpu.VMEM((group_rows, features), BF16),
                pltpu.VMEM((group_rows, features), BF16),
                pltpu.VMEM((features, group_rows), BF16),
                pltpu.VMEM((group_rows, features), F32),
                pltpu.VMEM((group_rows, features), F32),
                pltpu.VMEM((terms, tile, tile), F32),
                pltpu.VMEM((terms, tile, tile), F32),
            ],
        ),
        out_shape=[
            jax.ShapeDtypeStruct((len(own_parts), 2 * own_rows, features), BF16),
            jax.ShapeDtypeStruct((other_count, 2 * own_rows, features), BF16),
        ]
        + [
            jax.ShapeDtypeStruct((length, blocks, terms, row_share, tile), BF16)
            for _, _, length in weight_parts
        ],
        compiler_params=pltpu.CompilerParams(vmem_limit_bytes=56 * 1024 * 1024),
        cost_estimate=pl.CostEstimate(
            flops=flops, bytes_accessed=20_000_000, transcendentals=blocks * group_rows * tile
        ),
    )(offsets, counts, rows, *token_list, *weight_list)
    own_sums, other_sums, tile_terms = outs[0], outs[1], outs[2:]

    other_parts = [part for part in token_parts if part[1] != 0]
    by_part = {part: other_sums[at] for at, part in enumerate(other_parts)}
    if tensor_size == 2:
        own_sums = add(own_sums, swap(other_sums, "tensor", 1))
        sums = {at * near: own_sums[at] for at in range(far)}
    else:
        sums = {}
        for place, at in enumerate(sorted(token_items)):
            items = {0: own_sums[place]}
            items.update({other: by_part[(at, other)] for other in range(1, tensor_size)})
            sums[at] = scatter(items, "tensor", tensor_strides)[0]
    mine = scatter(sums, "dp", far_strides)[0]

    if split:
        own, to_1, to_2, to_3a, to_3b = tile_terms
        got_a, got_b = swap(to_3a, "dp", 1), swap(to_3b, "dp", 2)
        to_2 = jnp.concatenate([add(to_2[:half], got_a), to_2[half:]])
        to_1 = jnp.concatenate([to_1[:half], add(to_1[half:], got_b)])
        summed = add(own, swap(to_1, "dp", 1), swap(to_2, "dp", 2))
    else:
        summed = scatter(dict(enumerate(tile_terms)), "dp", near_strides)[0]
    back = [summed[0]] + [swap(summed[at], "dp", at * near) for at in range(1, far)]
    order = jnp.arange(far, dtype=jnp.int32) ^ far_at
    tile_grad = (
        jnp.take(jnp.stack(back), order, axis=0)
        .reshape(blocks_dev, 3, slot_count, row_share, tile)
        .transpose(3, 1, 0, 2, 4)
    )
    return mine[:own_rows], mine[own_rows:], tile_grad


def solution(mesh):
    return jax.shard_map(
        shards,
        mesh=mesh,
        in_specs=(
            P(("dp", "tensor"), None),
            P(("dp", "tensor"), None),
            P("dp", None, "tensor", None, None),
            P(None, "tensor"),
            P(None, "tensor", None),
        ),
        out_specs=(
            P(("dp", "tensor"), None),
            P(("dp", "tensor"), None),
            P("dp", None, "tensor", None, None),
        ),
        check_vma=False,
    )
```

```python
import functools
import math

import jax
import jax.numpy as jnp
from jax import lax
from jax.experimental import pallas as pl
from jax.experimental.pallas import tpu as pltpu
from jax.sharding import PartitionSpec as P

F32 = jnp.float32
BF16 = jnp.bfloat16
PLAIN = (((1,), (0,)), ((), ()))
TURNED = (((1,), (1,)), ((), ()))
PARAMS = pltpu.CompilerParams(vmem_limit_bytes=56 * 1024 * 1024)
dot = functools.partial(lax.dot_general, preferred_element_type=F32)


def swap(value, axis, stride):
    size = lax.axis_size(axis)
    return lax.ppermute(value, axis, [(at, at ^ stride) for at in range(size)])


def after(value, *others):
    return lax.optimization_barrier((value, *others))[0]


def add(first, *others):
    total = first.astype(F32)
    for other in others:
        total = total + other.astype(F32)
    return total.astype(BF16)


def strides_of(size, unit=1):
    found = []
    step = size // 2
    while step >= 1:
        found.append(step * unit)
        step //= 2
    return found


def gather(items, axis, strides):
    for stride in strides:
        items = {**items, **{at ^ stride: swap(one, axis, stride) for at, one in items.items()}}
    return items


def scatter(items, axis, strides):
    for stride in reversed(strides):
        kept = {}
        for at, one in items.items():
            if not at & stride:
                kept[at] = add(one, swap(items[at ^ stride], axis, stride))
        items = kept
    return items


def whole(shape, at=None):
    at = (0,) * len(shape) if at is None else at
    return pl.BlockSpec(shape, lambda *_: at)


def by_block(shape):
    return pl.BlockSpec((1,) + shape, lambda block, *_: (block,) + (0,) * len(shape))


def pack(block_at, firsts, tiles, *outs, blocks, slot_count):
    for at, out in enumerate(outs):
        capacity = out.shape[0] - slot_count

        def one(place, _, at=at, out=out, capacity=capacity):
            block = block_at[at, place]
            for matrix in range(3):
                first = firsts[matrix, block]
                for slot in range(slot_count):
                    out[first + slot] = tiles[(block * 3 + matrix) * slot_count + slot]
            return _

        lax.fori_loop(0, blocks, one, 0)


def unpack(home, firsts, counts, *refs, slot_count):
    out, held = refs[-2:]
    capacity = refs[0].shape[0]
    for at, ref in enumerate(refs[:-2]):
        held[at * capacity : (at + 1) * capacity] = ref[...]

    def one(block, _):
        base = home[0, block] * capacity
        for matrix in range(3):
            first = base + firsts[matrix, block]
            for slot in range(slot_count):
                value = held[first + slot].astype(F32)
                live = slot < counts[matrix, block]
                out[(block * 3 + matrix) * slot_count + slot] = jnp.where(live, value, 0.0).astype(BF16)
        return _

    lax.fori_loop(0, home.shape[1], one, 0)


def ahead(offsets, firsts, counts, rows, *refs, token_count, weight_parts, slot_count):
    token_refs, refs = refs[:token_count], refs[token_count:]
    weight_refs, refs = refs[: len(weight_parts)], refs[len(weight_parts) :]
    x_turned, whole_tiles, gate_slope, gate_act_out, hidden_out, hidden_turned = refs[:6]
    x_all, tiles = refs[6:]
    block = pl.program_id(0)
    own_rows = token_refs[0].shape[0]
    tile = tiles.shape[1]
    features = x_all.shape[1]

    @pl.when(block == 0)
    def _():
        for at, ref in enumerate(token_refs):
            x_all[at * own_rows : (at + 1) * own_rows, :] = ref[...]
        for at in range(features // tile):
            x_turned[at * tile : (at + 1) * tile, :] = x_all[:, at * tile : (at + 1) * tile].T

    for ref, (group_at, first_part, length) in zip(weight_refs, weight_parts):
        share = ref.shape[2]
        for at in range(length):
            offset = pl.multiple_of(offsets[group_at, first_part + at], share)
            for matrix in range(3):
                for slot in range(slot_count):
                    tiles[matrix * slot_count + slot, pl.ds(offset, share), :] = ref[
                        at, firsts[matrix, block] + slot
                    ].astype(F32)
    slots = range(slot_count)
    for matrix in range(3):
        for slot in slots:
            live = slot < counts[matrix, block]
            whole_tiles[0, matrix * slot_count + slot] = jnp.where(
                live, tiles[matrix * slot_count + slot], 0.0
            ).astype(BF16)

    def columns(matrix, slot):
        return pl.ds(pl.multiple_of(rows[matrix * slot_count + slot, block] * tile, tile), tile)

    gate_in = jnp.concatenate([x_all[:, columns(0, slot)] for slot in slots], axis=1)
    up_in = jnp.concatenate([x_all[:, columns(1, slot)] for slot in slots], axis=1)
    gate_tiles = whole_tiles[0, :slot_count].reshape(slot_count * tile, tile)
    up_tiles = whole_tiles[0, slot_count : 2 * slot_count].reshape(slot_count * tile, tile)
    gate_pre = dot(gate_in, gate_tiles, PLAIN)
    up_pre = dot(up_in, up_tiles, PLAIN)
    gate_sig = jax.nn.sigmoid(gate_pre)
    gate_act = gate_pre * gate_sig
    hidden = (gate_act * up_pre).astype(BF16)
    gate_slope[0] = up_pre * gate_sig * (1.0 + gate_pre * (1.0 - gate_sig))
    gate_act_out[0] = gate_act
    hidden_out[0] = hidden
    hidden_turned[0] = hidden.T


def behind(
    offsets, firsts, counts, rows, *refs, token_count, weight_parts, slot_count, grad_scale, own_parts
):
    token_refs, refs = refs[:token_count], refs[token_count:]
    x_turned, whole_tiles, gate_slope, gate_act, hidden, hidden_turned = refs[:6]
    ffn_own, ffn_other, input_own, input_other = refs[6:10]
    grad_refs, refs = refs[10 : 10 + len(weight_parts)], refs[10 + len(weight_parts) :]
    g_all, ffn_sum, input_sum, tile_out = refs
    block = pl.program_id(0)
    own_rows = token_refs[0].shape[0]
    tile = tile_out.shape[1]
    slots = range(slot_count)

    @pl.when(block == 0)
    def _():
        for at, ref in enumerate(token_refs):
            g_all[at * own_rows : (at + 1) * own_rows, :] = ref[...]
        ffn_sum[...] = jnp.zeros_like(ffn_sum)
        input_sum[...] = jnp.zeros_like(input_sum)

    def columns(matrix, slot):
        return pl.ds(pl.multiple_of(rows[matrix * slot_count + slot, block] * tile, tile), tile)

    gate_tiles = whole_tiles[0, :slot_count].reshape(slot_count * tile, tile)
    up_tiles = whole_tiles[0, slot_count : 2 * slot_count].reshape(slot_count * tile, tile)
    down_tiles = jnp.concatenate([whole_tiles[0, 2 * slot_count + slot] for slot in slots], axis=1)
    grad_in = jnp.concatenate([g_all[:, columns(2, slot)] for slot in slots], axis=1)
    hidden_grad = dot(grad_in, down_tiles, TURNED)
    ffn = dot(hidden[0], down_tiles, PLAIN)
    down_terms = dot(hidden_turned[0], grad_in, PLAIN)
    gate_grad = (hidden_grad * gate_slope[0]).astype(BF16)
    up_grad = (hidden_grad * gate_act[0]).astype(BF16)
    from_gate = dot(gate_grad, gate_tiles, TURNED)
    from_up = dot(up_grad, up_tiles, TURNED)
    for slot in slots:
        here = slice(slot * tile, (slot + 1) * tile)
        ffn_sum[:, columns(2, slot)] += ffn[:, here]
        input_sum[:, columns(0, slot)] += from_gate[:, here]
        input_sum[:, columns(1, slot)] += from_up[:, here]
        tile_out[slot] = dot(x_turned[columns(0, slot), :], gate_grad, PLAIN) * grad_scale
        tile_out[slot_count + slot] = dot(x_turned[columns(1, slot), :], up_grad, PLAIN) * grad_scale
        tile_out[2 * slot_count + slot] = down_terms[:, here] * grad_scale
    for matrix in range(3):
        for slot in slots:

            def store(matrix=matrix, slot=slot):
                for ref, (group_at, first_part, length) in zip(grad_refs, weight_parts):
                    share = ref.shape[2]
                    for at in range(length):
                        offset = pl.multiple_of(offsets[group_at, first_part + at], share)
                        ref[at, firsts[matrix, block] + slot] = tile_out[
                            matrix * slot_count + slot, pl.ds(offset, share), :
                        ].astype(BF16)

            pl.when(slot < counts[matrix, block])(store)

    @pl.when(block == pl.num_programs(0) - 1)
    def _():
        own_at, other_at = 0, 0
        for at in range(token_count):
            source = slice(at * own_rows, (at + 1) * own_rows)
            if at in own_parts:
                ffn_own[own_at] = ffn_sum[source, :].astype(BF16)
                input_own[own_at] = input_sum[source, :].astype(BF16)
                own_at += 1
            else:
                ffn_other[other_at] = ffn_sum[source, :].astype(BF16)
                input_other[other_at] = input_sum[source, :].astype(BF16)
                other_at += 1


def shards(tokens, out_grad, weight_tiles, tile_counts, tile_rows):
    row_share, _, blocks_dev, slot_count, tile = weight_tiles.shape
    own_rows, features = tokens.shape
    dp_size, tensor_size = lax.axis_size("dp"), lax.axis_size("tensor")
    far = math.gcd(4, math.gcd(dp_size, blocks_dev))
    near = dp_size // far
    blocks = blocks_dev // far
    terms = 3 * slot_count
    grad_scale = 1.0 / math.sqrt(own_rows * tensor_size * dp_size)
    me = lax.axis_index("dp")
    far_at, near_at = me // near, me % near
    far_strides, near_strides = strides_of(far, near), strides_of(near)
    tensor_strides = strides_of(tensor_size)

    capacity = (terms * blocks_dev - 3 * blocks_dev + 3 * (slot_count - 1) * (far - 1)) // far
    buffer = capacity + slot_count
    block_ids = jnp.arange(blocks_dev, dtype=jnp.int32)
    load = jnp.sum(tile_counts, axis=0)
    earlier = (load[:, None] > load[None, :]) | (
        (load[:, None] == load[None, :]) & (block_ids[:, None] < block_ids[None, :])
    )
    rank = jnp.sum(earlier.astype(jnp.int32), axis=0)
    home = rank % far
    before = (home[:, None] == home[None, :]) & (rank[:, None] < rank[None, :])
    start = jnp.sum(jnp.where(before, load[:, None], 0), axis=0)
    firsts = start[None, :] + jnp.concatenate(
        [jnp.zeros_like(tile_counts[:1]), tile_counts[:1], tile_counts[:1] + tile_counts[1:2]]
    )
    ranks_of = (
        jnp.arange(blocks, dtype=jnp.int32)[None, :] * far
        + (jnp.arange(far, dtype=jnp.int32)[:, None] ^ far_at)
    )
    block_at = jnp.sum(
        jnp.where(ranks_of[:, :, None] == rank[None, None, :], block_ids[None, None, :], 0), axis=2
    )
    table = jnp.concatenate(
        [firsts, tile_counts, jnp.transpose(tile_rows, (0, 2, 1)).reshape(terms, blocks_dev)]
    )
    own = jnp.sum(
        jnp.where(ranks_of[0][None, :, None] == rank[None, None, :], table[:, None, :], 0), axis=2
    )
    own_firsts, own_counts, own_cols = own[:3], own[3:6], own[6:]
    offsets = (
        (jnp.arange(far, dtype=jnp.int32)[None, :] ^ far_at) * near
        + (jnp.arange(near, dtype=jnp.int32)[:, None] ^ near_at)
    ) * row_share

    tile_list = jnp.transpose(weight_tiles, (2, 1, 3, 0, 4)).reshape(
        blocks_dev * terms, row_share, tile
    )
    packed_shape = (buffer, row_share, tile)
    packed = pl.pallas_call(
        functools.partial(pack, blocks=blocks, slot_count=slot_count),
        grid_spec=pltpu.PrefetchScalarGridSpec(
            num_scalar_prefetch=2,
            grid=(1,),
            in_specs=[whole(tile_list.shape)],
            out_specs=[whole(packed_shape)] * far,
        ),
        out_shape=[jax.ShapeDtypeStruct(packed_shape, BF16)] * far,
        compiler_params=PARAMS,
    )(block_at, firsts, tile_list)
    both = jnp.concatenate([tokens, out_grad], axis=0)
    early = {0: both}
    if far > 1:
        early[near] = swap(both, "dp", near)
    received = [swap(packed[at], "dp", at * near) for at in reversed(range(1, far))][::-1]
    held = jnp.stack([packed[0], *received])

    late_x, late_g = {}, {}
    for stride in far_strides[:-1]:
        x_source, g_source = after((tokens, out_grad), held)
        late_x[stride] = swap(x_source, "dp", stride)
        late_x[stride ^ near] = swap(late_x[stride], "dp", near)
        late_g[stride] = swap(after(g_source, late_x[stride]), "dp", stride)
        late_g[stride ^ near] = swap(late_g[stride], "dp", near)

    half = far // 2
    split = near == 4 and far % 2 == 0
    if split:
        from_1, from_2 = swap(held, "dp", 1), swap(held, "dp", 2)
        weight_list = [
            held, from_1, from_2, swap(from_1[:half], "dp", 2), swap(from_2[half:], "dp", 1)
        ]
        weight_parts = [(0, 0, far), (1, 0, far), (2, 0, far), (3, 0, half), (3, half, half)]
    else:
        items = gather({0: held}, "dp", near_strides)
        weight_list = [items[at] for at in range(near)]
        weight_parts = [(at, 0, far) for at in range(near)]

    far_order = [at * near for at in range(0, far, 2)] + [at * near for at in range(1, far, 2)]
    x_list, g_list, x_specs, g_specs, token_parts = [], [], [], [], []
    token_shape = (own_rows, features)
    for at in far_order:
        if at in early:
            for other, part in gather({0: early[at]}, "tensor", tensor_strides).items():
                token_parts.append((at, other))
                x_list.append(part)
                g_list.append(part)
                x_specs.append(whole(token_shape))
                g_specs.append(whole(token_shape, (1, 0)))
        else:
            x_parts = gather({0: late_x[at]}, "tensor", tensor_strides)
            g_parts = gather({0: late_g[at]}, "tensor", tensor_strides)
            for other in x_parts:
                token_parts.append((at, other))
                x_list.append(x_parts[other])
                g_list.append(g_parts[other])
                x_specs.append(whole(token_shape))
                g_specs.append(whole(token_shape))

    token_count = len(token_parts)
    group_rows = token_count * own_rows
    own_parts = tuple(at for at, (_, other) in enumerate(token_parts) if other == 0)
    other_parts = [part for part in token_parts if part[1] != 0]
    weight_specs = [whole((length,) + packed_shape) for _, _, length in weight_parts]
    middle_specs = [
        whole((features, group_rows)),
        by_block((terms, tile, tile)),
        by_block((group_rows, tile)),
        by_block((group_rows, tile)),
        by_block((group_rows, tile)),
        by_block((tile, group_rows)),
    ]
    middle_shapes = [
        jax.ShapeDtypeStruct((features, group_rows), BF16),
        jax.ShapeDtypeStruct((blocks, terms, tile, tile), BF16),
        jax.ShapeDtypeStruct((blocks, group_rows, tile), F32),
        jax.ShapeDtypeStruct((blocks, group_rows, tile), F32),
        jax.ShapeDtypeStruct((blocks, group_rows, tile), BF16),
        jax.ShapeDtypeStruct((blocks, tile, group_rows), BF16),
    ]
    flops = 2 * blocks * slot_count * group_rows * tile * tile
    middle = pl.pallas_call(
        functools.partial(
            ahead, token_count=token_count, weight_parts=weight_parts, slot_count=slot_count
        ),
        grid_spec=pltpu.PrefetchScalarGridSpec(
            num_scalar_prefetch=4,
            grid=(blocks,),
            in_specs=x_specs + weight_specs,
            out_specs=middle_specs,
            scratch_shapes=[
                pltpu.VMEM((group_rows, features), BF16),
                pltpu.VMEM((terms, tile, tile), F32),
            ],
        ),
        out_shape=middle_shapes,
        compiler_params=PARAMS,
        cost_estimate=pl.CostEstimate(
            flops=2 * flops, bytes_accessed=16_000_000, transcendentals=blocks * group_rows * tile
        ),
    )(offsets, own_firsts, own_counts, own_cols, *x_list, *weight_list)
    own_shape = (len(own_parts), own_rows, features)
    other_shape = (len(other_parts), own_rows, features)
    outs = pl.pallas_call(
        functools.partial(
            behind,
            token_count=token_count,
            weight_parts=weight_parts,
            slot_count=slot_count,
            grad_scale=grad_scale,
            own_parts=own_parts,
        ),
        grid_spec=pltpu.PrefetchScalarGridSpec(
            num_scalar_prefetch=4,
            grid=(blocks,),
            in_specs=g_specs + middle_specs,
            out_specs=[whole(own_shape), whole(other_shape)] * 2 + weight_specs,
            scratch_shapes=[
                pltpu.VMEM((group_rows, features), BF16),
                pltpu.VMEM((group_rows, features), F32),
                pltpu.VMEM((group_rows, features), F32),
                pltpu.VMEM((terms, tile, tile), F32),
            ],
        ),
        out_shape=[
            jax.ShapeDtypeStruct(own_shape, BF16),
            jax.ShapeDtypeStruct(other_shape, BF16),
        ]
        * 2
        + [
            jax.ShapeDtypeStruct((length,) + packed_shape, BF16) for _, _, length in weight_parts
        ],
        compiler_params=PARAMS,
        cost_estimate=pl.CostEstimate(
            flops=7 * flops, bytes_accessed=25_000_000, transcendentals=0
        ),
    )(offsets, own_firsts, own_counts, own_cols, *g_list, *middle)
    tile_terms = outs[4:]

    def finish(own_sums, other_sums):
        if tensor_size == 2 and far == 4:
            from_core = swap(other_sums, "tensor", 1)
            got = swap(add(own_sums[2:], from_core[2:]), "dp", near)
            last = swap(add(own_sums[1], from_core[1], got[1]), "dp", 2 * near)
            return add(own_sums[0], from_core[0], got[0], last)
        sums = {}
        for place, at in enumerate(far_order):
            items = {0: own_sums[place]}
            for index, (far_part, other) in enumerate(other_parts):
                if far_part == at:
                    items[other] = other_sums[index]
            sums[at] = scatter(items, "tensor", tensor_strides)[0]
        return scatter(sums, "dp", far_strides)[0]

    ffn_rows = finish(outs[0], outs[1])
    input_rows = finish(outs[2], outs[3])

    if split:
        own, to_1, to_2, to_3a, to_3b = tile_terms
        got_a, got_b = swap(to_3a, "dp", 1), swap(to_3b, "dp", 2)
        to_2 = jnp.concatenate([add(to_2[:half], got_a), to_2[half:]])
        to_1 = jnp.concatenate([to_1[:half], add(to_1[half:], got_b)])
        from_1, from_2 = swap(to_1, "dp", 1), swap(to_2, "dp", 2)
        summed = [add(own[at], from_1[at], from_2[at]) for at in range(far)]
    else:
        summed = scatter(dict(enumerate(tile_terms)), "dp", near_strides)[0]
    back = [summed[0]] + [swap(summed[at], "dp", at * near) for at in range(1, far)]
    grads = pl.pallas_call(
        functools.partial(unpack, slot_count=slot_count),
        grid_spec=pltpu.PrefetchScalarGridSpec(
            num_scalar_prefetch=3,
            grid=(1,),
            in_specs=[whole(packed_shape)] * far,
            out_specs=whole(tile_list.shape),
            scratch_shapes=[pltpu.VMEM((far * buffer, row_share, tile), BF16)],
        ),
        out_shape=jax.ShapeDtypeStruct(tile_list.shape, BF16),
        compiler_params=PARAMS,
    )((home ^ far_at)[None, :], firsts, tile_counts, *back)
    tile_grad = grads.reshape(blocks_dev, 3, slot_count, row_share, tile).transpose(3, 1, 0, 2, 4)
    return ffn_rows, input_rows, tile_grad


def solution(mesh):
    return jax.shard_map(
        shards,
        mesh=mesh,
        in_specs=(
            P(("dp", "tensor"), None),
            P(("dp", "tensor"), None),
            P("dp", None, "tensor", None, None),
            P(None, "tensor"),
            P(None, "tensor", None),
        ),
        out_specs=(
            P(("dp", "tensor"), None),
            P(("dp", "tensor"), None),
            P("dp", None, "tensor", None, None),
        ),
        check_vma=False,
    )
```

```python
import functools
import math

import jax
import jax.numpy as jnp
from jax import lax
from jax.experimental import pallas as pl
from jax.experimental.pallas import tpu as pltpu
from jax.sharding import PartitionSpec as P

F32 = jnp.float32
BF16 = jnp.bfloat16
PLAIN = (((1,), (0,)), ((), ()))
TURNED = (((1,), (1,)), ((), ()))
PARAMS = pltpu.CompilerParams(vmem_limit_bytes=56 * 1024 * 1024)
dot = functools.partial(lax.dot_general, preferred_element_type=F32)


def swap(value, axis, stride):
    size = lax.axis_size(axis)
    return lax.ppermute(value, axis, [(at, at ^ stride) for at in range(size)])


def after(value, *others):
    return lax.optimization_barrier((value, *others))[0]


def add(first, *others):
    total = first.astype(F32)
    for other in others:
        total = total + other.astype(F32)
    return total.astype(BF16)


def strides_of(size, unit=1):
    found = []
    step = size // 2
    while step >= 1:
        found.append(step * unit)
        step //= 2
    return found


def gather(items, axis, strides):
    for stride in strides:
        items = {**items, **{at ^ stride: swap(one, axis, stride) for at, one in items.items()}}
    return items


def scatter(items, axis, strides):
    for stride in reversed(strides):
        kept = {}
        for at, one in items.items():
            if not at & stride:
                kept[at] = add(one, swap(items[at ^ stride], axis, stride))
        items = kept
    return items


def whole(shape, at=None):
    at = (0,) * len(shape) if at is None else at
    return pl.BlockSpec(shape, lambda *_: at)


def by_block(shape):
    return pl.BlockSpec((1,) + shape, lambda block, *_: (block,) + (0,) * len(shape))


def pack(table, tiles, *outs, blocks, slot_count):
    spare = outs[0].shape[0] - 1
    for at, out in enumerate(outs):

        def one(place, _, at=at, out=out):
            column = at * blocks + place
            block = table[0, column]
            for matrix in range(3):
                first, count = table[1 + matrix, column], table[4 + matrix, column]
                for slot in range(slot_count):
                    to = jnp.where(slot < count, first + slot, spare)
                    out[to] = tiles[(block * 3 + matrix) * slot_count + slot]
            return _

        lax.fori_loop(0, blocks, one, 0)


def unpack(table, *refs, chunks, chunk_rows, blocks, slot_count):
    out, sources = refs[-1], refs[:-1]
    far = len(sources) // chunks
    chunk_blocks = blocks // chunks
    for chunk in range(chunks):
        for at in range(far):
            ref = sources[chunk * far + at]

            def one(place, _, at=at, ref=ref, chunk=chunk):
                column = at * blocks + chunk * chunk_blocks + place
                block = table[0, column]
                for matrix in range(3):
                    first = table[1 + matrix, column] - chunk * chunk_rows
                    count = table[4 + matrix, column]
                    for slot in range(slot_count):
                        live = slot < count
                        value = ref[jnp.where(live, first + slot, 0)].astype(F32)
                        out[(block * 3 + matrix) * slot_count + slot] = jnp.where(
                            live, value, 0.0
                        ).astype(BF16)
                return _

            lax.fori_loop(0, chunk_blocks, one, 0)


def offset_of(table, part, at, near, share):
    far_part = (part[1] + at) ^ table[16, 0]
    near_part = part[0] ^ table[16, 1]
    return pl.multiple_of((far_part * near + near_part) * share, share)


def assemble(table, *refs, weight_parts, slot_count, near):
    weight_refs, whole_tiles, tiles = refs[: len(weight_parts)], refs[-2], refs[-1]
    block = pl.program_id(0)
    spare = weight_refs[0].shape[1] - 1
    places = []
    for matrix in range(3):
        first, count = table[1 + matrix, block], table[4 + matrix, block]
        places += [jnp.where(slot < count, first + slot, spare) for slot in range(slot_count)]
    for ref, part in zip(weight_refs, weight_parts):
        share = ref.shape[2]
        for at in range(part[2]):
            offset = offset_of(table, part, at, near, share)
            for index, place in enumerate(places):
                tiles[index, pl.ds(offset, share), :] = ref[at, place].astype(F32)
    for index, place in enumerate(places):
        whole_tiles[0, index] = jnp.where(place != spare, tiles[index], 0.0).astype(BF16)


def store_parts(total, own, other, token_count, own_parts):
    own_rows = own.shape[1]
    own_at, other_at = 0, 0
    for at in range(token_count):
        value = total[at * own_rows : (at + 1) * own_rows, :].astype(BF16)
        if at in own_parts:
            own[own_at] = value
            own_at += 1
        else:
            other[other_at] = value
            other_at += 1


def tokens_at(refs, columns):
    return jnp.concatenate([ref[:, columns] for ref in refs], axis=0)


def ahead(table, *refs, token_count, slot_count, own_parts):
    token_refs, refs = refs[:token_count], refs[token_count:]
    whole_tiles, x_turned, gate_slope, gate_act_out, hidden_turned, ffn_own, ffn_other = refs[:7]
    ffn_sum = refs[7]
    block = pl.program_id(0)
    tile = whole_tiles.shape[3]
    slots = range(slot_count)

    @pl.when(block == 0)
    def _():
        for at in range(x_turned.shape[0] // tile):
            here = slice(at * tile, (at + 1) * tile)
            x_turned[here, :] = tokens_at(token_refs, here).T
        ffn_sum[...] = jnp.zeros_like(ffn_sum)

    def columns(matrix, slot):
        return pl.ds(pl.multiple_of(table[7 + matrix * slot_count + slot, block] * tile, tile), tile)

    gate_in = jnp.concatenate([tokens_at(token_refs, columns(0, slot)) for slot in slots], axis=1)
    up_in = jnp.concatenate([tokens_at(token_refs, columns(1, slot)) for slot in slots], axis=1)
    gate_tiles = whole_tiles[0, :slot_count].reshape(slot_count * tile, tile)
    up_tiles = whole_tiles[0, slot_count : 2 * slot_count].reshape(slot_count * tile, tile)
    down_tiles = jnp.concatenate([whole_tiles[0, 2 * slot_count + slot] for slot in slots], axis=1)
    gate_pre = dot(gate_in, gate_tiles, PLAIN)
    up_pre = dot(up_in, up_tiles, PLAIN)
    gate_sig = jax.nn.sigmoid(gate_pre)
    gate_act = gate_pre * gate_sig
    hidden = (gate_act * up_pre).astype(BF16)
    gate_slope[0] = up_pre * gate_sig * (1.0 + gate_pre * (1.0 - gate_sig))
    gate_act_out[0] = gate_act
    hidden_turned[0] = hidden.T
    ffn = dot(hidden, down_tiles, PLAIN)
    for slot in slots:
        ffn_sum[:, columns(2, slot)] += ffn[:, slot * tile : (slot + 1) * tile]

    @pl.when(block == pl.num_programs(0) - 1)
    def _():
        store_parts(ffn_sum, ffn_own, ffn_other, token_count, own_parts)


def behind(
    table, *refs, token_count, weight_parts, slot_count, grad_scale, own_parts, near, chunk, chunks,
    chunk_rows,
):
    token_refs, refs = refs[:token_count], refs[token_count:]
    whole_tiles, x_turned, gate_slope, gate_act, hidden_turned = refs[:5]
    refs = refs[5:]
    if chunk > 0:
        carried, refs = refs[0], refs[1:]
    if chunk < chunks - 1:
        carry, refs = refs[0], refs[1:]
    else:
        input_own, input_other, refs = refs[0], refs[1], refs[2:]
    grad_refs, refs = refs[: len(weight_parts)], refs[len(weight_parts) :]
    input_sum, tile_out = refs
    step = pl.program_id(0)
    block = step + chunk * pl.num_programs(0)
    tile = tile_out.shape[1]
    slots = range(slot_count)

    @pl.when(step == 0)
    def _():
        input_sum[...] = carried[...] if chunk > 0 else jnp.zeros_like(input_sum)

    def columns(matrix, slot):
        return pl.ds(pl.multiple_of(table[7 + matrix * slot_count + slot, block] * tile, tile), tile)

    gate_tiles = whole_tiles[0, :slot_count].reshape(slot_count * tile, tile)
    up_tiles = whole_tiles[0, slot_count : 2 * slot_count].reshape(slot_count * tile, tile)
    down_tiles = jnp.concatenate([whole_tiles[0, 2 * slot_count + slot] for slot in slots], axis=1)
    grad_in = jnp.concatenate([tokens_at(token_refs, columns(2, slot)) for slot in slots], axis=1)
    hidden_grad = dot(grad_in, down_tiles, TURNED)
    down_terms = dot(hidden_turned[0], grad_in, PLAIN)
    gate_grad = (hidden_grad * gate_slope[0]).astype(BF16)
    up_grad = (hidden_grad * gate_act[0]).astype(BF16)
    from_gate = dot(gate_grad, gate_tiles, TURNED)
    from_up = dot(up_grad, up_tiles, TURNED)
    for slot in slots:
        here = slice(slot * tile, (slot + 1) * tile)
        input_sum[:, columns(0, slot)] += from_gate[:, here]
        input_sum[:, columns(1, slot)] += from_up[:, here]
        tile_out[slot] = dot(x_turned[columns(0, slot), :], gate_grad, PLAIN) * grad_scale
        tile_out[slot_count + slot] = dot(x_turned[columns(1, slot), :], up_grad, PLAIN) * grad_scale
        tile_out[2 * slot_count + slot] = down_terms[:, here] * grad_scale
    spare = grad_refs[0].shape[1] - 1
    places = []
    for matrix in range(3):
        first, count = table[1 + matrix, block] - chunk * chunk_rows, table[4 + matrix, block]
        places += [jnp.where(slot < count, first + slot, spare) for slot in slots]
    for ref, part in zip(grad_refs, weight_parts):
        share = ref.shape[2]
        for at in range(part[2]):
            offset = offset_of(table, part, at, near, share)
            for index, place in enumerate(places):
                ref[at, place] = tile_out[index, pl.ds(offset, share), :].astype(BF16)

    @pl.when(step == pl.num_programs(0) - 1)
    def _():
        if chunk < chunks - 1:
            carry[...] = input_sum[...]
        else:
            store_parts(input_sum, input_own, input_other, token_count, own_parts)


def call(kernel, table, args, in_specs, out_specs, out_shape, grid=1, scratch=(), cost=0):
    return pl.pallas_call(
        kernel,
        grid_spec=pltpu.PrefetchScalarGridSpec(
            num_scalar_prefetch=1,
            grid=(grid,),
            in_specs=in_specs,
            out_specs=out_specs,
            scratch_shapes=scratch,
        ),
        out_shape=out_shape,
        compiler_params=PARAMS,
        cost_estimate=pl.CostEstimate(flops=0, bytes_accessed=cost, transcendentals=0),
    )(table, *args)


def shards(tokens, out_grad, weight_tiles, tile_counts, tile_rows):
    row_share, _, blocks_dev, slot_count, tile = weight_tiles.shape
    own_rows, features = tokens.shape
    dp_size, tensor_size = lax.axis_size("dp"), lax.axis_size("tensor")
    far = math.gcd(4, math.gcd(dp_size, blocks_dev))
    near = dp_size // far
    blocks = blocks_dev // far
    chunks = math.gcd(2, blocks)
    chunk_blocks = blocks // chunks
    groups = far * chunks
    terms = 3 * slot_count
    grad_scale = 1.0 / math.sqrt(own_rows * tensor_size * dp_size)
    me = lax.axis_index("dp")
    far_at, near_at = me // near, me % near
    far_strides, near_strides = strides_of(far, near), strides_of(near)
    tensor_strides = strides_of(tensor_size)
    shape = jax.ShapeDtypeStruct

    both = jnp.concatenate([tokens, out_grad], axis=0)
    early = {0: both}
    if far > 1:
        early[near] = swap(both, "dp", near)

    capacity = (terms * blocks_dev - 3 * blocks_dev + 3 * (slot_count - 1) * (groups - 1)) // groups
    chunk_rows = capacity + 1
    block_ids = jnp.arange(blocks_dev, dtype=jnp.int32)
    load = tile_counts[0] + tile_counts[1] + tile_counts[2]
    earlier = (load[:, None] > load[None, :]) | (
        (load[:, None] == load[None, :]) & (block_ids[:, None] < block_ids[None, :])
    )
    rank = jnp.sum(earlier.astype(jnp.int32), axis=0)
    group = rank % groups
    before = (group[:, None] == group[None, :]) & (rank[:, None] < rank[None, :])
    start = jnp.sum(jnp.where(before, load[:, None], 0), axis=0) + (group // far) * chunk_rows
    ranks_of = (
        jnp.arange(chunk_blocks, dtype=jnp.int32)[None, None, :] * groups
        + jnp.arange(chunks, dtype=jnp.int32)[None, :, None] * far
        + (jnp.arange(far, dtype=jnp.int32)[:, None, None] ^ far_at)
    ).reshape(blocks_dev)
    columns = jnp.concatenate(
        [
            block_ids[None, :],
            start[None, :],
            (start + tile_counts[0])[None, :],
            (start + tile_counts[0] + tile_counts[1])[None, :],
            tile_counts,
            jnp.transpose(tile_rows, (0, 2, 1)).reshape(terms, blocks_dev),
        ]
    )
    table = jnp.sum(
        jnp.where(ranks_of[None, :, None] == rank[None, None, :], columns[:, None, :], 0), axis=2
    )
    place = jnp.where(block_ids == 0, far_at, near_at).astype(jnp.int32)
    table = jnp.concatenate([table, place[None, :]])

    tile_list = jnp.transpose(weight_tiles, (2, 1, 3, 0, 4)).reshape(
        blocks_dev * terms, row_share, tile
    )
    packed_shape = (chunks * chunk_rows, row_share, tile)
    chunk_shape = (chunk_rows, row_share, tile)
    packed = call(
        functools.partial(pack, blocks=blocks, slot_count=slot_count),
        table,
        [tile_list],
        [whole(tile_list.shape)],
        [whole(packed_shape)] * far,
        [shape(packed_shape, BF16)] * far,
        cost=100_000_000,
    )
    received = [swap(packed[at], "dp", at * near) for at in reversed(range(1, far))][::-1]
    held = jnp.stack([packed[0], *received])

    half = far // 2
    split = near == 4 and far % 2 == 0
    if split:
        from_1, from_2 = swap(held, "dp", 1), swap(held, "dp", 2)
        pass_1, pass_2 = from_1[:half], from_2[half:]
        weight_list = [held, from_1, from_2, swap(pass_1, "dp", 2), swap(pass_2, "dp", 1)]
        weight_parts = [(0, 0, far), (1, 0, far), (2, 0, far), (3, 0, half), (3, half, half)]
    else:
        items = gather({0: held}, "dp", near_strides)
        pass_1 = pass_2 = held
        weight_list = [items[at] for at in range(near)]
        weight_parts = [(at, 0, far) for at in range(near)]

    late_x, late_g = {}, {}
    for stride in far_strides[:-1]:
        x_source, g_source = after((tokens, out_grad), held)
        late_x[stride] = swap(x_source, "dp", stride)
        x_back, g_source = after((late_x[stride], g_source), pass_1, pass_2, late_x[stride])
        late_x[stride ^ near] = swap(x_back, "dp", near)
        late_g[stride] = swap(g_source, "dp", stride)
        late_g[stride ^ near] = swap(late_g[stride], "dp", near)

    far_order = [at * near for at in range(0, far, 2)] + [at * near for at in range(1, far, 2)]
    x_list, g_list, x_specs, g_specs, token_parts = [], [], [], [], []
    token_shape = (own_rows, features)
    for at in far_order:
        if at in early:
            for other, part in gather({0: early[at]}, "tensor", tensor_strides).items():
                token_parts.append((at, other))
                x_list.append(part)
                g_list.append(part)
                x_specs.append(whole(token_shape))
                g_specs.append(whole(token_shape, (1, 0)))
        else:
            x_parts = gather({0: late_x[at]}, "tensor", tensor_strides)
            g_parts = gather({0: late_g[at]}, "tensor", tensor_strides)
            for other in x_parts:
                token_parts.append((at, other))
                x_list.append(x_parts[other])
                g_list.append(g_parts[other])
                x_specs.append(whole(token_shape))
                g_specs.append(whole(token_shape))

    token_count = len(token_parts)
    group_rows = token_count * own_rows
    own_parts = tuple(at for at, (_, other) in enumerate(token_parts) if other == 0)
    other_parts = [part for part in token_parts if part[1] != 0]
    own_shape = (len(own_parts), own_rows, features)
    other_shape = (len(other_parts), own_rows, features)

    if far == 4:
        weight_list = list(after(tuple(weight_list), *late_x.values()))
    whole_tiles = call(
        functools.partial(assemble, weight_parts=weight_parts, slot_count=slot_count, near=near),
        table,
        weight_list,
        [whole((length,) + packed_shape) for _, _, length in weight_parts],
        by_block((terms, tile, tile)),
        shape((blocks, terms, tile, tile), BF16),
        grid=blocks,
        scratch=[pltpu.VMEM((terms, tile, tile), F32)],
        cost=20_000_000,
    )
    if far == 4:
        x_list = list(after(tuple(x_list), late_g[far_strides[0]]))
    x_turned, gate_slope, gate_act, hidden_turned, ffn_own, ffn_other = call(
        functools.partial(
            ahead, token_count=token_count, slot_count=slot_count, own_parts=own_parts
        ),
        table,
        [*x_list, whole_tiles],
        x_specs + [by_block((terms, tile, tile))],
        [
            whole((features, group_rows)),
            by_block((group_rows, tile)),
            by_block((group_rows, tile)),
            by_block((tile, group_rows)),
            whole(own_shape),
            whole(other_shape),
        ],
        [
            shape((features, group_rows), BF16),
            shape((blocks, group_rows, tile), F32),
            shape((blocks, group_rows, tile), F32),
            shape((blocks, tile, group_rows), BF16),
            shape(own_shape, BF16),
            shape(other_shape, BF16),
        ],
        grid=blocks,
        scratch=[pltpu.VMEM((group_rows, features), F32)],
        cost=40_000_000,
    )

    def to_near(own_sums, other_sums):
        from_core = swap(other_sums, "tensor", 1)
        return from_core, add(own_sums[half:], from_core[half:])

    def to_far(own_sums, from_core, got):
        return add(own_sums[1], from_core[1], got[1])

    def generic(own_sums, other_sums):
        sums = {}
        for index, at in enumerate(far_order):
            items = {0: own_sums[index]}
            for other_index, (far_part, other) in enumerate(other_parts):
                if far_part == at:
                    items[other] = other_sums[other_index]
            sums[at] = scatter(items, "tensor", tensor_strides)[0]
        return scatter(sums, "dp", far_strides)[0]

    staged = tensor_size == 2 and far == 4 and split and chunks == 2
    if staged:
        ffn_core, ffn_near = to_near(ffn_own, ffn_other)

    def gradients(chunk, carried):
        def block_at(block_shape):
            return pl.BlockSpec(
                (1,) + block_shape,
                lambda block, *_: (block + chunk * chunk_blocks,) + (0,) * len(block_shape),
            )

        last = chunk == chunks - 1
        sum_shape = (group_rows, features)
        return call(
            functools.partial(
                behind,
                token_count=token_count,
                weight_parts=weight_parts,
                slot_count=slot_count,
                grad_scale=grad_scale,
                own_parts=own_parts,
                near=near,
                chunk=chunk,
                chunks=chunks,
                chunk_rows=chunk_rows,
            ),
            table,
            [*g_list, whole_tiles, x_turned, gate_slope, gate_act, hidden_turned, *carried],
            g_specs
            + [
                block_at((terms, tile, tile)),
                whole((features, group_rows)),
                block_at((group_rows, tile)),
                block_at((group_rows, tile)),
                block_at((tile, group_rows)),
            ]
            + [whole(sum_shape)] * len(carried),
            ([whole(own_shape), whole(other_shape)] if last else [whole(sum_shape)])
            + [whole((length,) + chunk_shape) for _, _, length in weight_parts],
            ([shape(own_shape, BF16), shape(other_shape, BF16)] if last else [shape(sum_shape, F32)])
            + [shape((length,) + chunk_shape, BF16) for _, _, length in weight_parts],
            grid=chunk_blocks,
            scratch=[
                pltpu.VMEM((group_rows, features), F32),
                pltpu.VMEM((terms, tile, tile), F32),
            ],
            cost=40_000_000,
        )

    def halves(parts):
        return swap(parts[3], "dp", 1), swap(parts[4], "dp", 2)

    def folded(parts, got_1, got_2):
        to_2 = jnp.concatenate([add(parts[2][:half], got_1), parts[2][half:]])
        to_1 = jnp.concatenate([parts[1][:half], add(parts[1][half:], got_2)])
        return to_1, to_2

    def summed(parts, to_1, to_2):
        from_1, from_2 = swap(to_1, "dp", 1), swap(to_2, "dp", 2)
        return [add(parts[0][at], from_1[at], from_2[at]) for at in range(far)]

    def sent_back(sums):
        return [sums[0]] + [swap(sums[at], "dp", at * near) for at in range(1, far)]

    if staged:
        carry, *first_parts = gradients(0, [])
        first_got = halves(first_parts)
        carry = after(carry, ffn_near)
        input_own, input_other, *second_parts = gradients(1, [carry])
        ffn_got = swap(ffn_near, "dp", near)
        first_folded = folded(first_parts, *first_got)
        second_got = halves(second_parts)
        ffn_last = to_far(ffn_own, ffn_core, ffn_got)
        input_core, input_near = to_near(input_own, input_other)
        ffn_far = swap(ffn_last, "dp", 2 * near)
        input_got = swap(input_near, "dp", near)
        first_sums = summed(first_parts, *first_folded)
        second_folded = after(folded(second_parts, *second_got), input_near, ffn_last)
        first_sums = after(first_sums, *second_folded)
        first_back = sent_back(first_sums)
        input_last = to_far(input_own, input_core, input_got)
        second_sums = after(summed(second_parts, *second_folded), input_last)
        input_far = swap(input_last, "dp", 2 * near)
        back = first_back + sent_back(second_sums)
        ffn_rows = add(ffn_own[0], ffn_core[0], ffn_got[0], ffn_far)
        input_rows = add(input_own[0], input_core[0], input_got[0], input_far)
    else:
        carried, back = [], []
        for chunk in range(chunks):
            outs = gradients(chunk, carried)
            carried, parts = outs[:-len(weight_parts)], outs[-len(weight_parts):]
            if split:
                sums = summed(parts, *folded(parts, *halves(parts)))
            else:
                sums = scatter(dict(enumerate(parts)), "dp", near_strides)[0]
            back += sent_back(sums)
        ffn_rows = generic(ffn_own, ffn_other)
        input_rows = generic(*carried)

    grads = call(
        functools.partial(
            unpack, chunks=chunks, chunk_rows=chunk_rows, blocks=blocks, slot_count=slot_count
        ),
        table,
        back,
        [whole(chunk_shape)] * len(back),
        whole(tile_list.shape),
        shape(tile_list.shape, BF16),
        cost=2_000_000,
    )
    tile_grad = grads.reshape(blocks_dev, 3, slot_count, row_share, tile).transpose(3, 1, 0, 2, 4)
    return ffn_rows, input_rows, tile_grad


def solution(mesh):
    return jax.shard_map(
        shards,
        mesh=mesh,
        in_specs=(
            P(("dp", "tensor"), None),
            P(("dp", "tensor"), None),
            P("dp", None, "tensor", None, None),
            P(None, "tensor"),
            P(None, "tensor", None),
        ),
        out_specs=(
            P(("dp", "tensor"), None),
            P(("dp", "tensor"), None),
            P("dp", None, "tensor", None, None),
        ),
        check_vma=False,
    )
```

```python
import functools
import math

import jax
import jax.numpy as jnp
from jax import lax
from jax.experimental import pallas as pl
from jax.experimental.pallas import tpu as pltpu
from jax.sharding import PartitionSpec as P

F32 = jnp.float32
BF16 = jnp.bfloat16
PLAIN = (((1,), (0,)), ((), ()))
TURNED = (((1,), (1,)), ((), ()))
PARAMS = pltpu.CompilerParams(vmem_limit_bytes=56 * 1024 * 1024)
dot = functools.partial(lax.dot_general, preferred_element_type=F32)


def swap(value, axis, stride):
    size = lax.axis_size(axis)
    return lax.ppermute(value, axis, [(at, at ^ stride) for at in range(size)])


def after(value, *others):
    return lax.optimization_barrier((value, *others))[0]


def add(first, *others):
    total = first.astype(F32)
    for other in others:
        total = total + other.astype(F32)
    return total.astype(BF16)


def strides_of(size, unit=1):
    found = []
    step = size // 2
    while step >= 1:
        found.append(step * unit)
        step //= 2
    return found


def gather(items, axis, strides):
    for stride in strides:
        items = {**items, **{at ^ stride: swap(one, axis, stride) for at, one in items.items()}}
    return items


def scatter(items, axis, strides):
    for stride in reversed(strides):
        kept = {}
        for at, one in items.items():
            if not at & stride:
                kept[at] = add(one, swap(items[at ^ stride], axis, stride))
        items = kept
    return items


def whole(shape, at=None):
    at = (0,) * len(shape) if at is None else at
    return pl.BlockSpec(shape, lambda *_: at)


def by_block(shape):
    return pl.BlockSpec((1,) + shape, lambda block, *_: (block,) + (0,) * len(shape))


def pack(table, tiles, *refs, blocks, slot_count):
    outs, lines = refs[:-1], refs[-1]
    spare = outs[0].shape[0] - 1
    share, terms, blocks_dev, _ = tiles.shape
    for row in range(share):
        for term in range(terms):
            at = (row * terms + term) * blocks_dev
            lines[at : at + blocks_dev, :] = tiles[row, term].astype(F32)
    for at, out in enumerate(outs):

        def one(place, _, at=at, out=out):
            column = at * blocks + place
            block = table[0, column]
            for matrix in range(3):
                first, count = table[1 + matrix, column], table[4 + matrix, column]
                for slot in range(slot_count):
                    to = jnp.where(slot < count, first + slot, spare)
                    source = (matrix * slot_count + slot) * blocks_dev + block
                    out[to] = lines[pl.ds(source, share, stride=terms * blocks_dev), :].astype(BF16)
            return _

        lax.fori_loop(0, blocks, one, 0)


def unpack(table, *refs, chunks, chunk_rows, blocks, slot_count):
    out, sources = refs[-1], refs[:-1]
    far = len(sources) // chunks
    chunk_blocks = blocks // chunks
    for chunk in range(chunks):
        for at in range(far):
            ref = sources[chunk * far + at]

            def one(place, _, at=at, ref=ref, chunk=chunk):
                column = at * blocks + chunk * chunk_blocks + place
                block = table[0, column]
                for matrix in range(3):
                    first = table[1 + matrix, column] - chunk * chunk_rows
                    count = table[4 + matrix, column]
                    for slot in range(slot_count):
                        live = slot < count
                        value = ref[jnp.where(live, first + slot, 0)].astype(F32)
                        out[(block * 3 + matrix) * slot_count + slot] = jnp.where(
                            live, value, 0.0
                        ).astype(BF16)
                return _

            lax.fori_loop(0, chunk_blocks, one, 0)


def offset_of(table, part, at, near, share):
    far_part = (part[1] + at) ^ table[16, 0]
    near_part = part[0] ^ table[16, 1]
    return pl.multiple_of((far_part * near + near_part) * share, share)


def assemble(table, *refs, weight_parts, near):
    weight_refs, out, tiles = refs[: len(weight_parts)], refs[-2], refs[-1]
    for ref, part in zip(weight_refs, weight_parts):
        share = ref.shape[2]
        for at in range(part[2]):
            offset = offset_of(table, part, at, near, share)
            tiles[:, pl.ds(offset, share), :] = ref[at].astype(F32)
    out[...] = tiles[...].astype(BF16)

    @pl.when(pl.program_id(0) == pl.num_programs(0) - 1)
    def _():
        out[out.shape[0] - 1] = jnp.zeros(out.shape[1:], BF16)


def places_of(table, block, slot_count, spare, base=0):
    places = []
    for matrix in range(3):
        first, count = table[1 + matrix, block] - base, table[4 + matrix, block]
        places += [jnp.where(slot < count, first + slot, spare) for slot in range(slot_count)]
    return places


def store_parts(total, own, other, token_count, own_parts):
    own_rows = own.shape[1]
    own_at, other_at = 0, 0
    for at in range(token_count):
        value = total[at * own_rows : (at + 1) * own_rows, :].astype(BF16)
        if at in own_parts:
            own[own_at] = value
            own_at += 1
        else:
            other[other_at] = value
            other_at += 1


def tokens_at(refs, columns):
    return jnp.concatenate([ref[:, columns] for ref in refs], axis=0)


def columns_of(table, block, index, tile):
    return pl.ds(pl.multiple_of(table[7 + index, block] * tile, tile), tile)


def ahead(table, *refs, token_count, slot_count, own_parts):
    token_refs, refs = refs[:token_count], refs[token_count:]
    tiles, x_turned, gate_slope, gate_act_out, hidden_turned, ffn_own, ffn_other, ffn_sum = refs
    block = pl.program_id(0)
    tile = tiles.shape[1]
    gate, up, down = (range(at * slot_count, (at + 1) * slot_count) for at in range(3))
    places = places_of(table, block, slot_count, tiles.shape[0] - 1)

    @pl.when(block == 0)
    def _():
        for at in range(x_turned.shape[0] // tile):
            here = slice(at * tile, (at + 1) * tile)
            x_turned[here, :] = tokens_at(token_refs, here).T
        ffn_sum[...] = jnp.zeros_like(ffn_sum)

    def tokens_of(indices):
        return jnp.concatenate(
            [tokens_at(token_refs, columns_of(table, block, index, tile)) for index in indices], axis=1
        )

    gate_tiles = jnp.concatenate([tiles[places[index]] for index in gate], axis=0)
    up_tiles = jnp.concatenate([tiles[places[index]] for index in up], axis=0)
    down_tiles = jnp.concatenate([tiles[places[index]] for index in down], axis=1)
    gate_pre = dot(tokens_of(gate), gate_tiles, PLAIN)
    up_pre = dot(tokens_of(up), up_tiles, PLAIN)
    gate_sig = jax.nn.sigmoid(gate_pre)
    gate_act = gate_pre * gate_sig
    hidden = (gate_act * up_pre).astype(BF16)
    gate_slope[0] = up_pre * gate_sig * (1.0 + gate_pre * (1.0 - gate_sig))
    gate_act_out[0] = gate_act
    hidden_turned[0] = hidden.T
    ffn = dot(hidden, down_tiles, PLAIN)
    for at, index in enumerate(down):
        ffn_sum[:, columns_of(table, block, index, tile)] += ffn[:, at * tile : (at + 1) * tile]

    @pl.when(block == pl.num_programs(0) - 1)
    def _():
        store_parts(ffn_sum, ffn_own, ffn_other, token_count, own_parts)


def behind(
    table, *refs, token_count, weight_parts, slot_count, grad_scale, near, chunk, chunk_rows
):
    token_refs, refs = refs[:token_count], refs[token_count:]
    tiles, x_turned, gate_slope, gate_act, hidden_turned, gate_out, up_out = refs[:7]
    grad_refs, sums = refs[7:-1], refs[-1]
    step = pl.program_id(0)
    block = step + chunk * pl.num_programs(0)
    tile = tiles.shape[1]
    gate, up, down = (range(at * slot_count, (at + 1) * slot_count) for at in range(3))
    places = places_of(table, block, slot_count, tiles.shape[0] - 1)
    down_tiles = jnp.concatenate([tiles[places[index]] for index in down], axis=1)
    grad_in = jnp.concatenate(
        [tokens_at(token_refs, columns_of(table, block, index, tile)) for index in down], axis=1
    )
    hidden_grad = dot(grad_in, down_tiles, TURNED)
    gate_grad = (hidden_grad * gate_slope[0]).astype(BF16)
    up_grad = (hidden_grad * gate_act[0]).astype(BF16)
    gate_out[0] = gate_grad
    up_out[0] = up_grad
    to = places_of(table, block, slot_count, sums.shape[0] - 1, chunk * chunk_rows)
    down_terms = dot(hidden_turned[0], grad_in, PLAIN) * grad_scale
    for at, index in enumerate(down):
        sums[to[index]] = down_terms[:, at * tile : (at + 1) * tile]
    for indices, grad in ((gate, gate_grad), (up, up_grad)):
        turned = jnp.concatenate(
            [x_turned[columns_of(table, block, index, tile), :] for index in indices], axis=0
        )
        tile_terms = dot(turned, grad, PLAIN) * grad_scale
        for at, index in enumerate(indices):
            sums[to[index]] = tile_terms[at * tile : (at + 1) * tile]

    @pl.when(step == pl.num_programs(0) - 1)
    def _():
        for ref, part in zip(grad_refs, weight_parts):
            share = ref.shape[2]
            for at in range(part[2]):
                offset = offset_of(table, part, at, near, share)
                ref[at] = sums[:, pl.ds(offset, share), :].astype(BF16)


def inward(table, *refs, chunks, slot_count, token_count, own_parts):
    grads, tiles, input_own, input_other, input_sum = refs[: 2 * chunks], *refs[2 * chunks :]
    step = pl.program_id(0)
    tile = tiles.shape[1]

    @pl.when(step == 0)
    def _():
        input_sum[...] = jnp.zeros_like(input_sum)

    for chunk in range(chunks):
        block = step + chunk * pl.num_programs(0)
        places = places_of(table, block, slot_count, tiles.shape[0] - 1)
        for matrix in range(2):
            indices = range(matrix * slot_count, (matrix + 1) * slot_count)
            whole_tiles = jnp.concatenate([tiles[places[index]] for index in indices], axis=0)
            terms = dot(grads[2 * chunk + matrix][0], whole_tiles, TURNED)
            for at, index in enumerate(indices):
                input_sum[:, columns_of(table, block, index, tile)] += terms[
                    :, at * tile : (at + 1) * tile
                ]

    @pl.when(step == pl.num_programs(0) - 1)
    def _():
        store_parts(input_sum, input_own, input_other, token_count, own_parts)


def call(kernel, table, args, in_specs, out_specs, out_shape, grid=1, scratch=(), cost=0):
    return pl.pallas_call(
        kernel,
        grid_spec=pltpu.PrefetchScalarGridSpec(
            num_scalar_prefetch=1,
            grid=(grid,),
            in_specs=in_specs,
            out_specs=out_specs,
            scratch_shapes=scratch,
        ),
        out_shape=out_shape,
        compiler_params=PARAMS,
        cost_estimate=pl.CostEstimate(flops=0, bytes_accessed=cost, transcendentals=0),
    )(table, *args)


def shards(tokens, out_grad, weight_tiles, tile_counts, tile_rows):
    row_share, _, blocks_dev, slot_count, tile = weight_tiles.shape
    own_rows, features = tokens.shape
    dp_size, tensor_size = lax.axis_size("dp"), lax.axis_size("tensor")
    far = math.gcd(4, math.gcd(dp_size, blocks_dev))
    near = dp_size // far
    blocks = blocks_dev // far
    chunks = math.gcd(2, blocks)
    chunk_blocks = blocks // chunks
    groups = far * chunks
    terms = 3 * slot_count
    grad_scale = 1.0 / math.sqrt(own_rows * tensor_size * dp_size)
    me = lax.axis_index("dp")
    far_at, near_at = me // near, me % near
    far_strides, near_strides = strides_of(far, near), strides_of(near)
    tensor_strides = strides_of(tensor_size)
    shape = jax.ShapeDtypeStruct

    x_items, g_items = {0: tokens}, {0: out_grad}
    if far > 1:
        x_items[near] = swap(tokens, "dp", near)

    capacity = (terms * blocks_dev - 3 * blocks_dev + 3 * (slot_count - 1) * (groups - 1)) // groups
    chunk_rows = capacity + 1
    block_ids = jnp.arange(blocks_dev, dtype=jnp.int32)
    load = tile_counts[0] + tile_counts[1] + tile_counts[2]
    earlier = (load[:, None] > load[None, :]) | (
        (load[:, None] == load[None, :]) & (block_ids[:, None] < block_ids[None, :])
    )
    rank = jnp.sum(earlier.astype(jnp.int32), axis=0)
    group = rank % groups
    before = (group[:, None] == group[None, :]) & (rank[:, None] < rank[None, :])
    start = jnp.sum(jnp.where(before, load[:, None], 0), axis=0) + (group // far) * chunk_rows
    ranks_of = (
        jnp.arange(chunk_blocks, dtype=jnp.int32)[None, None, :] * groups
        + jnp.arange(chunks, dtype=jnp.int32)[None, :, None] * far
        + (jnp.arange(far, dtype=jnp.int32)[:, None, None] ^ far_at)
    ).reshape(blocks_dev)
    columns = jnp.concatenate(
        [
            block_ids[None, :],
            start[None, :],
            (start + tile_counts[0])[None, :],
            (start + tile_counts[0] + tile_counts[1])[None, :],
            tile_counts,
            jnp.transpose(tile_rows, (0, 2, 1)).reshape(terms, blocks_dev),
        ]
    )
    table = jnp.sum(
        jnp.where(ranks_of[None, :, None] == rank[None, None, :], columns[:, None, :], 0), axis=2
    )
    place = jnp.where(block_ids == 0, far_at, near_at).astype(jnp.int32)
    table = jnp.concatenate([table, place[None, :]])

    tile_lines = jnp.transpose(weight_tiles, (0, 1, 3, 2, 4)).reshape(
        row_share, terms, blocks_dev, tile
    )
    slots = chunks * chunk_rows
    packed_shape = (slots, row_share, tile)
    chunk_shape = (chunk_rows, row_share, tile)
    packed = call(
        functools.partial(pack, blocks=blocks, slot_count=slot_count),
        table,
        [tile_lines],
        [whole(tile_lines.shape)],
        [whole(packed_shape)] * far,
        [shape(packed_shape, BF16)] * far,
        scratch=[pltpu.VMEM((row_share * terms * blocks_dev, tile), F32)],
        cost=1_000_000,
    )
    if far > 1:
        packed = after(tuple(packed), x_items[near])
    received = [swap(packed[at], "dp", at * near) for at in reversed(range(1, far))][::-1]
    held = jnp.stack([packed[0], *received])

    half = far // 2
    split = near == 4 and far % 2 == 0
    if split:
        from_1, from_2 = swap(held, "dp", 1), swap(held, "dp", 2)
        pass_1, pass_2 = from_1[:half], from_2[half:]
        weight_list = [held, from_1, from_2, swap(pass_1, "dp", 2), swap(pass_2, "dp", 1)]
        weight_parts = [(0, 0, far), (1, 0, far), (2, 0, far), (3, 0, half), (3, half, half)]
    else:
        items = gather({0: held}, "dp", near_strides)
        pass_1 = pass_2 = held
        weight_list = [items[at] for at in range(near)]
        weight_parts = [(at, 0, far) for at in range(near)]

    if far == 4:
        x_source, g_source = after((tokens, out_grad), held)
        x_items[2 * near] = swap(x_source, "dp", 2 * near)
        g_items[near] = swap(g_source, "dp", near)
        x_back, g_source = after((x_items[2 * near], g_source), pass_1, pass_2, x_items[2 * near])
        x_items[3 * near] = swap(x_back, "dp", near)
        g_items[2 * near] = swap(g_source, "dp", 2 * near)
        g_items[3 * near] = swap(g_items[2 * near], "dp", near)
        weight_list = list(after(tuple(weight_list), x_items[2 * near]))
    elif far == 2:
        g_items[near] = swap(out_grad, "dp", near)

    far_order = [at * near for at in range(0, far, 2)] + [at * near for at in range(1, far, 2)]
    x_list, g_list, token_parts = [], [], []
    token_shape = (own_rows, features)
    for at in far_order:
        x_parts = gather({0: x_items[at]}, "tensor", tensor_strides)
        g_parts = gather({0: g_items[at]}, "tensor", tensor_strides)
        for other in x_parts:
            token_parts.append((at, other))
            x_list.append(x_parts[other])
            g_list.append(g_parts[other])

    token_count = len(token_parts)
    group_rows = token_count * own_rows
    own_parts = tuple(at for at, (_, other) in enumerate(token_parts) if other == 0)
    other_parts = [part for part in token_parts if part[1] != 0]
    own_shape = (len(own_parts), own_rows, features)
    other_shape = (len(other_parts), own_rows, features)

    token_specs = [whole(token_shape)] * token_count
    steps = max(at for at in range(1, 9) if slots % at == 0)
    tiles_shape = (slots, tile, tile)
    tiles = call(
        functools.partial(assemble, weight_parts=weight_parts, near=near),
        table,
        weight_list,
        [
            pl.BlockSpec((length, slots // steps, row_share, tile), lambda step, *_: (0, step, 0, 0))
            for _, _, length in weight_parts
        ],
        pl.BlockSpec((slots // steps, tile, tile), lambda step, *_: (step, 0, 0)),
        shape(tiles_shape, BF16),
        grid=steps,
        scratch=[pltpu.VMEM((slots // steps, tile, tile), F32)],
        cost=10_000_000,
    )
    if far == 4:
        x_list = list(after(tuple(x_list), g_items[2 * near]))
    x_turned, gate_slope, gate_act, hidden_turned, ffn_own, ffn_other = call(
        functools.partial(
            ahead, token_count=token_count, slot_count=slot_count, own_parts=own_parts
        ),
        table,
        [*x_list, tiles],
        token_specs + [whole(tiles_shape)],
        [
            whole((features, group_rows)),
            by_block((group_rows, tile)),
            by_block((group_rows, tile)),
            by_block((tile, group_rows)),
            whole(own_shape),
            whole(other_shape),
        ],
        [
            shape((features, group_rows), BF16),
            shape((blocks, group_rows, tile), F32),
            shape((blocks, group_rows, tile), F32),
            shape((blocks, tile, group_rows), BF16),
            shape(own_shape, BF16),
            shape(other_shape, BF16),
        ],
        grid=blocks,
        scratch=[pltpu.VMEM((group_rows, features), F32)],
        cost=40_000_000,
    )

    def to_near(own_sums, other_sums):
        from_core = swap(other_sums, "tensor", 1)
        return from_core, add(own_sums[half:], from_core[half:])

    def to_far(own_sums, from_core, got):
        return add(own_sums[1], from_core[1], got[1])

    def generic(own_sums, other_sums):
        sums = {}
        for index, at in enumerate(far_order):
            items = {0: own_sums[index]}
            for other_index, (far_part, other) in enumerate(other_parts):
                if far_part == at:
                    items[other] = other_sums[other_index]
            sums[at] = scatter(items, "tensor", tensor_strides)[0]
        return scatter(sums, "dp", far_strides)[0]

    staged = tensor_size == 2 and far == 4 and split and chunks == 2
    if staged:
        ffn_core, ffn_near = to_near(ffn_own, ffn_other)

    def gradients(chunk):
        def block_at(block_shape):
            return pl.BlockSpec(
                (1,) + block_shape,
                lambda block, *_: (block + chunk * chunk_blocks,) + (0,) * len(block_shape),
            )

        outs = call(
            functools.partial(
                behind,
                token_count=token_count,
                weight_parts=weight_parts,
                slot_count=slot_count,
                grad_scale=grad_scale,
                near=near,
                chunk=chunk,
                chunk_rows=chunk_rows,
            ),
            table,
            [*g_list, tiles, x_turned, gate_slope, gate_act, hidden_turned],
            token_specs
            + [
                whole(tiles_shape),
                whole((features, group_rows)),
                block_at((group_rows, tile)),
                block_at((group_rows, tile)),
                block_at((tile, group_rows)),
            ],
            [by_block((group_rows, tile))] * 2
            + [whole((length,) + chunk_shape) for _, _, length in weight_parts],
            [shape((chunk_blocks, group_rows, tile), BF16)] * 2
            + [shape((length,) + chunk_shape, BF16) for _, _, length in weight_parts],
            grid=chunk_blocks,
            scratch=[pltpu.VMEM((chunk_rows, tile, tile), F32)],
            cost=25_000_000,
        )
        return outs[:2], outs[2:]

    def input_gradients(grads):
        return call(
            functools.partial(
                inward,
                chunks=chunks,
                slot_count=slot_count,
                token_count=token_count,
                own_parts=own_parts,
            ),
            table,
            [*grads, tiles],
            [by_block((group_rows, tile))] * len(grads) + [whole(tiles_shape)],
            [whole(own_shape), whole(other_shape)],
            [shape(own_shape, BF16), shape(other_shape, BF16)],
            grid=chunk_blocks,
            scratch=[pltpu.VMEM((group_rows, features), F32)],
            cost=25_000_000,
        )

    def halves(parts):
        return swap(parts[3], "dp", 1), swap(parts[4], "dp", 2)

    def folded(parts, got_1, got_2):
        to_2 = jnp.concatenate([add(parts[2][:half], got_1), parts[2][half:]])
        to_1 = jnp.concatenate([parts[1][:half], add(parts[1][half:], got_2)])
        return to_1, to_2

    def summed(parts, to_1, to_2):
        from_1, from_2 = swap(to_1, "dp", 1), swap(to_2, "dp", 2)
        return [add(parts[0][at], from_1[at], from_2[at]) for at in range(far)]

    def sent_back(sums):
        return [sums[0]] + [swap(sums[at], "dp", at * near) for at in range(1, far)]

    if staged:
        first_grads, first_parts = gradients(0)
        first_got = halves(first_parts)
        hidden_turned = after(hidden_turned, ffn_near, *first_grads)
        second_grads, second_parts = gradients(1)
        ffn_got = swap(ffn_near, "dp", near)
        first_folded = folded(first_parts, *first_got)
        second_got = halves(second_parts)
        second_grads = after(tuple(second_grads), *first_folded)
        input_own, input_other = input_gradients([*first_grads, *second_grads])
        ffn_last = to_far(ffn_own, ffn_core, ffn_got)
        ffn_far = swap(ffn_last, "dp", 2 * near)
        input_core, input_near = to_near(input_own, input_other)
        input_got = swap(input_near, "dp", near)
        first_sums = summed(first_parts, *first_folded)
        second_folded = after(folded(second_parts, *second_got), *second_grads)
        first_back = sent_back(after(first_sums, input_near))
        input_last = to_far(input_own, input_core, input_got)
        second_sums = summed(second_parts, *second_folded)
        input_far = swap(input_last, "dp", 2 * near)
        back = first_back + sent_back(second_sums)
        ffn_rows = add(ffn_own[0], ffn_core[0], ffn_got[0], ffn_far)
        input_rows = add(input_own[0], input_core[0], input_got[0], input_far)
    else:
        grads, back = [], []
        for chunk in range(chunks):
            chunk_grads, parts = gradients(chunk)
            grads += chunk_grads
            if split:
                sums = summed(parts, *folded(parts, *halves(parts)))
            else:
                sums = scatter(dict(enumerate(parts)), "dp", near_strides)[0]
            back += sent_back(sums)
        ffn_rows = generic(ffn_own, ffn_other)
        input_rows = generic(*input_gradients(grads))

    grads = call(
        functools.partial(
            unpack, chunks=chunks, chunk_rows=chunk_rows, blocks=blocks, slot_count=slot_count
        ),
        table,
        back,
        [whole(chunk_shape)] * len(back),
        whole((blocks_dev * terms, row_share, tile)),
        shape((blocks_dev * terms, row_share, tile), BF16),
        cost=2_000_000,
    )
    tile_grad = grads.reshape(blocks_dev, 3, slot_count, row_share, tile).transpose(3, 1, 0, 2, 4)
    return ffn_rows, input_rows, tile_grad


def solution(mesh):
    return jax.shard_map(
        shards,
        mesh=mesh,
        in_specs=(
            P(("dp", "tensor"), None),
            P(("dp", "tensor"), None),
            P("dp", None, "tensor", None, None),
            P(None, "tensor"),
            P(None, "tensor", None),
        ),
        out_specs=(
            P(("dp", "tensor"), None),
            P(("dp", "tensor"), None),
            P("dp", None, "tensor", None, None),
        ),
        check_vma=False,
    )
```

```python
import functools
import math

import jax
import jax.numpy as jnp
from jax import lax
from jax.experimental import pallas as pl
from jax.experimental.pallas import tpu as pltpu
from jax.sharding import PartitionSpec as P

F32 = jnp.float32
BF16 = jnp.bfloat16
PLAIN = (((1,), (0,)), ((), ()))
TURNED = (((1,), (1,)), ((), ()))
MIB = 1024 * 1024
UNROLL = 2
dot = functools.partial(lax.dot_general, preferred_element_type=F32)


def swap(value, axis, stride):
    size = lax.axis_size(axis)
    return lax.ppermute(value, axis, [(at, at ^ stride) for at in range(size)])


def after(value, *others):
    return lax.optimization_barrier((value, *others))[0]


def add(first, *others):
    total = first.astype(F32)
    for other in others:
        total = total + other.astype(F32)
    return total.astype(BF16)


def strides_of(size, unit=1):
    found = []
    step = size // 2
    while step >= 1:
        found.append(step * unit)
        step //= 2
    return found


def gather(items, axis, strides):
    for stride in strides:
        items = {**items, **{at ^ stride: swap(one, axis, stride) for at, one in items.items()}}
    return items


def scatter(items, axis, strides):
    for stride in reversed(strides):
        kept = {}
        for at, one in items.items():
            if not at & stride:
                kept[at] = add(one, swap(items[at ^ stride], axis, stride))
        items = kept
    return items


def whole(shape):
    return pl.BlockSpec(shape, lambda *_: (0,) * len(shape), pipeline_mode=pl.Buffered(1))


def pack(table, tiles, *refs, blocks, slot_count):
    outs, lines = refs[:-1], refs[-1]
    spare = outs[0].shape[0] - 1
    share, terms, blocks_dev, _ = tiles.shape
    for row in range(share):
        for term in range(terms):
            at = (row * terms + term) * blocks_dev
            lines[at : at + blocks_dev, :] = tiles[row, term].astype(F32)
    for at, out in enumerate(outs):

        def one(place, _, at=at, out=out):
            column = at * blocks + place
            block = table[0, column]
            for matrix in range(3):
                first, count = table[1 + matrix, column], table[4 + matrix, column]
                for slot in range(slot_count):
                    to = jnp.where(slot < count, first + slot, spare)
                    source = (matrix * slot_count + slot) * blocks_dev + block
                    out[to] = lines[pl.ds(source, share, stride=terms * blocks_dev), :].astype(BF16)
            return _

        lax.fori_loop(0, blocks, one, 0, unroll=True)


def unpack(table, *refs, chunks, chunk_rows, blocks, slot_count):
    out, lines, sources = refs[-2], refs[-1], refs[:-2]
    share, terms, blocks_dev, _ = out.shape
    far = len(sources) // chunks
    chunk_blocks = blocks // chunks
    for chunk in range(chunks):
        for at in range(far):
            ref = sources[chunk * far + at]

            def one(place, _, at=at, ref=ref, chunk=chunk):
                column = at * blocks + chunk * chunk_blocks + place
                block = table[0, column]
                for matrix in range(3):
                    first = table[1 + matrix, column] - chunk * chunk_rows
                    count = table[4 + matrix, column]
                    for slot in range(slot_count):
                        live = slot < count
                        value = ref[jnp.where(live, first + slot, 0)].astype(F32)
                        target = (matrix * slot_count + slot) * blocks_dev + block
                        lines[pl.ds(target, share, stride=terms * blocks_dev), :] = jnp.where(
                            live, value, 0.0
                        )
                return _

            lax.fori_loop(0, chunk_blocks, one, 0, unroll=True)
    for row in range(share):
        for term in range(terms):
            at = (row * terms + term) * blocks_dev
            out[row, term] = lines[at : at + blocks_dev, :].astype(BF16)


def offset_of(table, part, at, near, share):
    far_part = (part[1] + at) ^ table[16, 0]
    near_part = part[0] ^ table[16, 1]
    return pl.multiple_of((far_part * near + near_part) * share, share)


def assemble(table, *refs, weight_parts, near):
    weight_refs, out, tiles = refs[: len(weight_parts)], refs[-2], refs[-1]
    for ref, part in zip(weight_refs, weight_parts):
        share = ref.shape[2]
        for at in range(part[2]):
            offset = offset_of(table, part, at, near, share)
            tiles[:, pl.ds(offset, share), :] = ref[at].astype(F32)
    out[...] = tiles[...].astype(BF16)

    @pl.when(pl.program_id(0) == pl.num_programs(0) - 1)
    def _():
        out[out.shape[0] - 1] = jnp.zeros(out.shape[1:], BF16)


def places_of(table, block, slot_count, spare, base=0):
    places = []
    for matrix in range(3):
        first, count = table[1 + matrix, block] - base, table[4 + matrix, block]
        places += [jnp.where(slot < count, first + slot, spare) for slot in range(slot_count)]
    return places


def store_parts(total, own, other, parts):
    own_rows = own.shape[1]
    for at, (is_other, place) in enumerate(parts):
        ref = other if is_other else own
        ref[place] = total[at * own_rows : (at + 1) * own_rows, :].astype(BF16)


def tokens_at(refs, columns):
    return jnp.concatenate([ref[:, columns] for ref in refs], axis=0)


def columns_of(table, block, index, tile):
    return pl.ds(pl.multiple_of(table[7 + index, block] * tile, tile), tile)


def triples(slot_count):
    return [range(at * slot_count, (at + 1) * slot_count) for at in range(3)]


def in_turn(first, rest, blocks):
    group = max(size for size in range(1, UNROLL + 1) if blocks % size == 0)

    def some(at, _):
        held = first(at * group)
        for block in range(group):
            following = first(at * group + block + 1) if block + 1 < group else None
            rest(at * group + block, *held)
            held = following
        return _

    lax.fori_loop(0, blocks // group, some, 0)


def ahead(table, *refs, token_count, slot_count, parts):
    token_refs, refs = refs[:token_count], refs[token_count:]
    tiles, x_turned, gate_slope, gate_act_out, hidden_turned, ffn_own, ffn_other, ffn_sum = refs
    tile = tiles.shape[1]
    gate, up, down = triples(slot_count)

    for at in range(x_turned.shape[0] // tile):
        here = slice(at * tile, (at + 1) * tile)
        x_turned[here, :] = tokens_at(token_refs, here).T
    ffn_sum[...] = jnp.zeros_like(ffn_sum)

    def first(block):
        places = places_of(table, block, slot_count, tiles.shape[0] - 1)
        sums = []
        for indices in (gate, up):
            columns = [columns_of(table, block, index, tile) for index in indices]
            values = jnp.concatenate([tokens_at(token_refs, column) for column in columns], axis=1)
            weights = jnp.concatenate([tiles[places[index]] for index in indices], axis=0)
            sums.append(dot(values, weights, PLAIN))
        return places, *sums

    def rest(block, places, gate_pre, up_pre):
        gate_sig = jax.nn.sigmoid(gate_pre)
        gate_act = gate_pre * gate_sig
        hidden = (gate_act * up_pre).astype(BF16)
        gate_slope[block] = up_pre * gate_sig * (1.0 + gate_pre * (1.0 - gate_sig))
        gate_act_out[block] = gate_act
        hidden_turned[block] = hidden.T
        down_tiles = jnp.concatenate([tiles[places[index]] for index in down], axis=1)
        ffn = dot(hidden, down_tiles, PLAIN)
        for at, index in enumerate(down):
            ffn_sum[:, columns_of(table, block, index, tile)] += ffn[:, at * tile : (at + 1) * tile]

    in_turn(first, rest, gate_slope.shape[0])
    store_parts(ffn_sum, ffn_own, ffn_other, parts)


def behind(
    table, *refs, token_count, weight_parts, slot_count, grad_scale, near, chunks, chunk_rows, parts
):
    token_refs, refs = refs[:token_count], refs[token_count:]
    tiles, x_turned, gate_slope, gate_act, hidden_turned, input_own, input_other = refs[:7]
    grad_refs, input_sum, sums = refs[7:-2], refs[-2], refs[-1]
    tile = tiles.shape[1]
    gate, up, down = triples(slot_count)
    input_sum[...] = jnp.zeros_like(input_sum)

    def first(block):
        places = places_of(table, block, slot_count, tiles.shape[0] - 1)
        columns = [columns_of(table, block, index, tile) for index in range(3 * slot_count)]
        down_tiles = jnp.concatenate([tiles[places[index]] for index in down], axis=1)
        grad_in = jnp.concatenate([tokens_at(token_refs, columns[index]) for index in down], axis=1)
        return places, columns, grad_in, dot(grad_in, down_tiles, TURNED)

    def rest(block, places, columns, grad_in, hidden_grad):
        gate_grad = (hidden_grad * gate_slope[block]).astype(BF16)
        up_grad = (hidden_grad * gate_act[block]).astype(BF16)
        down_terms = dot(hidden_turned[block], grad_in, PLAIN) * grad_scale
        for at, index in enumerate(down):
            sums[places[index]] = down_terms[:, at * tile : (at + 1) * tile]
        for indices, grad in ((gate, gate_grad), (up, up_grad)):
            weights = jnp.concatenate([tiles[places[index]] for index in indices], axis=0)
            back = dot(grad, weights, TURNED)
            turned = jnp.concatenate([x_turned[columns[index], :] for index in indices], axis=0)
            terms = dot(turned, grad, PLAIN) * grad_scale
            for at, index in enumerate(indices):
                sums[places[index]] = terms[at * tile : (at + 1) * tile]
                input_sum[:, columns[index]] += back[:, at * tile : (at + 1) * tile]

    in_turn(first, rest, gate_slope.shape[0])
    store_parts(input_sum, input_own, input_other, parts)
    for chunk in range(chunks):
        rows = slice(chunk * chunk_rows, (chunk + 1) * chunk_rows)
        for index, part in enumerate(weight_parts):
            ref = grad_refs[chunk * len(weight_parts) + index]
            share = ref.shape[2]
            for at in range(part[2]):
                offset = offset_of(table, part, at, near, share)
                ref[at] = sums[rows, pl.ds(offset, share), :].astype(BF16)


def call(kernel, table, args, in_specs, out_specs, out_shape, grid=1, scratch=(), cost=0, vmem=40):
    return pl.pallas_call(
        kernel,
        grid_spec=pltpu.PrefetchScalarGridSpec(
            num_scalar_prefetch=1,
            grid=(grid,),
            in_specs=in_specs,
            out_specs=out_specs,
            scratch_shapes=scratch,
        ),
        out_shape=out_shape,
        compiler_params=pltpu.CompilerParams(vmem_limit_bytes=vmem * MIB),
        cost_estimate=pl.CostEstimate(flops=0, bytes_accessed=cost, transcendentals=0),
    )(table, *args)


def shards(tokens, out_grad, weight_tiles, tile_counts, tile_rows):
    row_share, _, blocks_dev, slot_count, tile = weight_tiles.shape
    own_rows, features = tokens.shape
    dp_size, tensor_size = lax.axis_size("dp"), lax.axis_size("tensor")
    far = math.gcd(4, math.gcd(dp_size, blocks_dev))
    near = dp_size // far
    blocks = blocks_dev // far
    chunks = math.gcd(2, blocks)
    chunk_blocks = blocks // chunks
    groups = far * chunks
    terms = 3 * slot_count
    grad_scale = 1.0 / math.sqrt(own_rows * tensor_size * dp_size)
    me = lax.axis_index("dp")
    far_at, near_at = me // near, me % near
    far_strides, near_strides = strides_of(far, near), strides_of(near)
    tensor_strides = strides_of(tensor_size)
    shape = jax.ShapeDtypeStruct

    x_items, g_items = {0: tokens}, {0: out_grad}
    if far > 1:
        x_items[near] = swap(tokens, "dp", near)

    capacity = (terms * blocks_dev - 3 * blocks_dev + 3 * (slot_count - 1) * (groups - 1)) // groups
    chunk_rows = capacity + 1
    block_ids = jnp.arange(blocks_dev, dtype=jnp.int32)
    load = tile_counts[0] + tile_counts[1] + tile_counts[2]
    earlier = (load[:, None] > load[None, :]) | (
        (load[:, None] == load[None, :]) & (block_ids[:, None] < block_ids[None, :])
    )
    rank = jnp.sum(earlier.astype(jnp.int32), axis=0)
    group = rank % groups
    before = (group[:, None] == group[None, :]) & (rank[:, None] < rank[None, :])
    start = jnp.sum(jnp.where(before, load[:, None], 0), axis=0) + (group // far) * chunk_rows
    ranks_of = (
        jnp.arange(chunk_blocks, dtype=jnp.int32)[None, None, :] * groups
        + jnp.arange(chunks, dtype=jnp.int32)[None, :, None] * far
        + (jnp.arange(far, dtype=jnp.int32)[:, None, None] ^ far_at)
    ).reshape(blocks_dev)
    columns = jnp.concatenate(
        [
            block_ids[None, :],
            start[None, :],
            (start + tile_counts[0])[None, :],
            (start + tile_counts[0] + tile_counts[1])[None, :],
            tile_counts,
            jnp.transpose(tile_rows, (0, 2, 1)).reshape(terms, blocks_dev),
        ]
    )
    table = jnp.sum(
        jnp.where(ranks_of[None, :, None] == rank[None, None, :], columns[:, None, :], 0), axis=2
    )
    place = jnp.where(block_ids == 0, far_at, near_at).astype(jnp.int32)
    table = jnp.concatenate([table, place[None, :]])

    tile_lines = jnp.transpose(weight_tiles, (0, 1, 3, 2, 4)).reshape(
        row_share, terms, blocks_dev, tile
    )
    slots = chunks * chunk_rows
    packed_shape = (slots, row_share, tile)
    chunk_shape = (chunk_rows, row_share, tile)
    packed = call(
        functools.partial(pack, blocks=blocks, slot_count=slot_count),
        table,
        [tile_lines],
        [whole(tile_lines.shape)],
        [whole(packed_shape)] * far,
        [shape(packed_shape, BF16)] * far,
        scratch=[pltpu.VMEM((row_share * terms * blocks_dev, tile), F32)],
        cost=1_000_000,
        vmem=24,
    )
    staged = tensor_size == 2 and far == 4 and near == 4 and chunks == 2
    if far > 1:
        packed = after(tuple(packed), x_items[near])
    received = [swap(packed[at], "dp", at * near) for at in reversed(range(1, far))][::-1]
    held = jnp.stack([packed[0], *received])
    x_core, g_core = {}, {}
    if staged:
        x_core = {at: swap(x_items[at], "tensor", 1) for at in (0, near)}
        g_core = {0: swap(out_grad, "tensor", 1)}
        held = after(held, *x_core.values(), *g_core.values())

    half = far // 2
    split = near == 4 and far % 2 == 0
    if split:
        from_1, from_2 = swap(held, "dp", 1), swap(held, "dp", 2)
        pass_1, pass_2 = from_1[:half], from_2[half:]
        weight_list = [held, from_1, from_2, swap(pass_1, "dp", 2), swap(pass_2, "dp", 1)]
        weight_parts = [(0, 0, far), (1, 0, far), (2, 0, far), (3, 0, half), (3, half, half)]
    else:
        items = gather({0: held}, "dp", near_strides)
        pass_1 = pass_2 = held
        weight_list = [items[at] for at in range(near)]
        weight_parts = [(at, 0, far) for at in range(near)]

    if far == 4:
        x_source, g_source = after((tokens, out_grad), held)
        x_items[2 * near] = swap(x_source, "dp", 2 * near)
        g_items[near] = swap(g_source, "dp", near)
        x_back, g_source = after((x_items[2 * near], g_source), pass_1, pass_2, x_items[2 * near])
        x_items[3 * near] = swap(x_back, "dp", near)
        g_items[2 * near] = swap(g_source, "dp", 2 * near)
        g_items[3 * near] = swap(g_items[2 * near], "dp", near)
        weight_list = list(after(tuple(weight_list), x_items[2 * near]))
    elif far == 2:
        g_items[near] = swap(out_grad, "dp", near)

    far_order = [at * near for at in range(0, far, 2)] + [at * near for at in range(1, far, 2)]
    if staged:
        order = [at * near for at in range(far)]
        x_late = swap(jnp.concatenate([x_items[at] for at in order[2:]]), "tensor", 1)
        g_late = swap(jnp.concatenate([g_items[at] for at in order[1:]]), "tensor", 1)
        x_list = [x_items[at] for at in order] + [x_core[at] for at in order[:2]] + [x_late]
        g_list = [g_items[at] for at in order] + [g_core[0], g_late]
        parts = [(other, far_order.index(at)) for other in (False, True) for at in order]
        other_parts = [(at, 1) for at in far_order]
    else:
        x_list, g_list, parts, other_parts = [], [], [], []
        for place, at in enumerate(far_order):
            x_parts = gather({0: x_items[at]}, "tensor", tensor_strides)
            g_parts = gather({0: g_items[at]}, "tensor", tensor_strides)
            for other in x_parts:
                parts.append((other != 0, len(other_parts) if other else place))
                if other:
                    other_parts.append((at, other))
                x_list.append(x_parts[other])
                g_list.append(g_parts[other])

    group_rows = far * tensor_size * own_rows
    own_shape = (far, own_rows, features)
    other_shape = (len(other_parts), own_rows, features)
    steps = 2 if slots % 2 == 0 else 1
    tiles_shape = (slots, tile, tile)
    tiles = call(
        functools.partial(assemble, weight_parts=weight_parts, near=near),
        table,
        weight_list,
        [
            pl.BlockSpec((length, slots // steps, row_share, tile), lambda step, *_: (0, step, 0, 0))
            for _, _, length in weight_parts
        ],
        pl.BlockSpec((slots // steps, tile, tile), lambda step, *_: (step, 0, 0)),
        shape(tiles_shape, BF16),
        grid=steps,
        scratch=[pltpu.VMEM((slots // steps, tile, tile), F32)],
        cost=10_000_000,
        vmem=24,
    )
    if far == 4:
        x_list = list(after(tuple(x_list), g_items[2 * near]))
    def specs_of(*groups):
        return [whole(one.shape) for group in groups for one in group]

    middle_shapes = [
        shape((features, group_rows), BF16),
        shape((blocks, group_rows, tile), F32),
        shape((blocks, group_rows, tile), F32),
        shape((blocks, tile, group_rows), BF16),
    ]
    sum_shapes = [shape(own_shape, BF16), shape(other_shape, BF16)]
    outs = call(
        functools.partial(ahead, token_count=len(x_list), slot_count=slot_count, parts=parts),
        table,
        [*x_list, tiles],
        specs_of(x_list, [tiles]),
        specs_of(middle_shapes, sum_shapes),
        middle_shapes + sum_shapes,
        scratch=[pltpu.VMEM((group_rows, features), F32)],
        cost=30_000_000,
    )
    middle, (ffn_own, ffn_other) = outs[:4], outs[4:]

    def to_near(own_sums, other_sums):
        from_core = swap(other_sums, "tensor", 1)
        return from_core, add(own_sums[half:], from_core[half:])

    def to_far(own_sums, from_core, got):
        return add(own_sums[1], from_core[1], got[1])

    def generic(own_sums, other_sums):
        sums = {}
        for index, at in enumerate(far_order):
            items = {0: own_sums[index]}
            for other_index, (far_part, other) in enumerate(other_parts):
                if far_part == at:
                    items[other] = other_sums[other_index]
            sums[at] = scatter(items, "tensor", tensor_strides)[0]
        return scatter(sums, "dp", far_strides)[0]

    if staged:
        ffn_core, ffn_near = to_near(ffn_own, ffn_other)
        middle = after(tuple(middle), ffn_near)
    part_shapes = [
        shape((length,) + chunk_shape, BF16) for _ in range(chunks) for _, _, length in weight_parts
    ]
    outs = call(
        functools.partial(
            behind,
            token_count=len(g_list),
            weight_parts=weight_parts,
            slot_count=slot_count,
            grad_scale=grad_scale,
            near=near,
            chunks=chunks,
            chunk_rows=chunk_rows,
            parts=parts,
        ),
        table,
        [*g_list, tiles, *middle],
        specs_of(g_list, [tiles], middle),
        specs_of(sum_shapes, part_shapes),
        sum_shapes + part_shapes,
        scratch=[pltpu.VMEM((group_rows, features), F32), pltpu.VMEM(tiles_shape, F32)],
        cost=40_000_000,
    )
    (input_own, input_other), tile_terms = outs[:2], outs[2:]
    tile_terms = [
        tile_terms[chunk * len(weight_parts) : (chunk + 1) * len(weight_parts)]
        for chunk in range(chunks)
    ]

    def halves(parts):
        return swap(parts[3], "dp", 1), swap(parts[4], "dp", 2)

    def folded(parts, got_1, got_2):
        others = ((0, 0),) * 3
        to_2 = add(parts[2], jnp.pad(got_1, ((0, far - half), *others)))
        to_1 = add(parts[1], jnp.pad(got_2, ((half, 0), *others)))
        return to_1, to_2

    def summed(parts, to_1, to_2):
        from_1, from_2 = swap(to_1, "dp", 1), swap(to_2, "dp", 2)
        return [add(parts[0][at], from_1[at], from_2[at]) for at in range(far)]

    def sent_back(sums):
        return [sums[0]] + [swap(sums[at], "dp", at * near) for at in range(1, far)]

    if staged:
        first_parts, second_parts = tile_terms
        first_got, second_got = halves(first_parts), halves(second_parts)
        ffn_got = swap(ffn_near, "dp", near)
        ffn_last = to_far(ffn_own, ffn_core, ffn_got)
        ffn_far = swap(ffn_last, "dp", 2 * near)
        input_core, input_near = to_near(input_own, input_other)
        input_got = swap(input_near, "dp", near)
        first_sums = summed(first_parts, *folded(first_parts, *first_got))
        second_folded = after(folded(second_parts, *second_got), input_near)
        first_back = sent_back(after(tuple(first_sums), *second_folded))
        input_last = to_far(input_own, input_core, input_got)
        input_far = swap(input_last, "dp", 2 * near)
        second_sums = summed(second_parts, *second_folded)
        back = first_back + sent_back(after(tuple(second_sums), input_last))
        ffn_rows = add(ffn_own[0], ffn_core[0], ffn_got[0], ffn_far)
        input_rows = add(input_own[0], input_core[0], input_got[0], input_far)
    else:
        back = []
        for terms_of in tile_terms:
            if split:
                sums = summed(terms_of, *folded(terms_of, *halves(terms_of)))
            else:
                sums = scatter(dict(enumerate(terms_of)), "dp", near_strides)[0]
            back += sent_back(sums)
        ffn_rows = generic(ffn_own, ffn_other)
        input_rows = generic(input_own, input_other)

    grads = call(
        functools.partial(
            unpack, chunks=chunks, chunk_rows=chunk_rows, blocks=blocks, slot_count=slot_count
        ),
        table,
        back,
        specs_of(back),
        whole(tile_lines.shape),
        shape(tile_lines.shape, BF16),
        scratch=[pltpu.VMEM((row_share * terms * blocks_dev, tile), F32)],
        cost=2_000_000,
        vmem=24,
    )
    tile_grad = jnp.transpose(
        grads.reshape(row_share, 3, slot_count, blocks_dev, tile), (0, 1, 3, 2, 4)
    )
    return ffn_rows, input_rows, tile_grad


def solution(mesh):
    return jax.shard_map(
        shards,
        mesh=mesh,
        in_specs=(
            P(("dp", "tensor"), None),
            P(("dp", "tensor"), None),
            P("dp", None, "tensor", None, None),
            P(None, "tensor"),
            P(None, "tensor", None),
        ),
        out_specs=(
            P(("dp", "tensor"), None),
            P(("dp", "tensor"), None),
            P("dp", None, "tensor", None, None),
        ),
        check_vma=False,
    )
```

```python
import functools
import math

import jax
import jax.numpy as jnp
from jax import lax
from jax.experimental import pallas as pl
from jax.experimental.pallas import tpu as pltpu
from jax.sharding import PartitionSpec as P

F32 = jnp.float32
BF16 = jnp.bfloat16
PLAIN = (((1,), (0,)), ((), ()))
TURNED = (((1,), (1,)), ((), ()))
MIB = 1024 * 1024
UNROLL = 2
dot = functools.partial(lax.dot_general, preferred_element_type=F32)


def swap(value, axis, stride):
    size = lax.axis_size(axis)
    return lax.ppermute(value, axis, [(at, at ^ stride) for at in range(size)])


def after(value, *others):
    return lax.optimization_barrier((value, *others))[0]


def add(first, *others):
    total = first.astype(F32)
    for other in others:
        total = total + other.astype(F32)
    return total.astype(BF16)


def strides_of(size, unit=1):
    found = []
    step = size // 2
    while step >= 1:
        found.append(step * unit)
        step //= 2
    return found


def gather(items, axis, strides):
    for stride in strides:
        items = {**items, **{at ^ stride: swap(one, axis, stride) for at, one in items.items()}}
    return items


def scatter(items, axis, strides):
    for stride in reversed(strides):
        kept = {}
        for at, one in items.items():
            if not at & stride:
                kept[at] = add(one, swap(items[at ^ stride], axis, stride))
        items = kept
    return items


def whole(shape, at=None):
    at = (0,) * len(shape) if at is None else at
    return pl.BlockSpec(shape, lambda *_: at, pipeline_mode=pl.Buffered(1))


def pack(table, tiles, *refs, blocks, slot_count):
    outs, lines = refs[:-1], refs[-1]
    spare = outs[0].shape[0] - 1
    share, terms, blocks_dev, _ = tiles.shape
    for row in range(share):
        for term in range(terms):
            at = (row * terms + term) * blocks_dev
            lines[at : at + blocks_dev, :] = tiles[row, term].astype(F32)
    for at, out in enumerate(outs):

        def one(place, _, at=at, out=out):
            column = at * blocks + place
            block = table[0, column]
            for matrix in range(3):
                first, count = table[1 + matrix, column], table[4 + matrix, column]
                for slot in range(slot_count):
                    to = jnp.where(slot < count, first + slot, spare)
                    source = (matrix * slot_count + slot) * blocks_dev + block
                    out[to] = lines[pl.ds(source, share, stride=terms * blocks_dev), :].astype(BF16)
            return _

        lax.fori_loop(0, blocks, one, 0, unroll=True)


def unpack(table, *refs, chunks, chunk_rows, blocks, slot_count):
    out, lines, sources = refs[-2], refs[-1], refs[:-2]
    share, terms, blocks_dev, _ = out.shape
    far = len(sources) // chunks
    chunk_blocks = blocks // chunks
    for chunk in range(chunks):
        for at in range(far):
            ref = sources[chunk * far + at]

            def one(place, _, at=at, ref=ref, chunk=chunk):
                column = at * blocks + chunk * chunk_blocks + place
                block = table[0, column]
                for matrix in range(3):
                    first = table[1 + matrix, column] - chunk * chunk_rows
                    count = table[4 + matrix, column]
                    for slot in range(slot_count):
                        live = slot < count
                        value = ref[jnp.where(live, first + slot, 0)].astype(F32)
                        target = (matrix * slot_count + slot) * blocks_dev + block
                        lines[pl.ds(target, share, stride=terms * blocks_dev), :] = jnp.where(
                            live, value, 0.0
                        )
                return _

            lax.fori_loop(0, chunk_blocks, one, 0, unroll=True)
    for row in range(share):
        for term in range(terms):
            at = (row * terms + term) * blocks_dev
            out[row, term] = lines[at : at + blocks_dev, :].astype(BF16)


def offset_of(table, part, at, near, share):
    far_part = (part[1] + at) ^ table[16, 0]
    near_part = part[0] ^ table[16, 1]
    return pl.multiple_of((far_part * near + near_part) * share, share)


def assemble(table, *refs, weight_parts, near):
    weight_refs, out, tiles = refs[: len(weight_parts)], refs[-2], refs[-1]
    for ref, part in zip(weight_refs, weight_parts):
        share = ref.shape[2]
        for at in range(part[2]):
            offset = offset_of(table, part, at, near, share)
            tiles[:, pl.ds(offset, share), :] = ref[at].astype(F32)
    out[...] = tiles[...].astype(BF16)

    @pl.when(pl.program_id(0) == pl.num_programs(0) - 1)
    def _():
        out[out.shape[0] - 1] = jnp.zeros(out.shape[1:], BF16)


def places_of(table, block, slot_count, spare, base=0):
    places = []
    for matrix in range(3):
        first, count = table[1 + matrix, block] - base, table[4 + matrix, block]
        places += [jnp.where(slot < count, first + slot, spare) for slot in range(slot_count)]
    return places


def store_parts(total, own, other, parts):
    own_rows = own.shape[1]
    for at, (is_other, place) in enumerate(parts):
        ref = other if is_other else own
        ref[place] = total[at * own_rows : (at + 1) * own_rows, :].astype(BF16)


def tokens_at(refs, columns):
    return jnp.concatenate([ref[:, columns] for ref in refs], axis=0)


def columns_of(table, block, index, tile):
    return pl.ds(pl.multiple_of(table[7 + index, block] * tile, tile), tile)


def triples(slot_count):
    return [range(at * slot_count, (at + 1) * slot_count) for at in range(3)]


def in_turn(first, rest, blocks):
    group = max(size for size in range(1, UNROLL + 1) if blocks % size == 0)

    def some(at, _):
        held = first(at * group)
        for block in range(group):
            following = first(at * group + block + 1) if block + 1 < group else None
            rest(at * group + block, *held)
            held = following
        return _

    lax.fori_loop(0, blocks // group, some, 0)


def ahead(table, *refs, token_count, slot_count, parts):
    token_refs, refs = refs[:token_count], refs[token_count:]
    tiles, x_turned, gate_slope, gate_act_out, hidden_turned, ffn_own, ffn_other, ffn_sum = refs
    tile = tiles.shape[1]
    gate, up, down = triples(slot_count)

    for at in range(x_turned.shape[0] // tile):
        here = slice(at * tile, (at + 1) * tile)
        x_turned[here, :] = tokens_at(token_refs, here).T
    ffn_sum[...] = jnp.zeros_like(ffn_sum)

    def first(block):
        places = places_of(table, block, slot_count, tiles.shape[0] - 1)
        sums = []
        for indices in (gate, up):
            columns = [columns_of(table, block, index, tile) for index in indices]
            values = jnp.concatenate([tokens_at(token_refs, column) for column in columns], axis=1)
            weights = jnp.concatenate([tiles[places[index]] for index in indices], axis=0)
            sums.append(dot(values, weights, PLAIN))
        return places, *sums

    def rest(block, places, gate_pre, up_pre):
        gate_sig = jax.nn.sigmoid(gate_pre)
        gate_act = gate_pre * gate_sig
        hidden = (gate_act * up_pre).astype(BF16)
        gate_slope[block] = up_pre * gate_sig * (1.0 + gate_pre * (1.0 - gate_sig))
        gate_act_out[block] = gate_act
        hidden_turned[block] = hidden.T
        down_tiles = jnp.concatenate([tiles[places[index]] for index in down], axis=1)
        ffn = dot(hidden, down_tiles, PLAIN)
        for at, index in enumerate(down):
            ffn_sum[:, columns_of(table, block, index, tile)] += ffn[:, at * tile : (at + 1) * tile]

    in_turn(first, rest, gate_slope.shape[0])
    store_parts(ffn_sum, ffn_own, ffn_other, parts)


def behind(
    table, *refs, token_count, weight_parts, slot_count, grad_scale, near, chunks, chunk_rows, parts
):
    token_refs, refs = refs[:token_count], refs[token_count:]
    tiles, x_turned, gate_slope, gate_act, hidden_turned, input_own, input_other = refs[:7]
    grad_refs, input_sum, sums = refs[7:-2], refs[-2], refs[-1]
    tile = tiles.shape[1]
    gate, up, down = triples(slot_count)
    input_sum[...] = jnp.zeros_like(input_sum)

    def first(block):
        places = places_of(table, block, slot_count, tiles.shape[0] - 1)
        columns = [columns_of(table, block, index, tile) for index in range(3 * slot_count)]
        down_tiles = jnp.concatenate([tiles[places[index]] for index in down], axis=1)
        grad_in = jnp.concatenate([tokens_at(token_refs, columns[index]) for index in down], axis=1)
        return places, columns, grad_in, dot(grad_in, down_tiles, TURNED)

    def rest(block, places, columns, grad_in, hidden_grad):
        gate_grad = (hidden_grad * gate_slope[block]).astype(BF16)
        up_grad = (hidden_grad * gate_act[block]).astype(BF16)
        down_terms = dot(hidden_turned[block], grad_in, PLAIN) * grad_scale
        for at, index in enumerate(down):
            sums[places[index]] = down_terms[:, at * tile : (at + 1) * tile]
        for indices, grad in ((gate, gate_grad), (up, up_grad)):
            weights = jnp.concatenate([tiles[places[index]] for index in indices], axis=0)
            back = dot(grad, weights, TURNED)
            turned = jnp.concatenate([x_turned[columns[index], :] for index in indices], axis=0)
            terms = dot(turned, grad, PLAIN) * grad_scale
            for at, index in enumerate(indices):
                sums[places[index]] = terms[at * tile : (at + 1) * tile]
                input_sum[:, columns[index]] += back[:, at * tile : (at + 1) * tile]

    in_turn(first, rest, gate_slope.shape[0])
    store_parts(input_sum, input_own, input_other, parts)
    for chunk in range(chunks):
        rows = slice(chunk * chunk_rows, (chunk + 1) * chunk_rows)
        for index, part in enumerate(weight_parts):
            ref = grad_refs[chunk * len(weight_parts) + index]
            share = ref.shape[2]
            for at in range(part[2]):
                offset = offset_of(table, part, at, near, share)
                ref[at] = sums[rows, pl.ds(offset, share), :].astype(BF16)


def call(kernel, table, args, in_specs, out_specs, out_shape, grid=1, scratch=(), cost=0, vmem=40):
    return pl.pallas_call(
        kernel,
        grid_spec=pltpu.PrefetchScalarGridSpec(
            num_scalar_prefetch=1,
            grid=(grid,),
            in_specs=in_specs,
            out_specs=out_specs,
            scratch_shapes=scratch,
        ),
        out_shape=out_shape,
        compiler_params=pltpu.CompilerParams(vmem_limit_bytes=vmem * MIB),
        cost_estimate=pl.CostEstimate(flops=0, bytes_accessed=cost, transcendentals=0),
    )(table, *args)


def shards(tokens, out_grad, weight_tiles, tile_counts, tile_rows):
    row_share, _, blocks_dev, slot_count, tile = weight_tiles.shape
    own_rows, features = tokens.shape
    dp_size, tensor_size = lax.axis_size("dp"), lax.axis_size("tensor")
    far = math.gcd(4, math.gcd(dp_size, blocks_dev))
    near = dp_size // far
    blocks = blocks_dev // far
    chunks = math.gcd(2, blocks)
    chunk_blocks = blocks // chunks
    groups = far * chunks
    terms = 3 * slot_count
    grad_scale = 1.0 / math.sqrt(own_rows * tensor_size * dp_size)
    me = lax.axis_index("dp")
    far_at, near_at = me // near, me % near
    far_strides, near_strides = strides_of(far, near), strides_of(near)
    tensor_strides = strides_of(tensor_size)
    shape = jax.ShapeDtypeStruct

    x_items, g_items = {0: tokens}, {0: out_grad}
    if far > 1:
        x_items[near] = swap(tokens, "dp", near)

    capacity = (terms * blocks_dev - 3 * blocks_dev + 3 * (slot_count - 1) * (groups - 1)) // groups
    chunk_rows = capacity + 1
    block_ids = jnp.arange(blocks_dev, dtype=jnp.int32)
    load = tile_counts[0] + tile_counts[1] + tile_counts[2]
    earlier = (load[:, None] > load[None, :]) | (
        (load[:, None] == load[None, :]) & (block_ids[:, None] < block_ids[None, :])
    )
    rank = jnp.sum(earlier.astype(jnp.int32), axis=0)
    group = rank % groups
    before = (group[:, None] == group[None, :]) & (rank[:, None] < rank[None, :])
    start = jnp.sum(jnp.where(before, load[:, None], 0), axis=0) + (group // far) * chunk_rows
    ranks_of = (
        jnp.arange(chunk_blocks, dtype=jnp.int32)[None, None, :] * groups
        + jnp.arange(chunks, dtype=jnp.int32)[None, :, None] * far
        + (jnp.arange(far, dtype=jnp.int32)[:, None, None] ^ far_at)
    ).reshape(blocks_dev)
    columns = jnp.concatenate(
        [
            block_ids[None, :],
            start[None, :],
            (start + tile_counts[0])[None, :],
            (start + tile_counts[0] + tile_counts[1])[None, :],
            tile_counts,
            jnp.transpose(tile_rows, (0, 2, 1)).reshape(terms, blocks_dev),
        ]
    )
    table = jnp.sum(
        jnp.where(ranks_of[None, :, None] == rank[None, None, :], columns[:, None, :], 0), axis=2
    )
    place = jnp.where(block_ids == 0, far_at, near_at).astype(jnp.int32)
    table = jnp.concatenate([table, place[None, :]])

    tile_lines = jnp.transpose(weight_tiles, (0, 1, 3, 2, 4)).reshape(
        row_share, terms, blocks_dev, tile
    )
    slots = chunks * chunk_rows
    packed_shape = (slots, row_share, tile)
    chunk_shape = (chunk_rows, row_share, tile)
    packed = call(
        functools.partial(pack, blocks=blocks, slot_count=slot_count),
        table,
        [tile_lines],
        [whole(tile_lines.shape)],
        [whole(packed_shape)] * far,
        [shape(packed_shape, BF16)] * far,
        scratch=[pltpu.VMEM((row_share * terms * blocks_dev, tile), F32)],
        cost=1_000_000,
        vmem=24,
    )
    staged = tensor_size == 2 and far == 4 and near == 4 and chunks == 2
    if far > 1:
        packed = after(tuple(packed), x_items[near])
    received = [swap(packed[at], "dp", at * near) for at in reversed(range(1, far))][::-1]
    held = jnp.stack([packed[0], *received])
    x_core, g_core = {}, {}
    if staged:
        x_core = {at: swap(x_items[at], "tensor", 1) for at in (0, near)}
        g_core = {0: swap(out_grad, "tensor", 1)}
        held = after(held, *x_core.values(), *g_core.values())

    half = far // 2
    split = near == 4 and far % 2 == 0
    if split:
        from_1, from_2 = swap(held, "dp", 1), swap(held, "dp", 2)
        pass_1, pass_2 = from_1[:half], from_2[half:]
        weight_list = [held, from_1, from_2, swap(pass_1, "dp", 2), swap(pass_2, "dp", 1)]
        weight_parts = [(0, 0, far), (1, 0, far), (2, 0, far), (3, 0, half), (3, half, half)]
    else:
        items = gather({0: held}, "dp", near_strides)
        pass_1 = pass_2 = held
        weight_list = [items[at] for at in range(near)]
        weight_parts = [(at, 0, far) for at in range(near)]

    pairs = {}
    if staged:
        pair, g_source = after((jnp.concatenate([tokens, out_grad]), out_grad), held)
        pairs[2 * near] = swap(pair, "dp", 2 * near)
        g_items[near] = swap(g_source, "dp", near)
        source = after(pairs[2 * near], pass_1, pass_2, g_items[near])
        pairs[3 * near] = swap(source, "dp", near)
        g_core[near] = swap(g_items[near], "tensor", 1)
        pairs_core = {2 * near: swap(pairs[2 * near], "tensor", 1)}
        last = after(pairs[3 * near], *weight_list[3:], g_core[near], pairs_core[2 * near])
        pairs_core[3 * near] = swap(last, "tensor", 1)
    else:
        for items, value in ((x_items, tokens), (g_items, out_grad)):
            items.update(gather({0: value}, "dp", far_strides))

    far_order = [at * near for at in range(0, far, 2)] + [at * near for at in range(1, far, 2)]
    if staged:
        order = [at * near for at in range(far)]
        token_shape = (own_rows, features)
        singles = [x_items[0], x_items[near], x_core[0], x_core[near]]
        doubles = [pairs[at] for at in order[2:]] + [pairs_core[at] for at in order[2:]]
        x_list = singles[:2] + doubles[:2] + singles[2:] + doubles[2:]
        singles = [g_items[0], g_items[near], g_core[0], g_core[near]]
        g_list = singles[:2] + doubles[:2] + singles[2:] + doubles[2:]
        x_specs = [whole(token_shape)] * len(x_list)
        g_specs = [whole(token_shape, (1 if at in (2, 3, 6, 7) else 0, 0)) for at in range(len(g_list))]
        parts = [(other, far_order.index(at)) for other in (False, True) for at in order]
        other_parts = [(at, 1) for at in far_order]
    else:
        x_list, g_list, parts, other_parts = [], [], [], []
        for place, at in enumerate(far_order):
            x_parts = gather({0: x_items[at]}, "tensor", tensor_strides)
            g_parts = gather({0: g_items[at]}, "tensor", tensor_strides)
            for other in x_parts:
                parts.append((other != 0, len(other_parts) if other else place))
                if other:
                    other_parts.append((at, other))
                x_list.append(x_parts[other])
                g_list.append(g_parts[other])
        x_specs = g_specs = [whole((own_rows, features))] * len(x_list)

    group_rows = far * tensor_size * own_rows
    own_shape = (far, own_rows, features)
    other_shape = (len(other_parts), own_rows, features)
    steps = 2 if slots % 2 == 0 else 1
    tiles_shape = (slots, tile, tile)
    tiles = call(
        functools.partial(assemble, weight_parts=weight_parts, near=near),
        table,
        weight_list,
        [
            pl.BlockSpec((length, slots // steps, row_share, tile), lambda step, *_: (0, step, 0, 0))
            for _, _, length in weight_parts
        ],
        pl.BlockSpec((slots // steps, tile, tile), lambda step, *_: (step, 0, 0)),
        shape(tiles_shape, BF16),
        grid=steps,
        scratch=[pltpu.VMEM((slots // steps, tile, tile), F32)],
        cost=10_000_000,
        vmem=24,
    )
    def specs_of(*groups):
        return [whole(one.shape) for group in groups for one in group]

    middle_shapes = [
        shape((features, group_rows), BF16),
        shape((blocks, group_rows, tile), F32),
        shape((blocks, group_rows, tile), F32),
        shape((blocks, tile, group_rows), BF16),
    ]
    sum_shapes = [shape(own_shape, BF16), shape(other_shape, BF16)]
    outs = call(
        functools.partial(ahead, token_count=len(x_list), slot_count=slot_count, parts=parts),
        table,
        [*x_list, tiles],
        x_specs + specs_of([tiles]),
        specs_of(middle_shapes, sum_shapes),
        middle_shapes + sum_shapes,
        scratch=[pltpu.VMEM((group_rows, features), F32)],
        cost=30_000_000,
    )
    middle, (ffn_own, ffn_other) = outs[:4], outs[4:]

    def to_near(own_sums, other_sums):
        from_core = swap(other_sums, "tensor", 1)
        return from_core, add(own_sums[half:], from_core[half:])

    def to_far(own_sums, from_core, got):
        return add(own_sums[1], from_core[1], got[1])

    def generic(own_sums, other_sums):
        sums = {}
        for index, at in enumerate(far_order):
            items = {0: own_sums[index]}
            for other_index, (far_part, other) in enumerate(other_parts):
                if far_part == at:
                    items[other] = other_sums[other_index]
            sums[at] = scatter(items, "tensor", tensor_strides)[0]
        return scatter(sums, "dp", far_strides)[0]

    if staged:
        ffn_core, ffn_near = to_near(ffn_own, ffn_other)
        middle = after(tuple(middle), ffn_near)
    part_shapes = [
        shape((length,) + chunk_shape, BF16) for _ in range(chunks) for _, _, length in weight_parts
    ]
    outs = call(
        functools.partial(
            behind,
            token_count=len(g_list),
            weight_parts=weight_parts,
            slot_count=slot_count,
            grad_scale=grad_scale,
            near=near,
            chunks=chunks,
            chunk_rows=chunk_rows,
            parts=parts,
        ),
        table,
        [*g_list, tiles, *middle],
        g_specs + specs_of([tiles], middle),
        specs_of(sum_shapes, part_shapes),
        sum_shapes + part_shapes,
        scratch=[pltpu.VMEM((group_rows, features), F32), pltpu.VMEM(tiles_shape, F32)],
        cost=40_000_000,
    )
    (input_own, input_other), tile_terms = outs[:2], outs[2:]
    tile_terms = [
        tile_terms[chunk * len(weight_parts) : (chunk + 1) * len(weight_parts)]
        for chunk in range(chunks)
    ]

    def halves(parts):
        return swap(parts[3], "dp", 1), swap(parts[4], "dp", 2)

    def folded(parts, got_1, got_2):
        others = ((0, 0),) * 3
        to_2 = add(parts[2], jnp.pad(got_1, ((0, far - half), *others)))
        to_1 = add(parts[1], jnp.pad(got_2, ((half, 0), *others)))
        return to_1, to_2

    def summed(parts, to_1, to_2):
        from_1, from_2 = swap(to_1, "dp", 1), swap(to_2, "dp", 2)
        return [add(parts[0][at], from_1[at], from_2[at]) for at in range(far)]

    def sent_back(sums):
        return [sums[0]] + [swap(sums[at], "dp", at * near) for at in range(1, far)]

    if staged:
        ffn_got = swap(ffn_near, "dp", near)
        tile_terms, input_other = after((tile_terms, input_other), ffn_got)
        first_parts, second_parts = tile_terms
        first_got, second_got = halves(first_parts), halves(second_parts)
        ffn_last = to_far(ffn_own, ffn_core, ffn_got)
        ffn_far = swap(ffn_last, "dp", 2 * near)
        input_core, input_near = to_near(input_own, input_other)
        input_got = swap(input_near, "dp", near)
        first_sums = summed(first_parts, *folded(first_parts, *first_got))
        second_folded = after(folded(second_parts, *second_got), input_near)
        first_back = sent_back(after(tuple(first_sums), *second_folded, input_got))
        input_last = after(to_far(input_own, input_core, input_got), ffn_far)
        input_far = swap(input_last, "dp", 2 * near)
        second_sums = summed(second_parts, *second_folded)
        back = first_back + sent_back(after(tuple(second_sums), input_last))
        back = list(after(tuple(back), input_far))
        ffn_rows = add(ffn_own[0], ffn_core[0], ffn_got[0], ffn_far)
        input_rows = add(input_own[0], input_core[0], input_got[0], input_far)
    else:
        back = []
        for terms_of in tile_terms:
            if split:
                sums = summed(terms_of, *folded(terms_of, *halves(terms_of)))
            else:
                sums = scatter(dict(enumerate(terms_of)), "dp", near_strides)[0]
            back += sent_back(sums)
        ffn_rows = generic(ffn_own, ffn_other)
        input_rows = generic(input_own, input_other)

    grads = call(
        functools.partial(
            unpack, chunks=chunks, chunk_rows=chunk_rows, blocks=blocks, slot_count=slot_count
        ),
        table,
        back,
        specs_of(back),
        whole(tile_lines.shape),
        shape(tile_lines.shape, BF16),
        scratch=[pltpu.VMEM((row_share * terms * blocks_dev, tile), F32)],
        cost=2_000_000,
        vmem=24,
    )
    tile_grad = jnp.transpose(
        grads.reshape(row_share, 3, slot_count, blocks_dev, tile), (0, 1, 3, 2, 4)
    )
    return ffn_rows, input_rows, tile_grad


def solution(mesh):
    return jax.shard_map(
        shards,
        mesh=mesh,
        in_specs=(
            P(("dp", "tensor"), None),
            P(("dp", "tensor"), None),
            P("dp", None, "tensor", None, None),
            P(None, "tensor"),
            P(None, "tensor", None),
        ),
        out_specs=(
            P(("dp", "tensor"), None),
            P(("dp", "tensor"), None),
            P("dp", None, "tensor", None, None),
        ),
        check_vma=False,
    )
```

```python
import functools
import math

import jax
import jax.numpy as jnp
from jax import lax
from jax.experimental import pallas as pl
from jax.experimental.pallas import tpu as pltpu
from jax.sharding import PartitionSpec as P

F32 = jnp.float32
BF16 = jnp.bfloat16
PLAIN = (((1,), (0,)), ((), ()))
TURNED = (((1,), (1,)), ((), ()))
MIB = 1024 * 1024
UNROLL = 2
dot = functools.partial(lax.dot_general, preferred_element_type=F32)


def swap(value, axis, stride):
    size = lax.axis_size(axis)
    return lax.ppermute(value, axis, [(at, at ^ stride) for at in range(size)])


def after(value, *others):
    return lax.optimization_barrier((value, *others))[0]


def add(first, *others):
    total = first.astype(F32)
    for other in others:
        total = total + other.astype(F32)
    return total.astype(BF16)


def strides_of(size, unit=1):
    found = []
    step = size // 2
    while step >= 1:
        found.append(step * unit)
        step //= 2
    return found


def gather(items, axis, strides):
    for stride in strides:
        items = {**items, **{at ^ stride: swap(one, axis, stride) for at, one in items.items()}}
    return items


def scatter(items, axis, strides):
    for stride in reversed(strides):
        kept = {}
        for at, one in items.items():
            if not at & stride:
                kept[at] = add(one, swap(items[at ^ stride], axis, stride))
        items = kept
    return items


def whole(shape):
    return pl.BlockSpec(shape, lambda *_: (0,) * len(shape), pipeline_mode=pl.Buffered(1))


def pack(table, tiles, *refs, blocks, slot_count):
    outs, lines = refs[:-1], refs[-1]
    spare = outs[0].shape[0] - 1
    share, terms, blocks_dev, _ = tiles.shape
    for row in range(share):
        for term in range(terms):
            at = (row * terms + term) * blocks_dev
            lines[at : at + blocks_dev, :] = tiles[row, term].astype(F32)
    for at, out in enumerate(outs):

        def one(place, _, at=at, out=out):
            column = at * blocks + place
            block = table[0, column]
            for matrix in range(3):
                first, count = table[1 + matrix, column], table[4 + matrix, column]
                for slot in range(slot_count):
                    to = jnp.where(slot < count, first + slot, spare)
                    source = (matrix * slot_count + slot) * blocks_dev + block
                    out[to] = lines[pl.ds(source, share, stride=terms * blocks_dev), :].astype(BF16)
            return _

        lax.fori_loop(0, blocks, one, 0, unroll=True)


def unpack(table, *refs, chunks, chunk_rows, blocks, slot_count):
    out, lines, sources = refs[-2], refs[-1], refs[:-2]
    share, terms, blocks_dev, _ = out.shape
    far = len(sources) // chunks
    chunk_blocks = blocks // chunks
    for chunk in range(chunks):
        for at in range(far):
            ref = sources[chunk * far + at]

            def one(place, _, at=at, ref=ref, chunk=chunk):
                column = at * blocks + chunk * chunk_blocks + place
                block = table[0, column]
                for matrix in range(3):
                    first = table[1 + matrix, column] - chunk * chunk_rows
                    count = table[4 + matrix, column]
                    for slot in range(slot_count):
                        live = slot < count
                        value = ref[jnp.where(live, first + slot, 0)].astype(F32)
                        target = (matrix * slot_count + slot) * blocks_dev + block
                        lines[pl.ds(target, share, stride=terms * blocks_dev), :] = jnp.where(
                            live, value, 0.0
                        )
                return _

            lax.fori_loop(0, chunk_blocks, one, 0, unroll=True)
    for row in range(share):
        for term in range(terms):
            at = (row * terms + term) * blocks_dev
            out[row, term] = lines[at : at + blocks_dev, :].astype(BF16)


def offset_of(table, part, at, near, share):
    far_part = (part[1] + at) ^ table[16, 0]
    near_part = part[0] ^ table[16, 1]
    return pl.multiple_of((far_part * near + near_part) * share, share)


def assemble(table, *refs, weight_parts, near):
    weight_refs, out, tiles = refs[: len(weight_parts)], refs[-2], refs[-1]
    for ref, part in zip(weight_refs, weight_parts):
        share = ref.shape[2]
        for at in range(part[2]):
            offset = offset_of(table, part, at, near, share)
            tiles[:, pl.ds(offset, share), :] = ref[at].astype(F32)
    out[...] = tiles[...].astype(BF16)

    @pl.when(pl.program_id(0) == pl.num_programs(0) - 1)
    def _():
        out[out.shape[0] - 1] = jnp.zeros(out.shape[1:], BF16)


def places_of(table, block, slot_count, spare, base=0):
    places = []
    for matrix in range(3):
        first, count = table[1 + matrix, block] - base, table[4 + matrix, block]
        places += [jnp.where(slot < count, first + slot, spare) for slot in range(slot_count)]
    return places


def store_parts(total, own, other, parts):
    own_rows = own.shape[1]
    for at, (is_other, place) in enumerate(parts):
        ref = other if is_other else own
        ref[place] = total[at * own_rows : (at + 1) * own_rows, :].astype(BF16)


def tokens_at(refs, columns):
    return jnp.concatenate([ref[:, columns] for ref in refs], axis=0)


def columns_of(table, block, index, tile):
    return pl.ds(pl.multiple_of(table[7 + index, block] * tile, tile), tile)


def triples(slot_count):
    return [range(at * slot_count, (at + 1) * slot_count) for at in range(3)]


def in_turn(first, rest, blocks):
    group = max(size for size in range(1, UNROLL + 1) if blocks % size == 0)

    def some(at, _):
        held = first(at * group)
        for block in range(group):
            following = first(at * group + block + 1) if block + 1 < group else None
            rest(at * group + block, *held)
            held = following
        return _

    lax.fori_loop(0, blocks // group, some, 0)


def ahead(table, *refs, token_count, slot_count, parts):
    token_refs, refs = refs[:token_count], refs[token_count:]
    tiles, x_turned, gate_slope, gate_act_out, hidden_turned, ffn_own, ffn_other, ffn_sum = refs
    tile = tiles.shape[1]
    gate, up, down = triples(slot_count)

    for at in range(x_turned.shape[0] // tile):
        here = slice(at * tile, (at + 1) * tile)
        x_turned[here, :] = tokens_at(token_refs, here).T
    ffn_sum[...] = jnp.zeros_like(ffn_sum)

    def first(block):
        places = places_of(table, block, slot_count, tiles.shape[0] - 1)
        sums = []
        for indices in (gate, up):
            columns = [columns_of(table, block, index, tile) for index in indices]
            values = jnp.concatenate([tokens_at(token_refs, column) for column in columns], axis=1)
            weights = jnp.concatenate([tiles[places[index]] for index in indices], axis=0)
            sums.append(dot(values, weights, PLAIN))
        return places, *sums

    def rest(block, places, gate_pre, up_pre):
        gate_sig = jax.nn.sigmoid(gate_pre)
        gate_act = gate_pre * gate_sig
        hidden = (gate_act * up_pre).astype(BF16)
        gate_slope[block] = up_pre * gate_sig * (1.0 + gate_pre * (1.0 - gate_sig))
        gate_act_out[block] = gate_act
        hidden_turned[block] = hidden.T
        down_tiles = jnp.concatenate([tiles[places[index]] for index in down], axis=1)
        ffn = dot(hidden, down_tiles, PLAIN)
        for at, index in enumerate(down):
            ffn_sum[:, columns_of(table, block, index, tile)] += ffn[:, at * tile : (at + 1) * tile]

    in_turn(first, rest, gate_slope.shape[0])
    store_parts(ffn_sum, ffn_own, ffn_other, parts)


def behind(
    table, *refs, token_count, weight_parts, slot_count, grad_scale, near, chunks, chunk_rows, parts
):
    token_refs, refs = refs[:token_count], refs[token_count:]
    tiles, x_turned, gate_slope, gate_act, hidden_turned, input_own, input_other = refs[:7]
    grad_refs, input_sum, sums = refs[7:-2], refs[-2], refs[-1]
    tile = tiles.shape[1]
    gate, up, down = triples(slot_count)
    input_sum[...] = jnp.zeros_like(input_sum)

    def first(block):
        places = places_of(table, block, slot_count, tiles.shape[0] - 1)
        columns = [columns_of(table, block, index, tile) for index in range(3 * slot_count)]
        down_tiles = jnp.concatenate([tiles[places[index]] for index in down], axis=1)
        grad_in = jnp.concatenate([tokens_at(token_refs, columns[index]) for index in down], axis=1)
        return places, columns, grad_in, dot(grad_in, down_tiles, TURNED)

    def rest(block, places, columns, grad_in, hidden_grad):
        gate_grad = (hidden_grad * gate_slope[block]).astype(BF16)
        up_grad = (hidden_grad * gate_act[block]).astype(BF16)
        down_terms = dot(hidden_turned[block], grad_in, PLAIN) * grad_scale
        for at, index in enumerate(down):
            sums[places[index]] = down_terms[:, at * tile : (at + 1) * tile]
        for indices, grad in ((gate, gate_grad), (up, up_grad)):
            weights = jnp.concatenate([tiles[places[index]] for index in indices], axis=0)
            back = dot(grad, weights, TURNED)
            turned = jnp.concatenate([x_turned[columns[index], :] for index in indices], axis=0)
            terms = dot(turned, grad, PLAIN) * grad_scale
            for at, index in enumerate(indices):
                sums[places[index]] = terms[at * tile : (at + 1) * tile]
                input_sum[:, columns[index]] += back[:, at * tile : (at + 1) * tile]

    in_turn(first, rest, gate_slope.shape[0])
    store_parts(input_sum, input_own, input_other, parts)
    for chunk in range(chunks):
        rows = slice(chunk * chunk_rows, (chunk + 1) * chunk_rows)
        for index, part in enumerate(weight_parts):
            ref = grad_refs[chunk * len(weight_parts) + index]
            share = ref.shape[2]
            for at in range(part[2]):
                offset = offset_of(table, part, at, near, share)
                ref[at] = sums[rows, pl.ds(offset, share), :].astype(BF16)


def call(kernel, table, args, in_specs, out_specs, out_shape, grid=1, scratch=(), cost=0, vmem=40):
    return pl.pallas_call(
        kernel,
        grid_spec=pltpu.PrefetchScalarGridSpec(
            num_scalar_prefetch=1,
            grid=(grid,),
            in_specs=in_specs,
            out_specs=out_specs,
            scratch_shapes=scratch,
        ),
        out_shape=out_shape,
        compiler_params=pltpu.CompilerParams(vmem_limit_bytes=vmem * MIB),
        cost_estimate=pl.CostEstimate(flops=0, bytes_accessed=cost, transcendentals=0),
    )(table, *args)


def shards(tokens, out_grad, weight_tiles, tile_counts, tile_rows):
    row_share, _, blocks_dev, slot_count, tile = weight_tiles.shape
    own_rows, features = tokens.shape
    dp_size, tensor_size = lax.axis_size("dp"), lax.axis_size("tensor")
    far = math.gcd(4, math.gcd(dp_size, blocks_dev))
    near = dp_size // far
    blocks = blocks_dev // far
    chunks = 1
    chunk_blocks = blocks // chunks
    groups = far * chunks
    terms = 3 * slot_count
    grad_scale = 1.0 / math.sqrt(own_rows * tensor_size * dp_size)
    me = lax.axis_index("dp")
    far_at, near_at = me // near, me % near
    far_strides, near_strides = strides_of(far, near), strides_of(near)
    tensor_strides = strides_of(tensor_size)
    shape = jax.ShapeDtypeStruct

    x_items, g_items = {0: tokens}, {0: out_grad}
    if far > 1:
        x_items[near] = swap(tokens, "dp", near)

    capacity = (terms * blocks_dev - 3 * blocks_dev + 3 * (slot_count - 1) * (groups - 1)) // groups
    chunk_rows = capacity + 1
    block_ids = jnp.arange(blocks_dev, dtype=jnp.int32)
    load = tile_counts[0] + tile_counts[1] + tile_counts[2]
    earlier = (load[:, None] > load[None, :]) | (
        (load[:, None] == load[None, :]) & (block_ids[:, None] < block_ids[None, :])
    )
    rank = jnp.sum(earlier.astype(jnp.int32), axis=0)
    group = rank % groups
    before = (group[:, None] == group[None, :]) & (rank[:, None] < rank[None, :])
    start = jnp.sum(jnp.where(before, load[:, None], 0), axis=0) + (group // far) * chunk_rows
    ranks_of = (
        jnp.arange(chunk_blocks, dtype=jnp.int32)[None, None, :] * groups
        + jnp.arange(chunks, dtype=jnp.int32)[None, :, None] * far
        + (jnp.arange(far, dtype=jnp.int32)[:, None, None] ^ far_at)
    ).reshape(blocks_dev)
    columns = jnp.concatenate(
        [
            block_ids[None, :],
            start[None, :],
            (start + tile_counts[0])[None, :],
            (start + tile_counts[0] + tile_counts[1])[None, :],
            tile_counts,
            jnp.transpose(tile_rows, (0, 2, 1)).reshape(terms, blocks_dev),
        ]
    )
    table = jnp.sum(
        jnp.where(ranks_of[None, :, None] == rank[None, None, :], columns[:, None, :], 0), axis=2
    )
    place = jnp.where(block_ids == 0, far_at, near_at).astype(jnp.int32)
    table = jnp.concatenate([table, place[None, :]])

    tile_lines = jnp.transpose(weight_tiles, (0, 1, 3, 2, 4)).reshape(
        row_share, terms, blocks_dev, tile
    )
    slots = chunks * chunk_rows
    packed_shape = (slots, row_share, tile)
    chunk_shape = (chunk_rows, row_share, tile)
    packed = call(
        functools.partial(pack, blocks=blocks, slot_count=slot_count),
        table,
        [tile_lines],
        [whole(tile_lines.shape)],
        [whole(packed_shape)] * far,
        [shape(packed_shape, BF16)] * far,
        scratch=[pltpu.VMEM((row_share * terms * blocks_dev, tile), F32)],
        cost=1_000_000,
        vmem=24,
    )
    staged = tensor_size == 2 and far == 4 and near == 4
    if far > 1:
        packed = after(tuple(packed), x_items[near])
    received = [swap(packed[at], "dp", at * near) for at in reversed(range(1, far))][::-1]
    held = jnp.stack([packed[0], *received])
    x_core, g_core = {}, {}
    if staged:
        x_core = {at: swap(x_items[at], "tensor", 1) for at in (0, near)}
        g_core = {0: swap(out_grad, "tensor", 1)}
        held = after(held, *x_core.values(), *g_core.values())

    half = far // 2
    split = near == 4 and far % 2 == 0
    if split:
        from_1, from_2 = swap(held, "dp", 1), swap(held, "dp", 2)
        pass_1, pass_2 = from_1[:half], from_2[half:]
        weight_list = [held, from_1, from_2, swap(pass_1, "dp", 2), swap(pass_2, "dp", 1)]
        weight_parts = [(0, 0, far), (1, 0, far), (2, 0, far), (3, 0, half), (3, half, half)]
    else:
        items = gather({0: held}, "dp", near_strides)
        pass_1 = pass_2 = held
        weight_list = [items[at] for at in range(near)]
        weight_parts = [(at, 0, far) for at in range(near)]

    if staged:
        x_source, g_source = after((tokens, out_grad), held)
        x_items[2 * near] = swap(x_source, "dp", 2 * near)
        g_items[near] = swap(g_source, "dp", near)
        x_source, g_source = after((x_items[2 * near], out_grad), x_items[2 * near], g_items[near])
        x_items[3 * near] = swap(x_source, "dp", near)
        g_items[2 * near] = swap(g_source, "dp", 2 * near)
        g_items[3 * near] = swap(g_items[2 * near], "dp", near)
        x_late = jnp.concatenate([x_items[2 * near], x_items[3 * near]])
        x_late = swap(after(x_late, *weight_list[3:], g_items[2 * near]), "tensor", 1)
        g_late = jnp.concatenate([g_items[at * near] for at in range(1, far)])
        g_late = swap(g_late, "tensor", 1)
    else:
        for items, value in ((x_items, tokens), (g_items, out_grad)):
            items.update(gather({0: value}, "dp", far_strides))

    far_order = [at * near for at in range(0, far, 2)] + [at * near for at in range(1, far, 2)]
    if staged:
        order = [at * near for at in range(far)]
        x_list = [x_items[at] for at in order] + [x_core[at] for at in order[:2]] + [x_late]
        g_list = [g_items[at] for at in order] + [g_core[0], g_late]
        parts = [(other, far_order.index(at)) for other in (False, True) for at in order]
        other_parts = [(at, 1) for at in far_order]
    else:
        x_list, g_list, parts, other_parts = [], [], [], []
        for place, at in enumerate(far_order):
            x_parts = gather({0: x_items[at]}, "tensor", tensor_strides)
            g_parts = gather({0: g_items[at]}, "tensor", tensor_strides)
            for other in x_parts:
                parts.append((other != 0, len(other_parts) if other else place))
                if other:
                    other_parts.append((at, other))
                x_list.append(x_parts[other])
                g_list.append(g_parts[other])

    group_rows = far * tensor_size * own_rows
    own_shape = (far, own_rows, features)
    other_shape = (len(other_parts), own_rows, features)
    steps = 2 if slots % 2 == 0 else 1
    tiles_shape = (slots, tile, tile)
    tiles = call(
        functools.partial(assemble, weight_parts=weight_parts, near=near),
        table,
        weight_list,
        [
            pl.BlockSpec((length, slots // steps, row_share, tile), lambda step, *_: (0, step, 0, 0))
            for _, _, length in weight_parts
        ],
        pl.BlockSpec((slots // steps, tile, tile), lambda step, *_: (step, 0, 0)),
        shape(tiles_shape, BF16),
        grid=steps,
        scratch=[pltpu.VMEM((slots // steps, tile, tile), F32)],
        cost=10_000_000,
        vmem=24,
    )
    def specs_of(*groups):
        return [whole(one.shape) for group in groups for one in group]

    middle_shapes = [
        shape((features, group_rows), BF16),
        shape((blocks, group_rows, tile), F32),
        shape((blocks, group_rows, tile), F32),
        shape((blocks, tile, group_rows), BF16),
    ]
    sum_shapes = [shape(own_shape, BF16), shape(other_shape, BF16)]
    outs = call(
        functools.partial(ahead, token_count=len(x_list), slot_count=slot_count, parts=parts),
        table,
        [*x_list, tiles],
        specs_of(x_list, [tiles]),
        specs_of(middle_shapes, sum_shapes),
        middle_shapes + sum_shapes,
        scratch=[pltpu.VMEM((group_rows, features), F32)],
        cost=30_000_000,
    )
    middle, (ffn_own, ffn_other) = outs[:4], outs[4:]

    def to_near(own_sums, other_sums):
        from_core = swap(other_sums, "tensor", 1)
        return from_core, add(own_sums[half:], from_core[half:])

    def to_far(own_sums, from_core, got):
        return add(own_sums[1], from_core[1], got[1])

    def generic(own_sums, other_sums):
        sums = {}
        for index, at in enumerate(far_order):
            items = {0: own_sums[index]}
            for other_index, (far_part, other) in enumerate(other_parts):
                if far_part == at:
                    items[other] = other_sums[other_index]
            sums[at] = scatter(items, "tensor", tensor_strides)[0]
        return scatter(sums, "dp", far_strides)[0]

    if staged:
        ffn_core, ffn_near = to_near(ffn_own, after(ffn_other, g_items[3 * near]))
        middle = after(tuple(middle), ffn_near)
    part_shapes = [
        shape((length,) + chunk_shape, BF16) for _ in range(chunks) for _, _, length in weight_parts
    ]
    outs = call(
        functools.partial(
            behind,
            token_count=len(g_list),
            weight_parts=weight_parts,
            slot_count=slot_count,
            grad_scale=grad_scale,
            near=near,
            chunks=chunks,
            chunk_rows=chunk_rows,
            parts=parts,
        ),
        table,
        [*g_list, tiles, *middle],
        specs_of(g_list, [tiles], middle),
        specs_of(sum_shapes, part_shapes),
        sum_shapes + part_shapes,
        scratch=[pltpu.VMEM((group_rows, features), F32), pltpu.VMEM(tiles_shape, F32)],
        cost=40_000_000,
    )
    (input_own, input_other), tile_terms = outs[:2], outs[2:]
    tile_terms = [
        tile_terms[chunk * len(weight_parts) : (chunk + 1) * len(weight_parts)]
        for chunk in range(chunks)
    ]

    def halves(parts):
        return swap(parts[3], "dp", 1), swap(parts[4], "dp", 2)

    def folded(parts, got_1, got_2):
        others = ((0, 0),) * 3
        to_2 = add(parts[2], jnp.pad(got_1, ((0, far - half), *others)))
        to_1 = add(parts[1], jnp.pad(got_2, ((half, 0), *others)))
        return to_1, to_2

    def summed(parts, to_1, to_2):
        from_1, from_2 = swap(to_1, "dp", 1), swap(to_2, "dp", 2)
        return [add(parts[0][at], from_1[at], from_2[at]) for at in range(far)]

    def sent_back(sums):
        return [sums[0]] + [swap(sums[at], "dp", at * near) for at in range(1, far)]

    if staged:
        ffn_got = swap(ffn_near, "dp", near)
        tile_terms, input_other = after((tile_terms, input_other), ffn_got)
        (tile_terms,) = tile_terms
        got = halves(tile_terms)
        ffn_last = to_far(ffn_own, ffn_core, ffn_got)
        ffn_far = swap(ffn_last, "dp", 2 * near)
        input_core, input_near = to_near(input_own, input_other)
        input_got = swap(input_near, "dp", near)
        to_1, to_2 = after(folded(tile_terms, *got), input_near, ffn_far)
        input_last = to_far(input_own, input_core, input_got)
        input_far = swap(input_last, "dp", 2 * near)
        sums = after(tuple(summed(tile_terms, to_1, to_2)), input_last)
        back = list(after(tuple(sent_back(sums)), input_far))
        ffn_rows = add(ffn_own[0], ffn_core[0], ffn_got[0], ffn_far)
        input_rows = add(input_own[0], input_core[0], input_got[0], input_far)
    else:
        back = []
        for terms_of in tile_terms:
            if split:
                sums = summed(terms_of, *folded(terms_of, *halves(terms_of)))
            else:
                sums = scatter(dict(enumerate(terms_of)), "dp", near_strides)[0]
            back += sent_back(sums)
        ffn_rows = generic(ffn_own, ffn_other)
        input_rows = generic(input_own, input_other)

    grads = call(
        functools.partial(
            unpack, chunks=chunks, chunk_rows=chunk_rows, blocks=blocks, slot_count=slot_count
        ),
        table,
        back,
        specs_of(back),
        whole(tile_lines.shape),
        shape(tile_lines.shape, BF16),
        scratch=[pltpu.VMEM((row_share * terms * blocks_dev, tile), F32)],
        cost=2_000_000,
        vmem=24,
    )
    tile_grad = jnp.transpose(
        grads.reshape(row_share, 3, slot_count, blocks_dev, tile), (0, 1, 3, 2, 4)
    )
    return ffn_rows, input_rows, tile_grad


def solution(mesh):
    return jax.shard_map(
        shards,
        mesh=mesh,
        in_specs=(
            P(("dp", "tensor"), None),
            P(("dp", "tensor"), None),
            P("dp", None, "tensor", None, None),
            P(None, "tensor"),
            P(None, "tensor", None),
        ),
        out_specs=(
            P(("dp", "tensor"), None),
            P(("dp", "tensor"), None),
            P("dp", None, "tensor", None, None),
        ),
        check_vma=False,
    )
```

```python
import functools
import math

import jax
import jax.numpy as jnp
from jax import lax
from jax.experimental import pallas as pl
from jax.experimental.pallas import tpu as pltpu
from jax.sharding import PartitionSpec as P

F32 = jnp.float32
BF16 = jnp.bfloat16
PLAIN = (((1,), (0,)), ((), ()))
TURNED = (((1,), (1,)), ((), ()))
MIB = 1024 * 1024
UNROLL = 7
dot = functools.partial(lax.dot_general, preferred_element_type=F32)


def swap(value, axis, stride):
    size = lax.axis_size(axis)
    return lax.ppermute(value, axis, [(at, at ^ stride) for at in range(size)])


def after(value, *others):
    return lax.optimization_barrier((value, *others))[0]


def add(first, *others):
    total = first.astype(F32)
    for other in others:
        total = total + other.astype(F32)
    return total.astype(BF16)


def strides_of(size, unit=1):
    found = []
    step = size // 2
    while step >= 1:
        found.append(step * unit)
        step //= 2
    return found


def gather(items, axis, strides):
    for stride in strides:
        items = {**items, **{at ^ stride: swap(one, axis, stride) for at, one in items.items()}}
    return items


def scatter(items, axis, strides):
    for stride in reversed(strides):
        kept = {}
        for at, one in items.items():
            if not at & stride:
                kept[at] = add(one, swap(items[at ^ stride], axis, stride))
        items = kept
    return items


def whole(shape):
    return pl.BlockSpec(shape, lambda *_: (0,) * len(shape), pipeline_mode=pl.Buffered(1))


def pack(table, tiles, *refs, blocks, slot_count):
    outs, lines = refs[:-1], refs[-1]
    spare = outs[0].shape[0] - 1
    share, terms, blocks_dev, _ = tiles.shape
    for row in range(share):
        for term in range(terms):
            at = (row * terms + term) * blocks_dev
            lines[at : at + blocks_dev, :] = tiles[row, term].astype(F32)
    for at, out in enumerate(outs):

        def one(place, _, at=at, out=out):
            column = at * blocks + place
            block = table[0, column]
            for matrix in range(3):
                first, count = table[1 + matrix, column], table[4 + matrix, column]
                for slot in range(slot_count):
                    to = jnp.where(slot < count, first + slot, spare)
                    source = (matrix * slot_count + slot) * blocks_dev + block
                    out[to] = lines[pl.ds(source, share, stride=terms * blocks_dev), :].astype(BF16)
            return _

        lax.fori_loop(0, blocks, one, 0, unroll=True)


def unpack(table, *refs, blocks, slot_count):
    out, lines, sources = refs[-2], refs[-1], refs[:-2]
    share, terms, blocks_dev, _ = out.shape
    for at, ref in enumerate(sources):

        def one(place, _, at=at, ref=ref):
            column = at * blocks + place
            block = table[0, column]
            for matrix in range(3):
                first, count = table[1 + matrix, column], table[4 + matrix, column]
                for slot in range(slot_count):
                    live = slot < count
                    value = ref[jnp.where(live, first + slot, 0)].astype(F32)
                    target = (matrix * slot_count + slot) * blocks_dev + block
                    lines[pl.ds(target, share, stride=terms * blocks_dev), :] = jnp.where(
                        live, value, 0.0
                    )
            return _

        lax.fori_loop(0, blocks, one, 0, unroll=True)
    for row in range(share):
        for term in range(terms):
            at = (row * terms + term) * blocks_dev
            out[row, term] = lines[at : at + blocks_dev, :].astype(BF16)


def offset_of(table, part, at, near, share):
    far_part = (part[1] + at) ^ table[16, 0]
    near_part = part[0] ^ table[16, 1]
    return pl.multiple_of((far_part * near + near_part) * share, share)


def assemble(table, *refs, weight_parts, near):
    weight_refs, out, tiles = refs[: len(weight_parts)], refs[-2], refs[-1]
    for ref, part in zip(weight_refs, weight_parts):
        share = ref.shape[2]
        for at in range(part[2]):
            offset = offset_of(table, part, at, near, share)
            tiles[:, pl.ds(offset, share), :] = ref[at].astype(F32)
    out[...] = tiles[...].astype(BF16)

    @pl.when(pl.program_id(0) == pl.num_programs(0) - 1)
    def _():
        out[out.shape[0] - 1] = jnp.zeros(out.shape[1:], BF16)


def places_of(table, block, slot_count, spare):
    places = []
    for matrix in range(3):
        first, count = table[1 + matrix, block], table[4 + matrix, block]
        places += [jnp.where(slot < count, first + slot, spare) for slot in range(slot_count)]
    return places


def store_parts(total, own, other, parts):
    own_rows = own.shape[1]
    for at, (is_other, place) in enumerate(parts):
        ref = other if is_other else own
        ref[place] = total[at * own_rows : (at + 1) * own_rows, :].astype(BF16)


def tokens_at(refs, columns):
    return jnp.concatenate([ref[:, columns] for ref in refs], axis=0)


def columns_of(table, block, index, tile):
    return pl.ds(pl.multiple_of(table[7 + index, block] * tile, tile), tile)


def triples(slot_count):
    return [range(at * slot_count, (at + 1) * slot_count) for at in range(3)]


def in_turn(first, rest, blocks):
    group = max(size for size in range(1, UNROLL + 1) if blocks % size == 0)

    def some(at, _):
        held = first(at * group)
        for block in range(group):
            following = first(at * group + block + 1) if block + 1 < group else None
            rest(at * group + block, *held)
            held = following
        return _

    lax.fori_loop(0, blocks // group, some, 0)


def ahead(table, *refs, token_count, slot_count, parts):
    token_refs, refs = refs[:token_count], refs[token_count:]
    tiles, x_turned, gate_slope, gate_act_out, hidden_turned, ffn_own, ffn_other, ffn_sum = refs
    tile = tiles.shape[1]
    gate, up, down = triples(slot_count)

    for at in range(x_turned.shape[0] // tile):
        here = slice(at * tile, (at + 1) * tile)
        x_turned[here, :] = tokens_at(token_refs, here).T
    ffn_sum[...] = jnp.zeros_like(ffn_sum)

    def first(block):
        places = places_of(table, block, slot_count, tiles.shape[0] - 1)
        sums = []
        for indices in (gate, up):
            columns = [columns_of(table, block, index, tile) for index in indices]
            values = jnp.concatenate([tokens_at(token_refs, column) for column in columns], axis=1)
            weights = jnp.concatenate([tiles[places[index]] for index in indices], axis=0)
            sums.append(dot(values, weights, PLAIN))
        return places, *sums

    def rest(block, places, gate_pre, up_pre):
        gate_sig = jax.nn.sigmoid(gate_pre)
        gate_act = gate_pre * gate_sig
        hidden = (gate_act * up_pre).astype(BF16)
        gate_slope[block] = up_pre * gate_sig * (1.0 + gate_pre * (1.0 - gate_sig))
        gate_act_out[block] = gate_act
        hidden_turned[block] = hidden.T
        down_tiles = jnp.concatenate([tiles[places[index]] for index in down], axis=1)
        ffn = dot(hidden, down_tiles, PLAIN)
        for at, index in enumerate(down):
            ffn_sum[:, columns_of(table, block, index, tile)] += ffn[:, at * tile : (at + 1) * tile]

    in_turn(first, rest, gate_slope.shape[0])
    store_parts(ffn_sum, ffn_own, ffn_other, parts)


def behind(table, *refs, token_count, weight_parts, slot_count, grad_scale, near, parts):
    token_refs, refs = refs[:token_count], refs[token_count:]
    tiles, x_turned, gate_slope, gate_act, hidden_turned, input_own, input_other = refs[:7]
    grad_refs, input_sum, sums = refs[7:-2], refs[-2], refs[-1]
    tile = tiles.shape[1]
    gate, up, down = triples(slot_count)
    input_sum[...] = jnp.zeros_like(input_sum)

    def first(block):
        places = places_of(table, block, slot_count, tiles.shape[0] - 1)
        columns = [columns_of(table, block, index, tile) for index in range(3 * slot_count)]
        down_tiles = jnp.concatenate([tiles[places[index]] for index in down], axis=1)
        grad_in = jnp.concatenate([tokens_at(token_refs, columns[index]) for index in down], axis=1)
        return places, columns, grad_in, dot(grad_in, down_tiles, TURNED)

    def rest(block, places, columns, grad_in, hidden_grad):
        gate_grad = (hidden_grad * gate_slope[block]).astype(BF16)
        up_grad = (hidden_grad * gate_act[block]).astype(BF16)
        down_terms = dot(hidden_turned[block], grad_in, PLAIN) * grad_scale
        for at, index in enumerate(down):
            sums[places[index]] = down_terms[:, at * tile : (at + 1) * tile]
        for indices, grad in ((gate, gate_grad), (up, up_grad)):
            weights = jnp.concatenate([tiles[places[index]] for index in indices], axis=0)
            back = dot(grad, weights, TURNED)
            turned = jnp.concatenate([x_turned[columns[index], :] for index in indices], axis=0)
            terms = dot(turned, grad, PLAIN) * grad_scale
            for at, index in enumerate(indices):
                sums[places[index]] = terms[at * tile : (at + 1) * tile]
                input_sum[:, columns[index]] += back[:, at * tile : (at + 1) * tile]

    in_turn(first, rest, gate_slope.shape[0])
    store_parts(input_sum, input_own, input_other, parts)
    for ref, part in zip(grad_refs, weight_parts):
        share = ref.shape[2]
        for at in range(part[2]):
            offset = offset_of(table, part, at, near, share)
            ref[at] = sums[:, pl.ds(offset, share), :].astype(BF16)


def fold(table, part_1, part_2, got_1, got_2, out_1, out_2):
    half = got_1.shape[0]
    out_2[:half] = add(part_2[:half], got_1[...])
    out_2[half:] = part_2[half:]
    out_1[:half] = part_1[:half]
    out_1[half:] = add(part_1[half:], got_2[...])


def call(kernel, table, args, in_specs, out_specs, out_shape, grid=1, scratch=(), cost=0, vmem=40):
    return pl.pallas_call(
        kernel,
        grid_spec=pltpu.PrefetchScalarGridSpec(
            num_scalar_prefetch=1,
            grid=(grid,),
            in_specs=in_specs,
            out_specs=out_specs,
            scratch_shapes=scratch,
        ),
        out_shape=out_shape,
        compiler_params=pltpu.CompilerParams(vmem_limit_bytes=vmem * MIB),
        cost_estimate=pl.CostEstimate(flops=0, bytes_accessed=cost, transcendentals=0),
    )(table, *args)


def shards(tokens, out_grad, weight_tiles, tile_counts, tile_rows):
    row_share, _, blocks_dev, slot_count, tile = weight_tiles.shape
    own_rows, features = tokens.shape
    dp_size, tensor_size = lax.axis_size("dp"), lax.axis_size("tensor")
    far = math.gcd(4, math.gcd(dp_size, blocks_dev))
    near = dp_size // far
    blocks = blocks_dev // far
    terms = 3 * slot_count
    grad_scale = 1.0 / math.sqrt(own_rows * tensor_size * dp_size)
    me = lax.axis_index("dp")
    far_at, near_at = me // near, me % near
    far_strides, near_strides = strides_of(far, near), strides_of(near)
    tensor_strides = strides_of(tensor_size)
    shape = jax.ShapeDtypeStruct

    x_items, g_items = {0: tokens}, {0: out_grad}
    if far > 1:
        x_items[near] = swap(tokens, "dp", near)

    capacity = (terms * blocks_dev - 3 * blocks_dev + 3 * (slot_count - 1) * (far - 1)) // far
    slots = capacity + 1
    block_ids = jnp.arange(blocks_dev, dtype=jnp.int32)
    load = tile_counts[0] + tile_counts[1] + tile_counts[2]
    earlier = (load[:, None] > load[None, :]) | (
        (load[:, None] == load[None, :]) & (block_ids[:, None] < block_ids[None, :])
    )
    rank = jnp.sum(earlier.astype(jnp.int32), axis=0)
    home = rank % far
    before = (home[:, None] == home[None, :]) & (rank[:, None] < rank[None, :])
    start = jnp.sum(jnp.where(before, load[:, None], 0), axis=0)
    ranks_of = (
        jnp.arange(blocks, dtype=jnp.int32)[None, :] * far
        + (jnp.arange(far, dtype=jnp.int32)[:, None] ^ far_at)
    ).reshape(blocks_dev)
    columns = jnp.concatenate(
        [
            block_ids[None, :],
            start[None, :],
            (start + tile_counts[0])[None, :],
            (start + tile_counts[0] + tile_counts[1])[None, :],
            tile_counts,
            jnp.transpose(tile_rows, (0, 2, 1)).reshape(terms, blocks_dev),
        ]
    )
    table = jnp.sum(
        jnp.where(ranks_of[None, :, None] == rank[None, None, :], columns[:, None, :], 0), axis=2
    )
    place = jnp.where(block_ids == 0, far_at, near_at).astype(jnp.int32)
    table = jnp.concatenate([table, place[None, :]])

    tile_lines = jnp.transpose(weight_tiles, (0, 1, 3, 2, 4)).reshape(
        row_share, terms, blocks_dev, tile
    )
    packed_shape = (slots, row_share, tile)
    packed = call(
        functools.partial(pack, blocks=blocks, slot_count=slot_count),
        table,
        [tile_lines],
        [whole(tile_lines.shape)],
        [whole(packed_shape)] * far,
        [shape(packed_shape, BF16)] * far,
        scratch=[pltpu.VMEM((row_share * terms * blocks_dev, tile), F32)],
        cost=1_000_000,
        vmem=24,
    )
    staged = tensor_size == 2 and far == 4 and near == 4
    received = [swap(packed[at], "dp", at * near) for at in reversed(range(1, far))][::-1]
    held = jnp.stack([packed[0], *received])
    x_core, g_core = {}, {}
    if staged:
        x_core = {at: swap(x_items[at], "tensor", 1) for at in (0, near)}
        g_core = {0: swap(out_grad, "tensor", 1)}
        held = after(held, *x_core.values(), *g_core.values())

    half = far // 2
    split = near == 4 and far % 2 == 0
    if split:
        from_1, from_2 = swap(held, "dp", 1), swap(held, "dp", 2)
        pass_1, pass_2 = from_1[:half], from_2[half:]
        weight_list = [held, from_1, from_2, swap(pass_1, "dp", 2), swap(pass_2, "dp", 1)]
        weight_parts = [(0, 0, far), (1, 0, far), (2, 0, far), (3, 0, half), (3, half, half)]
    else:
        items = gather({0: held}, "dp", near_strides)
        pass_1 = pass_2 = held
        weight_list = [items[at] for at in range(near)]
        weight_parts = [(at, 0, far) for at in range(near)]

    if staged:
        x_source, g_source = after((tokens, out_grad), held)
        x_items[2 * near] = swap(x_source, "dp", 2 * near)
        g_items[near] = swap(g_source, "dp", near)
        x_source, g_source = after((x_items[2 * near], out_grad), x_items[2 * near], g_items[near])
        x_items[3 * near] = swap(x_source, "dp", near)
        g_items[2 * near] = swap(g_source, "dp", 2 * near)
        g_items[3 * near] = swap(g_items[2 * near], "dp", near)
        x_late = jnp.concatenate([x_items[2 * near], x_items[3 * near]])
        x_late = swap(after(x_late, *weight_list[3:], g_items[2 * near]), "tensor", 1)
        g_late = jnp.concatenate([g_items[at * near] for at in range(1, far)])
        g_late = swap(g_late, "tensor", 1)
    else:
        for items, value in ((x_items, tokens), (g_items, out_grad)):
            items.update(gather({0: value}, "dp", far_strides))

    far_order = [at * near for at in range(0, far, 2)] + [at * near for at in range(1, far, 2)]
    if staged:
        order = [at * near for at in range(far)]
        x_list = [x_items[at] for at in order] + [x_core[at] for at in order[:2]] + [x_late]
        g_list = [g_items[at] for at in order] + [g_core[0], g_late]
        parts = [(other, far_order.index(at)) for other in (False, True) for at in order]
        other_parts = [(at, 1) for at in far_order]
    else:
        x_list, g_list, parts, other_parts = [], [], [], []
        for place, at in enumerate(far_order):
            x_parts = gather({0: x_items[at]}, "tensor", tensor_strides)
            g_parts = gather({0: g_items[at]}, "tensor", tensor_strides)
            for other in x_parts:
                parts.append((other != 0, len(other_parts) if other else place))
                if other:
                    other_parts.append((at, other))
                x_list.append(x_parts[other])
                g_list.append(g_parts[other])

    group_rows = far * tensor_size * own_rows
    own_shape = (far, own_rows, features)
    other_shape = (len(other_parts), own_rows, features)
    steps = 2 if slots % 2 == 0 else 1
    tiles_shape = (slots, tile, tile)
    tiles = call(
        functools.partial(assemble, weight_parts=weight_parts, near=near),
        table,
        weight_list,
        [
            pl.BlockSpec((length, slots // steps, row_share, tile), lambda step, *_: (0, step, 0, 0))
            for _, _, length in weight_parts
        ],
        pl.BlockSpec((slots // steps, tile, tile), lambda step, *_: (step, 0, 0)),
        shape(tiles_shape, BF16),
        grid=steps,
        scratch=[pltpu.VMEM((slots // steps, tile, tile), F32)],
        cost=10_000_000,
        vmem=24,
    )
    def specs_of(*groups):
        return [whole(one.shape) for group in groups for one in group]

    middle_shapes = [
        shape((features, group_rows), BF16),
        shape((blocks, group_rows, tile), F32),
        shape((blocks, group_rows, tile), F32),
        shape((blocks, tile, group_rows), BF16),
    ]
    sum_shapes = [shape(own_shape, BF16), shape(other_shape, BF16)]
    outs = call(
        functools.partial(ahead, token_count=len(x_list), slot_count=slot_count, parts=parts),
        table,
        [*x_list, tiles],
        specs_of(x_list, [tiles]),
        specs_of(middle_shapes, sum_shapes),
        middle_shapes + sum_shapes,
        scratch=[pltpu.VMEM((group_rows, features), F32)],
        cost=30_000_000,
    )
    middle, (ffn_own, ffn_other) = outs[:4], outs[4:]

    def to_near(own_sums, other_sums):
        from_core = swap(other_sums, "tensor", 1)
        return from_core, add(own_sums[half:], from_core[half:])

    def to_far(own_sums, from_core, got):
        return add(own_sums[1], from_core[1], got[1])

    def generic(own_sums, other_sums):
        sums = {}
        for index, at in enumerate(far_order):
            items = {0: own_sums[index]}
            for other_index, (far_part, other) in enumerate(other_parts):
                if far_part == at:
                    items[other] = other_sums[other_index]
            sums[at] = scatter(items, "tensor", tensor_strides)[0]
        return scatter(sums, "dp", far_strides)[0]

    if staged:
        ffn_core, ffn_near = to_near(ffn_own, after(ffn_other, g_items[3 * near]))
        middle = after(tuple(middle), ffn_near)
    part_shapes = [shape((length,) + packed_shape, BF16) for _, _, length in weight_parts]
    outs = call(
        functools.partial(
            behind,
            token_count=len(g_list),
            weight_parts=weight_parts,
            slot_count=slot_count,
            grad_scale=grad_scale,
            near=near,
            parts=parts,
        ),
        table,
        [*g_list, tiles, *middle],
        specs_of(g_list, [tiles], middle),
        specs_of(sum_shapes, part_shapes),
        sum_shapes + part_shapes,
        scratch=[pltpu.VMEM((group_rows, features), F32), pltpu.VMEM(tiles_shape, F32)],
        cost=40_000_000,
    )
    (input_own, input_other), tile_terms = outs[:2], outs[2:]

    def halves(parts):
        return swap(parts[3], "dp", 1), swap(parts[4], "dp", 2)

    def folded(parts, got_1, got_2):
        args = [parts[1], parts[2], got_1, got_2]
        out_shapes = [shape(parts[1].shape, BF16)] * 2
        return call(
            fold, table, args, specs_of(args), specs_of(out_shapes), out_shapes, cost=40_000_000, vmem=16
        )

    def summed(parts, to_1, to_2):
        from_1, from_2 = swap(to_1, "dp", 1), swap(to_2, "dp", 2)
        return [add(parts[0][at], from_1[at], from_2[at]) for at in range(far)]

    def sent_back(sums):
        return [sums[0]] + [swap(sums[at], "dp", at * near) for at in range(1, far)]

    if staged:
        ffn_got = swap(ffn_near, "dp", near)
        tile_terms, input_other = after((tile_terms, input_other), ffn_got)
        got = halves(tile_terms)
        ffn_last = to_far(ffn_own, ffn_core, ffn_got)
        ffn_far = swap(ffn_last, "dp", 2 * near)
        input_core, input_near = to_near(input_own, input_other)
        input_got = swap(after(input_near, ffn_far), "dp", near)
        to_1, to_2 = folded(after(tile_terms, ffn_last), *got)
        input_last = to_far(input_own, input_core, input_got)
        input_far = swap(input_last, "dp", 2 * near)
        sums = after(tuple(summed(tile_terms, to_1, to_2)), input_last)
        back = list(after(tuple(sent_back(sums)), input_far))
        ffn_rows = add(ffn_own[0], ffn_core[0], ffn_got[0], ffn_far)
        input_rows = add(input_own[0], input_core[0], input_got[0], input_far)
    else:
        if split:
            sums = summed(tile_terms, *folded(tile_terms, *halves(tile_terms)))
        else:
            sums = scatter(dict(enumerate(tile_terms)), "dp", near_strides)[0]
        back = sent_back(sums)
        ffn_rows = generic(ffn_own, ffn_other)
        input_rows = generic(input_own, input_other)

    grads = call(
        functools.partial(
            unpack, blocks=blocks, slot_count=slot_count
        ),
        table,
        back,
        specs_of(back),
        whole(tile_lines.shape),
        shape(tile_lines.shape, BF16),
        scratch=[pltpu.VMEM((row_share * terms * blocks_dev, tile), F32)],
        cost=2_000_000,
        vmem=24,
    )
    tile_grad = jnp.transpose(
        grads.reshape(row_share, 3, slot_count, blocks_dev, tile), (0, 1, 3, 2, 4)
    )
    return ffn_rows, input_rows, tile_grad


def solution(mesh):
    return jax.shard_map(
        shards,
        mesh=mesh,
        in_specs=(
            P(("dp", "tensor"), None),
            P(("dp", "tensor"), None),
            P("dp", None, "tensor", None, None),
            P(None, "tensor"),
            P(None, "tensor", None),
        ),
        out_specs=(
            P(("dp", "tensor"), None),
            P(("dp", "tensor"), None),
            P("dp", None, "tensor", None, None),
        ),
        check_vma=False,
    )
```

```python
import functools
import math

import jax
import jax.numpy as jnp
from jax import lax
from jax.experimental import pallas as pl
from jax.experimental.pallas import tpu as pltpu
from jax.sharding import PartitionSpec as P

F32 = jnp.float32
BF16 = jnp.bfloat16
PLAIN = (((1,), (0,)), ((), ()))
TURNED = (((1,), (1,)), ((), ()))
MIB = 1024 * 1024
UNROLL = 7
dot = functools.partial(lax.dot_general, preferred_element_type=F32)


def swap(value, axis, stride):
    size = lax.axis_size(axis)
    return lax.ppermute(value, axis, [(at, at ^ stride) for at in range(size)])


def after(value, *others):
    return lax.optimization_barrier((value, *others))[0]


def add(first, *others):
    total = first.astype(F32)
    for other in others:
        total = total + other.astype(F32)
    return total.astype(BF16)


def strides_of(size, unit=1):
    found = []
    step = size // 2
    while step >= 1:
        found.append(step * unit)
        step //= 2
    return found


def gather(items, axis, strides):
    for stride in strides:
        items = {**items, **{at ^ stride: swap(one, axis, stride) for at, one in items.items()}}
    return items


def scatter(items, axis, strides):
    for stride in reversed(strides):
        kept = {}
        for at, one in items.items():
            if not at & stride:
                kept[at] = add(one, swap(items[at ^ stride], axis, stride))
        items = kept
    return items


def whole(shape):
    return pl.BlockSpec(shape, lambda *_: (0,) * len(shape), pipeline_mode=pl.Buffered(1))


def pack(table, tiles, *refs, blocks, slot_count):
    outs, lines = refs[:-1], refs[-1]
    spare = outs[0].shape[0] - 1
    share, terms, blocks_dev, _ = tiles.shape
    for row in range(share):
        for term in range(terms):
            at = (row * terms + term) * blocks_dev
            lines[at : at + blocks_dev, :] = tiles[row, term].astype(F32)
    for at, out in enumerate(outs):

        def one(place, _, at=at, out=out):
            column = at * blocks + place
            block = table[0, column]
            for matrix in range(3):
                first, count = table[1 + matrix, column], table[4 + matrix, column]
                for slot in range(slot_count):
                    to = jnp.where(slot < count, first + slot, spare)
                    source = (matrix * slot_count + slot) * blocks_dev + block
                    out[to] = lines[pl.ds(source, share, stride=terms * blocks_dev), :].astype(BF16)
            return _

        lax.fori_loop(0, blocks, one, 0, unroll=True)


def unpack(table, *refs, blocks, slot_count):
    out, lines, sources = refs[-2], refs[-1], refs[:-2]
    share, terms, blocks_dev, _ = out.shape
    for at, ref in enumerate(sources):

        def one(place, _, at=at, ref=ref):
            column = at * blocks + place
            block = table[0, column]
            for matrix in range(3):
                first, count = table[1 + matrix, column], table[4 + matrix, column]
                for slot in range(slot_count):
                    live = slot < count
                    value = ref[jnp.where(live, first + slot, 0)].astype(F32)
                    target = (matrix * slot_count + slot) * blocks_dev + block
                    lines[pl.ds(target, share, stride=terms * blocks_dev), :] = jnp.where(
                        live, value, 0.0
                    )
            return _

        lax.fori_loop(0, blocks, one, 0, unroll=True)
    for row in range(share):
        for term in range(terms):
            at = (row * terms + term) * blocks_dev
            out[row, term] = lines[at : at + blocks_dev, :].astype(BF16)


def offset_of(table, part, at, near, share):
    far_part = (part[1] + at) ^ table[16, 0]
    near_part = part[0] ^ table[16, 1]
    return pl.multiple_of((far_part * near + near_part) * share, share)


def assemble(table, *refs, weight_parts, near):
    weight_refs, out, tiles = refs[: len(weight_parts)], refs[-2], refs[-1]
    for ref, part in zip(weight_refs, weight_parts):
        share = ref.shape[2]
        for at in range(part[2]):
            offset = offset_of(table, part, at, near, share)
            tiles[:, pl.ds(offset, share), :] = ref[at].astype(F32)
    out[...] = tiles[...].astype(BF16)

    @pl.when(pl.program_id(0) == pl.num_programs(0) - 1)
    def _():
        out[out.shape[0] - 1] = jnp.zeros(out.shape[1:], BF16)


def places_of(table, block, slot_count, spare):
    places = []
    for matrix in range(3):
        first, count = table[1 + matrix, block], table[4 + matrix, block]
        places += [jnp.where(slot < count, first + slot, spare) for slot in range(slot_count)]
    return places


def store_parts(total, own, other, parts):
    own_rows = own.shape[1]
    for at, (is_other, place) in enumerate(parts):
        ref = other if is_other else own
        ref[place] = total[at * own_rows : (at + 1) * own_rows, :].astype(BF16)


def tokens_at(refs, columns):
    return jnp.concatenate([ref[:, columns] for ref in refs], axis=0)


def columns_of(table, block, index, tile):
    return pl.ds(pl.multiple_of(table[7 + index, block] * tile, tile), tile)


def triples(slot_count):
    return [range(at * slot_count, (at + 1) * slot_count) for at in range(3)]


def in_turn(first, rest, blocks):
    group = max(size for size in range(1, UNROLL + 1) if blocks % size == 0)

    def some(at, _):
        held = first(at * group)
        for block in range(group):
            following = first(at * group + block + 1) if block + 1 < group else None
            rest(at * group + block, *held)
            held = following
        return _

    lax.fori_loop(0, blocks // group, some, 0)


def ahead(table, *refs, token_count, slot_count, parts):
    token_refs, refs = refs[:token_count], refs[token_count:]
    tiles, x_turned, gate_slope, gate_act_out, hidden_turned, ffn_own, ffn_other, ffn_sum = refs
    tile = tiles.shape[1]
    gate, up, down = triples(slot_count)

    for at in range(x_turned.shape[0] // tile):
        here = slice(at * tile, (at + 1) * tile)
        x_turned[here, :] = tokens_at(token_refs, here).T
    ffn_sum[...] = jnp.zeros_like(ffn_sum)

    def first(block):
        places = places_of(table, block, slot_count, tiles.shape[0] - 1)
        sums = []
        for indices in (gate, up):
            columns = [columns_of(table, block, index, tile) for index in indices]
            values = jnp.concatenate([tokens_at(token_refs, column) for column in columns], axis=1)
            weights = jnp.concatenate([tiles[places[index]] for index in indices], axis=0)
            sums.append(dot(values, weights, PLAIN))
        return places, *sums

    def rest(block, places, gate_pre, up_pre):
        gate_sig = jax.nn.sigmoid(gate_pre)
        gate_act = gate_pre * gate_sig
        hidden = (gate_act * up_pre).astype(BF16)
        gate_slope[block] = up_pre * gate_sig * (1.0 + gate_pre * (1.0 - gate_sig))
        gate_act_out[block] = gate_act
        hidden_turned[block] = hidden.T
        down_tiles = jnp.concatenate([tiles[places[index]] for index in down], axis=1)
        ffn = dot(hidden, down_tiles, PLAIN)
        for at, index in enumerate(down):
            ffn_sum[:, columns_of(table, block, index, tile)] += ffn[:, at * tile : (at + 1) * tile]

    in_turn(first, rest, gate_slope.shape[0])
    store_parts(ffn_sum, ffn_own, ffn_other, parts)


def behind(table, *refs, token_count, weight_parts, slot_count, grad_scale, near, parts):
    token_refs, refs = refs[:token_count], refs[token_count:]
    tiles, x_turned, gate_slope, gate_act, hidden_turned, input_own, input_other = refs[:7]
    grad_refs, input_sum, sums = refs[7:-2], refs[-2], refs[-1]
    tile = tiles.shape[1]
    gate, up, down = triples(slot_count)
    input_sum[...] = jnp.zeros_like(input_sum)

    def first(block):
        places = places_of(table, block, slot_count, tiles.shape[0] - 1)
        columns = [columns_of(table, block, index, tile) for index in range(3 * slot_count)]
        down_tiles = jnp.concatenate([tiles[places[index]] for index in down], axis=1)
        grad_in = jnp.concatenate([tokens_at(token_refs, columns[index]) for index in down], axis=1)
        return places, columns, grad_in, dot(grad_in, down_tiles, TURNED)

    def rest(block, places, columns, grad_in, hidden_grad):
        gate_grad = (hidden_grad * gate_slope[block]).astype(BF16)
        up_grad = (hidden_grad * gate_act[block]).astype(BF16)
        down_terms = dot(hidden_turned[block], grad_in, PLAIN) * grad_scale
        for at, index in enumerate(down):
            sums[places[index]] = down_terms[:, at * tile : (at + 1) * tile]
        for indices, grad in ((gate, gate_grad), (up, up_grad)):
            weights = jnp.concatenate([tiles[places[index]] for index in indices], axis=0)
            back = dot(grad, weights, TURNED)
            turned = jnp.concatenate([x_turned[columns[index], :] for index in indices], axis=0)
            terms = dot(turned, grad, PLAIN) * grad_scale
            for at, index in enumerate(indices):
                sums[places[index]] = terms[at * tile : (at + 1) * tile]
                input_sum[:, columns[index]] += back[:, at * tile : (at + 1) * tile]

    in_turn(first, rest, gate_slope.shape[0])
    store_parts(input_sum, input_own, input_other, parts)
    for ref, part in zip(grad_refs, weight_parts):
        share = ref.shape[2]
        for at in range(part[2]):
            offset = offset_of(table, part, at, near, share)
            ref[at] = sums[:, pl.ds(offset, share), :].astype(BF16)


def fold(table, part_1, part_2, got_1, got_2, out_1, out_2):
    half = got_1.shape[0]
    out_2[:half] = add(part_2[:half], got_1[...])
    out_2[half:] = part_2[half:]
    out_1[:half] = part_1[:half]
    out_1[half:] = add(part_1[half:], got_2[...])


def call(kernel, table, args, in_specs, out_specs, out_shape, grid=1, scratch=(), cost=0, vmem=40):
    return pl.pallas_call(
        kernel,
        grid_spec=pltpu.PrefetchScalarGridSpec(
            num_scalar_prefetch=1,
            grid=(grid,),
            in_specs=in_specs,
            out_specs=out_specs,
            scratch_shapes=scratch,
        ),
        out_shape=out_shape,
        compiler_params=pltpu.CompilerParams(vmem_limit_bytes=vmem * MIB),
        cost_estimate=pl.CostEstimate(flops=0, bytes_accessed=cost, transcendentals=0),
    )(table, *args)


def shards(tokens, out_grad, weight_tiles, tile_counts, tile_rows):
    row_share, _, blocks_dev, slot_count, tile = weight_tiles.shape
    own_rows, features = tokens.shape
    dp_size, tensor_size = lax.axis_size("dp"), lax.axis_size("tensor")
    far = math.gcd(4, math.gcd(dp_size, blocks_dev))
    near = dp_size // far
    blocks = blocks_dev // far
    terms = 3 * slot_count
    grad_scale = 1.0 / math.sqrt(own_rows * tensor_size * dp_size)
    me = lax.axis_index("dp")
    far_at, near_at = me // near, me % near
    far_strides, near_strides = strides_of(far, near), strides_of(near)
    tensor_strides = strides_of(tensor_size)
    shape = jax.ShapeDtypeStruct

    x_items, g_items = {0: tokens}, {0: out_grad}
    if far > 1:
        x_items[near] = swap(tokens, "dp", near)

    capacity = (terms * blocks_dev - 3 * blocks_dev + 3 * (slot_count - 1) * (far - 1)) // far
    slots = capacity + 1
    block_ids = jnp.arange(blocks_dev, dtype=jnp.int32)
    load = tile_counts[0] + tile_counts[1] + tile_counts[2]
    earlier = (load[:, None] > load[None, :]) | (
        (load[:, None] == load[None, :]) & (block_ids[:, None] < block_ids[None, :])
    )
    rank = jnp.sum(earlier.astype(jnp.int32), axis=0)
    home = rank % far
    before = (home[:, None] == home[None, :]) & (rank[:, None] < rank[None, :])
    start = jnp.sum(jnp.where(before, load[:, None], 0), axis=0)
    ranks_of = (
        jnp.arange(blocks, dtype=jnp.int32)[None, :] * far
        + (jnp.arange(far, dtype=jnp.int32)[:, None] ^ far_at)
    ).reshape(blocks_dev)
    columns = jnp.concatenate(
        [
            block_ids[None, :],
            start[None, :],
            (start + tile_counts[0])[None, :],
            (start + tile_counts[0] + tile_counts[1])[None, :],
            tile_counts,
            jnp.transpose(tile_rows, (0, 2, 1)).reshape(terms, blocks_dev),
        ]
    )
    table = jnp.sum(
        jnp.where(ranks_of[None, :, None] == rank[None, None, :], columns[:, None, :], 0), axis=2
    )
    place = jnp.where(block_ids == 0, far_at, near_at).astype(jnp.int32)
    table = jnp.concatenate([table, place[None, :]])

    tile_lines = jnp.transpose(weight_tiles, (0, 1, 3, 2, 4)).reshape(
        row_share, terms, blocks_dev, tile
    )
    packed_shape = (slots, row_share, tile)
    packed = call(
        functools.partial(pack, blocks=blocks, slot_count=slot_count),
        table,
        [tile_lines],
        [whole(tile_lines.shape)],
        [whole(packed_shape)] * far,
        [shape(packed_shape, BF16)] * far,
        scratch=[pltpu.VMEM((row_share * terms * blocks_dev, tile), F32)],
        cost=1_000_000,
        vmem=24,
    )
    staged = tensor_size == 2 and far == 4 and near == 4
    received = [swap(packed[at], "dp", at * near) for at in reversed(range(1, far))][::-1]
    held = jnp.stack([packed[0], *received])
    x_core, g_core = {}, {}
    if staged:
        x_core = {at: swap(x_items[at], "tensor", 1) for at in (0, near)}
        g_core = {0: swap(out_grad, "tensor", 1)}
        held = after(held, *x_core.values(), *g_core.values())

    half = far // 2
    split = near == 4 and far % 2 == 0
    if split:
        from_1, from_2 = swap(held, "dp", 1), swap(held, "dp", 2)
        pass_1, pass_2 = from_1[:half], from_2[half:]
        weight_list = [held, from_1, from_2, swap(pass_1, "dp", 2), swap(pass_2, "dp", 1)]
        weight_parts = [(0, 0, far), (1, 0, far), (2, 0, far), (3, 0, half), (3, half, half)]
    else:
        items = gather({0: held}, "dp", near_strides)
        pass_1 = pass_2 = held
        weight_list = [items[at] for at in range(near)]
        weight_parts = [(at, 0, far) for at in range(near)]

    if staged:
        x_source, g_source = after((tokens, out_grad), held)
        x_items[2 * near] = swap(x_source, "dp", 2 * near)
        g_items[near] = swap(g_source, "dp", near)
        x_source, g_source = after((x_items[2 * near], out_grad), x_items[2 * near], g_items[near])
        x_items[3 * near] = swap(x_source, "dp", near)
        g_items[2 * near] = swap(g_source, "dp", 2 * near)
        g_items[3 * near] = swap(g_items[2 * near], "dp", near)
        x_late = jnp.concatenate([x_items[2 * near], x_items[3 * near]])
        x_late = swap(after(x_late, *weight_list[3:], g_items[2 * near]), "tensor", 1)
        g_late = jnp.concatenate([g_items[at * near] for at in range(1, far)])
        g_late = swap(g_late, "tensor", 1)
    else:
        for items, value in ((x_items, tokens), (g_items, out_grad)):
            items.update(gather({0: value}, "dp", far_strides))

    far_order = [at * near for at in range(0, far, 2)] + [at * near for at in range(1, far, 2)]
    if staged:
        order = [at * near for at in range(far)]
        x_list = [x_items[at] for at in order] + [x_core[at] for at in order[:2]] + [x_late]
        g_list = [g_items[at] for at in order] + [g_core[0], g_late]
        parts = [(other, far_order.index(at)) for other in (False, True) for at in order]
        other_parts = [(at, 1) for at in far_order]
    else:
        x_list, g_list, parts, other_parts = [], [], [], []
        for place, at in enumerate(far_order):
            x_parts = gather({0: x_items[at]}, "tensor", tensor_strides)
            g_parts = gather({0: g_items[at]}, "tensor", tensor_strides)
            for other in x_parts:
                parts.append((other != 0, len(other_parts) if other else place))
                if other:
                    other_parts.append((at, other))
                x_list.append(x_parts[other])
                g_list.append(g_parts[other])

    group_rows = far * tensor_size * own_rows
    own_shape = (far, own_rows, features)
    other_shape = (len(other_parts), own_rows, features)
    steps = 2 if slots % 2 == 0 else 1
    tiles_shape = (slots, tile, tile)
    tiles = call(
        functools.partial(assemble, weight_parts=weight_parts, near=near),
        table,
        weight_list,
        [
            pl.BlockSpec((length, slots // steps, row_share, tile), lambda step, *_: (0, step, 0, 0))
            for _, _, length in weight_parts
        ],
        pl.BlockSpec((slots // steps, tile, tile), lambda step, *_: (step, 0, 0)),
        shape(tiles_shape, BF16),
        grid=steps,
        scratch=[pltpu.VMEM((slots // steps, tile, tile), F32)],
        cost=10_000_000,
        vmem=24,
    )
    def specs_of(*groups):
        return [whole(one.shape) for group in groups for one in group]

    middle_shapes = [
        shape((features, group_rows), BF16),
        shape((blocks, group_rows, tile), F32),
        shape((blocks, group_rows, tile), F32),
        shape((blocks, tile, group_rows), BF16),
    ]
    sum_shapes = [shape(own_shape, BF16), shape(other_shape, BF16)]
    outs = call(
        functools.partial(ahead, token_count=len(x_list), slot_count=slot_count, parts=parts),
        table,
        [*x_list, tiles],
        specs_of(x_list, [tiles]),
        specs_of(middle_shapes, sum_shapes),
        middle_shapes + sum_shapes,
        scratch=[pltpu.VMEM((group_rows, features), F32)],
        cost=30_000_000,
    )
    middle, (ffn_own, ffn_other) = outs[:4], outs[4:]

    def to_near(own_sums, other_sums):
        from_core = swap(other_sums, "tensor", 1)
        return from_core, add(own_sums[half:], from_core[half:])

    def to_far(own_sums, from_core, got):
        return add(own_sums[1], from_core[1], got[1])

    def generic(own_sums, other_sums):
        sums = {}
        for index, at in enumerate(far_order):
            items = {0: own_sums[index]}
            for other_index, (far_part, other) in enumerate(other_parts):
                if far_part == at:
                    items[other] = other_sums[other_index]
            sums[at] = scatter(items, "tensor", tensor_strides)[0]
        return scatter(sums, "dp", far_strides)[0]

    if staged:
        ffn_core, ffn_near = to_near(ffn_own, after(ffn_other, g_items[3 * near]))
        middle = after(tuple(middle), ffn_near)
    part_shapes = [shape((length,) + packed_shape, BF16) for _, _, length in weight_parts]
    outs = call(
        functools.partial(
            behind,
            token_count=len(g_list),
            weight_parts=weight_parts,
            slot_count=slot_count,
            grad_scale=grad_scale,
            near=near,
            parts=parts,
        ),
        table,
        [*g_list, tiles, *middle],
        specs_of(g_list, [tiles], middle),
        specs_of(sum_shapes, part_shapes),
        sum_shapes + part_shapes,
        scratch=[pltpu.VMEM((group_rows, features), F32), pltpu.VMEM(tiles_shape, F32)],
        cost=40_000_000,
    )
    (input_own, input_other), tile_terms = outs[:2], outs[2:]

    def halves(parts):
        return swap(parts[3], "dp", 1), swap(parts[4], "dp", 2)

    def folded(parts, got_1, got_2):
        args = [parts[1], parts[2], got_1, got_2]
        out_shapes = [shape(parts[1].shape, BF16)] * 2
        return call(
            fold, table, args, specs_of(args), specs_of(out_shapes), out_shapes, cost=40_000_000, vmem=16
        )

    def summed(parts, to_1, to_2):
        from_1, from_2 = swap(to_1, "dp", 1), swap(to_2, "dp", 2)
        return [add(parts[0][at], from_1[at], from_2[at]) for at in range(far)]

    def sent_back(sums):
        return [sums[0]] + [swap(sums[at], "dp", at * near) for at in range(1, far)]

    if staged:
        ffn_got = swap(ffn_near, "dp", near)
        input_other = after(input_other, ffn_got)
        got = halves(tile_terms)
        ffn_last = to_far(ffn_own, ffn_core, ffn_got)
        ffn_far = swap(ffn_last, "dp", 2 * near)
        input_core, input_near = to_near(input_own, input_other)
        input_got = swap(input_near, "dp", near)
        to_1, to_2 = folded(after(tile_terms, ffn_last, input_near), *got)
        input_last = after(to_far(input_own, input_core, input_got), ffn_far)
        input_far = swap(input_last, "dp", 2 * near)
        sums = after(tuple(summed(tile_terms, to_1, to_2)), input_last)
        back = list(after(tuple(sent_back(sums)), input_far))
        ffn_rows = add(ffn_own[0], ffn_core[0], ffn_got[0], ffn_far)
        input_rows = add(input_own[0], input_core[0], input_got[0], input_far)
    else:
        if split:
            sums = summed(tile_terms, *folded(tile_terms, *halves(tile_terms)))
        else:
            sums = scatter(dict(enumerate(tile_terms)), "dp", near_strides)[0]
        back = sent_back(sums)
        ffn_rows = generic(ffn_own, ffn_other)
        input_rows = generic(input_own, input_other)

    grads = call(
        functools.partial(
            unpack, blocks=blocks, slot_count=slot_count
        ),
        table,
        back,
        specs_of(back),
        whole(tile_lines.shape),
        shape(tile_lines.shape, BF16),
        scratch=[pltpu.VMEM((row_share * terms * blocks_dev, tile), F32)],
        cost=2_000_000,
        vmem=24,
    )
    tile_grad = jnp.transpose(
        grads.reshape(row_share, 3, slot_count, blocks_dev, tile), (0, 1, 3, 2, 4)
    )
    return ffn_rows, input_rows, tile_grad


def solution(mesh):
    return jax.shard_map(
        shards,
        mesh=mesh,
        in_specs=(
            P(("dp", "tensor"), None),
            P(("dp", "tensor"), None),
            P("dp", None, "tensor", None, None),
            P(None, "tensor"),
            P(None, "tensor", None),
        ),
        out_specs=(
            P(("dp", "tensor"), None),
            P(("dp", "tensor"), None),
            P("dp", None, "tensor", None, None),
        ),
        check_vma=False,
    )
```

```python
import functools
import math

import jax
import jax.numpy as jnp
from jax import lax
from jax.experimental import pallas as pl
from jax.experimental.pallas import tpu as pltpu
from jax.sharding import PartitionSpec as P

F32 = jnp.float32
BF16 = jnp.bfloat16
PLAIN = (((1,), (0,)), ((), ()))
TURNED = (((1,), (1,)), ((), ()))
MIB = 1024 * 1024
UNROLL = 7
dot = functools.partial(lax.dot_general, preferred_element_type=F32)


def swap(value, axis, stride):
    size = lax.axis_size(axis)
    return lax.ppermute(value, axis, [(at, at ^ stride) for at in range(size)])


def after(value, *others):
    return lax.optimization_barrier((value, *others))[0]


def add(first, *others):
    total = first.astype(F32)
    for other in others:
        total = total + other.astype(F32)
    return total.astype(BF16)


def strides_of(size, unit=1):
    found = []
    step = size // 2
    while step >= 1:
        found.append(step * unit)
        step //= 2
    return found


def gather(items, axis, strides):
    for stride in strides:
        items = {**items, **{at ^ stride: swap(one, axis, stride) for at, one in items.items()}}
    return items


def scatter(items, axis, strides):
    for stride in reversed(strides):
        kept = {}
        for at, one in items.items():
            if not at & stride:
                kept[at] = add(one, swap(items[at ^ stride], axis, stride))
        items = kept
    return items


def whole(shape):
    return pl.BlockSpec(shape, lambda *_: (0,) * len(shape), pipeline_mode=pl.Buffered(1))


def pack(table, tiles, *refs, blocks, slot_count):
    outs, lines = refs[:-1], refs[-1]
    spare = outs[0].shape[0] - 1
    share, terms, blocks_dev, _ = tiles.shape
    for row in range(share):
        for term in range(terms):
            at = (row * terms + term) * blocks_dev
            lines[at : at + blocks_dev, :] = tiles[row, term].astype(F32)
    for at, out in enumerate(outs):

        def one(place, _, at=at, out=out):
            column = at * blocks + place
            block = table[0, column]
            for matrix in range(3):
                first, count = table[1 + matrix, column], table[4 + matrix, column]
                for slot in range(slot_count):
                    to = jnp.where(slot < count, first + slot, spare)
                    source = (matrix * slot_count + slot) * blocks_dev + block
                    out[to] = lines[pl.ds(source, share, stride=terms * blocks_dev), :].astype(BF16)
            return _

        lax.fori_loop(0, blocks, one, 0, unroll=True)


def unpack(table, *refs, blocks, slot_count):
    out, lines, sources = refs[-2], refs[-1], refs[:-2]
    share, terms, blocks_dev, _ = out.shape
    for at, ref in enumerate(sources):

        def one(place, _, at=at, ref=ref):
            column = at * blocks + place
            block = table[0, column]
            for matrix in range(3):
                first, count = table[1 + matrix, column], table[4 + matrix, column]
                for slot in range(slot_count):
                    live = slot < count
                    value = ref[jnp.where(live, first + slot, 0)].astype(F32)
                    target = (matrix * slot_count + slot) * blocks_dev + block
                    lines[pl.ds(target, share, stride=terms * blocks_dev), :] = jnp.where(
                        live, value, 0.0
                    )
            return _

        lax.fori_loop(0, blocks, one, 0, unroll=True)
    for row in range(share):
        for term in range(terms):
            at = (row * terms + term) * blocks_dev
            out[row, term] = lines[at : at + blocks_dev, :].astype(BF16)


def offset_of(table, part, at, near, share):
    far_part = (part[1] + at) ^ table[16, 0]
    near_part = part[0] ^ table[16, 1]
    return pl.multiple_of((far_part * near + near_part) * share, share)


def assemble(table, *refs, weight_parts, near):
    weight_refs, out, tiles = refs[: len(weight_parts)], refs[-2], refs[-1]
    for ref, part in zip(weight_refs, weight_parts):
        share = ref.shape[2]
        for at in range(part[2]):
            offset = offset_of(table, part, at, near, share)
            tiles[:, pl.ds(offset, share), :] = ref[at].astype(F32)
    out[...] = tiles[...].astype(BF16)

    @pl.when(pl.program_id(0) == pl.num_programs(0) - 1)
    def _():
        out[out.shape[0] - 1] = jnp.zeros(out.shape[1:], BF16)


def places_of(table, block, slot_count, spare):
    places = []
    for matrix in range(3):
        first, count = table[1 + matrix, block], table[4 + matrix, block]
        places += [jnp.where(slot < count, first + slot, spare) for slot in range(slot_count)]
    return places


def store_parts(total, own, other, parts):
    own_rows = own.shape[1]
    for at, (is_other, place) in enumerate(parts):
        ref = other if is_other else own
        ref[place] = total[at * own_rows : (at + 1) * own_rows, :].astype(BF16)


def tokens_at(refs, columns):
    return jnp.concatenate([ref[:, columns] for ref in refs], axis=0)


def columns_of(table, block, index, tile):
    return pl.ds(pl.multiple_of(table[7 + index, block] * tile, tile), tile)


def triples(slot_count):
    return [range(at * slot_count, (at + 1) * slot_count) for at in range(3)]


def in_turn(first, rest, blocks):
    group = max(size for size in range(1, UNROLL + 1) if blocks % size == 0)

    def some(at, _):
        held = first(at * group)
        for block in range(group):
            following = first(at * group + block + 1) if block + 1 < group else None
            rest(at * group + block, *held)
            held = following
        return _

    lax.fori_loop(0, blocks // group, some, 0)


def ahead(table, *refs, token_count, slot_count, parts):
    token_refs, refs = refs[:token_count], refs[token_count:]
    tiles, x_turned, gate_slope, gate_act_out, hidden_turned, ffn_own, ffn_other, ffn_sum = refs
    tile = tiles.shape[1]
    gate, up, down = triples(slot_count)

    for at in range(x_turned.shape[0] // tile):
        here = slice(at * tile, (at + 1) * tile)
        x_turned[here, :] = tokens_at(token_refs, here).T
    ffn_sum[...] = jnp.zeros_like(ffn_sum)

    def first(block):
        places = places_of(table, block, slot_count, tiles.shape[0] - 1)
        sums = []
        for indices in (gate, up):
            columns = [columns_of(table, block, index, tile) for index in indices]
            values = jnp.concatenate([tokens_at(token_refs, column) for column in columns], axis=1)
            weights = jnp.concatenate([tiles[places[index]] for index in indices], axis=0)
            sums.append(dot(values, weights, PLAIN))
        return places, *sums

    def rest(block, places, gate_pre, up_pre):
        gate_sig = jax.nn.sigmoid(gate_pre)
        gate_act = gate_pre * gate_sig
        hidden = (gate_act * up_pre).astype(BF16)
        gate_slope[block] = up_pre * gate_sig * (1.0 + gate_pre * (1.0 - gate_sig))
        gate_act_out[block] = gate_act
        hidden_turned[block] = hidden.T
        down_tiles = jnp.concatenate([tiles[places[index]] for index in down], axis=1)
        ffn = dot(hidden, down_tiles, PLAIN)
        for at, index in enumerate(down):
            ffn_sum[:, columns_of(table, block, index, tile)] += ffn[:, at * tile : (at + 1) * tile]

    in_turn(first, rest, gate_slope.shape[0])
    store_parts(ffn_sum, ffn_own, ffn_other, parts)


def behind(table, *refs, token_count, weight_parts, slot_count, grad_scale, near, parts):
    token_refs, refs = refs[:token_count], refs[token_count:]
    tiles, x_turned, gate_slope, gate_act, hidden_turned, input_own, input_other = refs[:7]
    grad_refs, input_sum, sums = refs[7:-2], refs[-2], refs[-1]
    tile = tiles.shape[1]
    gate, up, down = triples(slot_count)
    input_sum[...] = jnp.zeros_like(input_sum)

    def first(block):
        places = places_of(table, block, slot_count, tiles.shape[0] - 1)
        columns = [columns_of(table, block, index, tile) for index in range(3 * slot_count)]
        down_tiles = jnp.concatenate([tiles[places[index]] for index in down], axis=1)
        grad_in = jnp.concatenate([tokens_at(token_refs, columns[index]) for index in down], axis=1)
        return places, columns, grad_in, dot(grad_in, down_tiles, TURNED)

    def rest(block, places, columns, grad_in, hidden_grad):
        gate_grad = (hidden_grad * gate_slope[block]).astype(BF16)
        up_grad = (hidden_grad * gate_act[block]).astype(BF16)
        down_terms = dot(hidden_turned[block], grad_in, PLAIN) * grad_scale
        for at, index in enumerate(down):
            sums[places[index]] = down_terms[:, at * tile : (at + 1) * tile]
        for indices, grad in ((gate, gate_grad), (up, up_grad)):
            weights = jnp.concatenate([tiles[places[index]] for index in indices], axis=0)
            back = dot(grad, weights, TURNED)
            turned = jnp.concatenate([x_turned[columns[index], :] for index in indices], axis=0)
            terms = dot(turned, grad, PLAIN) * grad_scale
            for at, index in enumerate(indices):
                sums[places[index]] = terms[at * tile : (at + 1) * tile]
                input_sum[:, columns[index]] += back[:, at * tile : (at + 1) * tile]

    in_turn(first, rest, gate_slope.shape[0])
    store_parts(input_sum, input_own, input_other, parts)
    for ref, part in zip(grad_refs, weight_parts):
        share = ref.shape[2]
        for at in range(part[2]):
            offset = offset_of(table, part, at, near, share)
            ref[at] = sums[:, pl.ds(offset, share), :].astype(BF16)


def fold(table, part_1, part_2, got_1, got_2, out_1, out_2):
    half = got_1.shape[0]
    out_2[:half] = add(part_2[:half], got_1[...])
    out_2[half:] = part_2[half:]
    out_1[:half] = part_1[:half]
    out_1[half:] = add(part_1[half:], got_2[...])


def call(kernel, table, args, in_specs, out_specs, out_shape, grid=1, scratch=(), cost=0, vmem=40):
    return pl.pallas_call(
        kernel,
        grid_spec=pltpu.PrefetchScalarGridSpec(
            num_scalar_prefetch=1,
            grid=(grid,),
            in_specs=in_specs,
            out_specs=out_specs,
            scratch_shapes=scratch,
        ),
        out_shape=out_shape,
        compiler_params=pltpu.CompilerParams(vmem_limit_bytes=vmem * MIB),
        cost_estimate=pl.CostEstimate(flops=0, bytes_accessed=cost, transcendentals=0),
    )(table, *args)


def shards(tokens, out_grad, weight_tiles, tile_counts, tile_rows):
    row_share, _, blocks_dev, slot_count, tile = weight_tiles.shape
    own_rows, features = tokens.shape
    dp_size, tensor_size = lax.axis_size("dp"), lax.axis_size("tensor")
    far = math.gcd(4, math.gcd(dp_size, blocks_dev))
    near = dp_size // far
    blocks = blocks_dev // far
    terms = 3 * slot_count
    grad_scale = 1.0 / math.sqrt(own_rows * tensor_size * dp_size)
    me = lax.axis_index("dp")
    far_at, near_at = me // near, me % near
    far_strides, near_strides = strides_of(far, near), strides_of(near)
    tensor_strides = strides_of(tensor_size)
    shape = jax.ShapeDtypeStruct

    staged = tensor_size == 2 and far == 4 and near == 4
    x_items, g_items = {0: tokens}, {0: out_grad}
    if staged:
        x_items[2 * near] = swap(tokens, "dp", 2 * near)
        x_items[near] = swap(tokens, "dp", near)
        g_items[near] = swap(out_grad, "dp", near)

    capacity = (terms * blocks_dev - 3 * blocks_dev + 3 * (slot_count - 1) * (far - 1)) // far
    slots = capacity + 1
    block_ids = jnp.arange(blocks_dev, dtype=jnp.int32)
    load = tile_counts[0] + tile_counts[1] + tile_counts[2]
    earlier = (load[:, None] > load[None, :]) | (
        (load[:, None] == load[None, :]) & (block_ids[:, None] < block_ids[None, :])
    )
    rank = jnp.sum(earlier.astype(jnp.int32), axis=0)
    home = rank % far
    before = (home[:, None] == home[None, :]) & (rank[:, None] < rank[None, :])
    start = jnp.sum(jnp.where(before, load[:, None], 0), axis=0)
    ranks_of = (
        jnp.arange(blocks, dtype=jnp.int32)[None, :] * far
        + (jnp.arange(far, dtype=jnp.int32)[:, None] ^ far_at)
    ).reshape(blocks_dev)
    columns = jnp.concatenate(
        [
            block_ids[None, :],
            start[None, :],
            (start + tile_counts[0])[None, :],
            (start + tile_counts[0] + tile_counts[1])[None, :],
            tile_counts,
            jnp.transpose(tile_rows, (0, 2, 1)).reshape(terms, blocks_dev),
        ]
    )
    table = jnp.sum(
        jnp.where(ranks_of[None, :, None] == rank[None, None, :], columns[:, None, :], 0), axis=2
    )
    place = jnp.where(block_ids == 0, far_at, near_at).astype(jnp.int32)
    table = jnp.concatenate([table, place[None, :]])

    tile_lines = jnp.transpose(weight_tiles, (0, 1, 3, 2, 4)).reshape(
        row_share, terms, blocks_dev, tile
    )
    packed_shape = (slots, row_share, tile)
    packed = call(
        functools.partial(pack, blocks=blocks, slot_count=slot_count),
        table,
        [tile_lines],
        [whole(tile_lines.shape)],
        [whole(packed_shape)] * far,
        [shape(packed_shape, BF16)] * far,
        scratch=[pltpu.VMEM((row_share * terms * blocks_dev, tile), F32)],
        cost=30_000_000,
        vmem=24,
    )
    if staged:
        packed = after(tuple(packed), x_items[2 * near])
    received = {at: swap(packed[at], "dp", at * near) for at in range(1, far)}
    half = far // 2
    split = near == 4 and far % 2 == 0
    if staged:
        held_a = jnp.stack([packed[0], received[1]])
        a_1, a_2 = swap(held_a, "dp", 1), swap(held_a, "dp", 2)
        held_b = jnp.stack([received[2], received[3]])
        held_b, x_source, g_source = after(
            (held_b, x_items[2 * near], out_grad), a_1, a_2, x_items[near], g_items[near]
        )
        b_1, b_2 = swap(held_b, "dp", 1), swap(held_b, "dp", 2)
        g_items[2 * near] = swap(g_source, "dp", 2 * near)
        x_items[3 * near] = swap(x_source, "dp", near)
        a_far, b_far = after((a_1, b_2), b_1, g_items[2 * near], x_items[3 * near])
        a_3, b_3 = swap(a_far, "dp", 2), swap(b_far, "dp", 1)
        x_own = jnp.concatenate(after([x_items[at * near] for at in range(far)], b_1, b_2, g_items[2 * near]))
        x_core = swap(x_own, "tensor", 1)
        g_items[3 * near] = swap(g_items[2 * near], "dp", near)
        g_own = jnp.concatenate([g_items[at * near] for at in range(far)])
        g_core = swap(g_own, "tensor", 1)
        weight_list = [held_a, a_1, a_2, a_3, held_b, b_1, b_2, after(b_3, g_items[3 * near])]
        held_parts = [(at, first, half) for first in (0, half) for at in range(near)]
    else:
        held = jnp.stack([packed[0], *received.values()])
        items = gather({0: held}, "dp", near_strides)
        weight_list = [items[at] for at in range(near)]
        held_parts = [(at, 0, far) for at in range(near)]
        for items, value in ((x_items, tokens), (g_items, out_grad)):
            items.update(gather({0: value}, "dp", far_strides))
    weight_parts = [(at, 0, far) for at in range(near)]
    if split:
        weight_parts[3:] = [(3, 0, half), (3, half, half)]

    far_order = [at * near for at in range(0, far, 2)] + [at * near for at in range(1, far, 2)]
    if staged:
        order = [at * near for at in range(far)]
        x_list, g_list = [x_own, x_core], [g_own, g_core]
        parts = [(other, far_order.index(at)) for other in (False, True) for at in order]
        other_parts = [(at, 1) for at in far_order]
    else:
        x_list, g_list, parts, other_parts = [], [], [], []
        for place, at in enumerate(far_order):
            x_parts = gather({0: x_items[at]}, "tensor", tensor_strides)
            g_parts = gather({0: g_items[at]}, "tensor", tensor_strides)
            for other in x_parts:
                parts.append((other != 0, len(other_parts) if other else place))
                if other:
                    other_parts.append((at, other))
                x_list.append(x_parts[other])
                g_list.append(g_parts[other])

    group_rows = far * tensor_size * own_rows
    own_shape = (far, own_rows, features)
    other_shape = (len(other_parts), own_rows, features)
    steps = 2 if slots % 2 == 0 else 1
    tiles_shape = (slots, tile, tile)
    tiles = call(
        functools.partial(assemble, weight_parts=held_parts, near=near),
        table,
        weight_list,
        [
            pl.BlockSpec((length, slots // steps, row_share, tile), lambda step, *_: (0, step, 0, 0))
            for _, _, length in held_parts
        ],
        pl.BlockSpec((slots // steps, tile, tile), lambda step, *_: (step, 0, 0)),
        shape(tiles_shape, BF16),
        grid=steps,
        scratch=[pltpu.VMEM((slots // steps, tile, tile), F32)],
        cost=10_000_000,
        vmem=24,
    )
    def specs_of(*groups):
        return [whole(one.shape) for group in groups for one in group]

    middle_shapes = [
        shape((features, group_rows), BF16),
        shape((blocks, group_rows, tile), F32),
        shape((blocks, group_rows, tile), F32),
        shape((blocks, tile, group_rows), BF16),
    ]
    sum_shapes = [shape(own_shape, BF16), shape(other_shape, BF16)]
    outs = call(
        functools.partial(ahead, token_count=len(x_list), slot_count=slot_count, parts=parts),
        table,
        [*x_list, tiles],
        specs_of(x_list, [tiles]),
        specs_of(middle_shapes, sum_shapes),
        middle_shapes + sum_shapes,
        scratch=[pltpu.VMEM((group_rows, features), F32)],
        cost=30_000_000,
    )
    middle, (ffn_own, ffn_other) = outs[:4], outs[4:]

    def to_near(own_sums, other_sums):
        from_core = swap(other_sums, "tensor", 1)
        return from_core, add(own_sums[half:], from_core[half:])

    def to_far(own_sums, from_core, got):
        return add(own_sums[1], from_core[1], got[1])

    def generic(own_sums, other_sums):
        sums = {}
        for index, at in enumerate(far_order):
            items = {0: own_sums[index]}
            for other_index, (far_part, other) in enumerate(other_parts):
                if far_part == at:
                    items[other] = other_sums[other_index]
            sums[at] = scatter(items, "tensor", tensor_strides)[0]
        return scatter(sums, "dp", far_strides)[0]

    if staged:
        ffn_core, ffn_near = to_near(ffn_own, after(ffn_other, g_items[3 * near]))
        middle = after(tuple(middle), ffn_near)
    part_shapes = [shape((length,) + packed_shape, BF16) for _, _, length in weight_parts]
    outs = call(
        functools.partial(
            behind,
            token_count=len(g_list),
            weight_parts=weight_parts,
            slot_count=slot_count,
            grad_scale=grad_scale,
            near=near,
            parts=parts,
        ),
        table,
        [*g_list, tiles, *middle],
        specs_of(g_list, [tiles], middle),
        specs_of(sum_shapes, part_shapes),
        sum_shapes + part_shapes,
        scratch=[pltpu.VMEM((group_rows, features), F32), pltpu.VMEM(tiles_shape, F32)],
        cost=40_000_000,
    )
    (input_own, input_other), tile_terms = outs[:2], outs[2:]

    def halves(parts):
        return swap(parts[3], "dp", 1), swap(parts[4], "dp", 2)

    def folded(parts, got_1, got_2):
        args = [parts[1], parts[2], got_1, got_2]
        out_shapes = [shape(parts[1].shape, BF16)] * 2
        return call(
            fold, table, args, specs_of(args), specs_of(out_shapes), out_shapes, cost=40_000_000, vmem=16
        )

    def summed(parts, to_1, to_2):
        from_1, from_2 = swap(to_1, "dp", 1), swap(to_2, "dp", 2)
        return [add(parts[0][at], from_1[at], from_2[at]) for at in range(far)]

    def sent_back(sums):
        return [sums[0]] + [swap(sums[at], "dp", at * near) for at in range(1, far)]

    if staged:
        ffn_got = swap(ffn_near, "dp", near)
        input_other = after(input_other, ffn_got)
        got = halves(tile_terms)
        ffn_last = to_far(ffn_own, ffn_core, ffn_got)
        ffn_far = swap(ffn_last, "dp", 2 * near)
        input_core, input_near = to_near(input_own, input_other)
        input_got = swap(input_near, "dp", near)
        to_1, to_2 = folded(after(tile_terms, ffn_last, input_near), *got)
        input_last = after(to_far(input_own, input_core, input_got), ffn_far)
        input_far = swap(input_last, "dp", 2 * near)
        sums = after(tuple(summed(tile_terms, to_1, to_2)), input_last)
        back = list(after(tuple(sent_back(sums)), input_far))
        ffn_rows = add(ffn_own[0], ffn_core[0], ffn_got[0], ffn_far)
        input_rows = add(input_own[0], input_core[0], input_got[0], input_far)
    else:
        if split:
            sums = summed(tile_terms, *folded(tile_terms, *halves(tile_terms)))
        else:
            sums = scatter(dict(enumerate(tile_terms)), "dp", near_strides)[0]
        back = sent_back(sums)
        ffn_rows = generic(ffn_own, ffn_other)
        input_rows = generic(input_own, input_other)

    grads = call(
        functools.partial(
            unpack, blocks=blocks, slot_count=slot_count
        ),
        table,
        back,
        specs_of(back),
        whole(tile_lines.shape),
        shape(tile_lines.shape, BF16),
        scratch=[pltpu.VMEM((row_share * terms * blocks_dev, tile), F32)],
        cost=2_000_000,
        vmem=24,
    )
    tile_grad = jnp.transpose(
        grads.reshape(row_share, 3, slot_count, blocks_dev, tile), (0, 1, 3, 2, 4)
    )
    return ffn_rows, input_rows, tile_grad


def solution(mesh):
    return jax.shard_map(
        shards,
        mesh=mesh,
        in_specs=(
            P(("dp", "tensor"), None),
            P(("dp", "tensor"), None),
            P("dp", None, "tensor", None, None),
            P(None, "tensor"),
            P(None, "tensor", None),
        ),
        out_specs=(
            P(("dp", "tensor"), None),
            P(("dp", "tensor"), None),
            P("dp", None, "tensor", None, None),
        ),
        check_vma=False,
    )
```

```python
import functools
import math

import jax
import jax.numpy as jnp
from jax import lax
from jax.experimental import pallas as pl
from jax.experimental.pallas import tpu as pltpu
from jax.sharding import PartitionSpec as P

F32 = jnp.float32
BF16 = jnp.bfloat16
PLAIN = (((1,), (0,)), ((), ()))
TURNED = (((1,), (1,)), ((), ()))
MIB = 1024 * 1024
UNROLL = 7
dot = functools.partial(lax.dot_general, preferred_element_type=F32)


def swap(value, axis, stride):
    size = lax.axis_size(axis)
    return lax.ppermute(value, axis, [(at, at ^ stride) for at in range(size)])


def after(value, *others):
    return lax.optimization_barrier((value, *others))[0]


def add(first, *others):
    total = first.astype(F32)
    for other in others:
        total = total + other.astype(F32)
    return total.astype(BF16)


def strides_of(size, unit=1):
    found = []
    step = size // 2
    while step >= 1:
        found.append(step * unit)
        step //= 2
    return found


def gather(items, axis, strides):
    for stride in strides:
        items = {**items, **{at ^ stride: swap(one, axis, stride) for at, one in items.items()}}
    return items


def scatter(items, axis, strides):
    for stride in reversed(strides):
        kept = {}
        for at, one in items.items():
            if not at & stride:
                kept[at] = add(one, swap(items[at ^ stride], axis, stride))
        items = kept
    return items


def whole(shape):
    return pl.BlockSpec(shape, lambda *_: (0,) * len(shape), pipeline_mode=pl.Buffered(1))


def pack(table, tiles, *refs, blocks, slot_count):
    outs, lines = refs[:-1], refs[-1]
    spare = outs[0].shape[0] - 1
    share, terms, blocks_dev, _ = tiles.shape
    for row in range(share):
        for term in range(terms):
            at = (row * terms + term) * blocks_dev
            lines[at : at + blocks_dev, :] = tiles[row, term].astype(F32)
    for at, out in enumerate(outs):

        def one(place, _, at=at, out=out):
            column = at * blocks + place
            block = table[0, column]
            for matrix in range(3):
                first, count = table[1 + matrix, column], table[4 + matrix, column]
                for slot in range(slot_count):
                    to = jnp.where(slot < count, first + slot, spare)
                    source = (matrix * slot_count + slot) * blocks_dev + block
                    out[to] = lines[pl.ds(source, share, stride=terms * blocks_dev), :].astype(BF16)
            return _

        lax.fori_loop(0, blocks, one, 0, unroll=True)


def unpack(table, *refs, blocks, slot_count):
    out, lines, sources = refs[-2], refs[-1], refs[:-2]
    share, terms, blocks_dev, _ = out.shape
    for at, ref in enumerate(sources):

        def one(place, _, at=at, ref=ref):
            column = at * blocks + place
            block = table[0, column]
            for matrix in range(3):
                first, count = table[1 + matrix, column], table[4 + matrix, column]
                for slot in range(slot_count):
                    live = slot < count
                    value = ref[jnp.where(live, first + slot, 0)].astype(F32)
                    target = (matrix * slot_count + slot) * blocks_dev + block
                    lines[pl.ds(target, share, stride=terms * blocks_dev), :] = jnp.where(
                        live, value, 0.0
                    )
            return _

        lax.fori_loop(0, blocks, one, 0, unroll=True)
    for row in range(share):
        for term in range(terms):
            at = (row * terms + term) * blocks_dev
            out[row, term] = lines[at : at + blocks_dev, :].astype(BF16)


def offset_of(table, part, at, near, share):
    far_part = (part[1] + at) ^ table[16, 0]
    near_part = part[0] ^ table[16, 1]
    return pl.multiple_of((far_part * near + near_part) * share, share)


def assemble(table, *refs, weight_parts, near):
    weight_refs, out, tiles = refs[: len(weight_parts)], refs[-2], refs[-1]
    for ref, part in zip(weight_refs, weight_parts):
        share = ref.shape[2]
        for at in range(part[2]):
            offset = offset_of(table, part, at, near, share)
            tiles[:, pl.ds(offset, share), :] = ref[at].astype(F32)
    out[...] = tiles[...].astype(BF16)

    @pl.when(pl.program_id(0) == pl.num_programs(0) - 1)
    def _():
        out[out.shape[0] - 1] = jnp.zeros(out.shape[1:], BF16)


def places_of(table, block, slot_count, spare):
    places = []
    for matrix in range(3):
        first, count = table[1 + matrix, block], table[4 + matrix, block]
        places += [jnp.where(slot < count, first + slot, spare) for slot in range(slot_count)]
    return places


def store_parts(total, own, other, parts):
    own_rows = own.shape[1]
    for at, (is_other, place) in enumerate(parts):
        ref = other if is_other else own
        ref[place] = total[at * own_rows : (at + 1) * own_rows, :].astype(BF16)


def tokens_at(refs, columns):
    return jnp.concatenate([ref[:, columns] for ref in refs], axis=0)


def columns_of(table, block, index, tile):
    return pl.ds(pl.multiple_of(table[7 + index, block] * tile, tile), tile)


def triples(slot_count):
    return [range(at * slot_count, (at + 1) * slot_count) for at in range(3)]


def in_turn(first, rest, blocks):
    group = max(size for size in range(1, UNROLL + 1) if blocks % size == 0)

    def some(at, _):
        held = first(at * group)
        for block in range(group):
            following = first(at * group + block + 1) if block + 1 < group else None
            rest(at * group + block, *held)
            held = following
        return _

    lax.fori_loop(0, blocks // group, some, 0)


def ahead(table, *refs, token_count, slot_count, parts):
    token_refs, refs = refs[:token_count], refs[token_count:]
    tiles, x_turned, gate_slope, gate_act_out, hidden_turned, ffn_own, ffn_other, ffn_sum = refs
    tile = tiles.shape[1]
    gate, up, down = triples(slot_count)

    for at in range(x_turned.shape[0] // tile):
        here = slice(at * tile, (at + 1) * tile)
        x_turned[here, :] = tokens_at(token_refs, here).T
    ffn_sum[...] = jnp.zeros_like(ffn_sum)

    def first(block):
        places = places_of(table, block, slot_count, tiles.shape[0] - 1)
        sums = []
        for indices in (gate, up):
            columns = [columns_of(table, block, index, tile) for index in indices]
            values = jnp.concatenate([tokens_at(token_refs, column) for column in columns], axis=1)
            weights = jnp.concatenate([tiles[places[index]] for index in indices], axis=0)
            sums.append(dot(values, weights, PLAIN))
        return places, *sums

    def rest(block, places, gate_pre, up_pre):
        gate_sig = jax.nn.sigmoid(gate_pre)
        gate_act = gate_pre * gate_sig
        hidden = (gate_act * up_pre).astype(BF16)
        gate_slope[block] = up_pre * gate_sig * (1.0 + gate_pre * (1.0 - gate_sig))
        gate_act_out[block] = gate_act
        hidden_turned[block] = hidden.T
        down_tiles = jnp.concatenate([tiles[places[index]] for index in down], axis=1)
        ffn = dot(hidden, down_tiles, PLAIN)
        for at, index in enumerate(down):
            ffn_sum[:, columns_of(table, block, index, tile)] += ffn[:, at * tile : (at + 1) * tile]

    in_turn(first, rest, gate_slope.shape[0])
    store_parts(ffn_sum, ffn_own, ffn_other, parts)


def behind(table, *refs, token_count, weight_parts, slot_count, grad_scale, near, parts):
    token_refs, refs = refs[:token_count], refs[token_count:]
    tiles, x_turned, gate_slope, gate_act, hidden_turned, input_own, input_other = refs[:7]
    grad_refs, input_sum, sums = refs[7:-2], refs[-2], refs[-1]
    tile = tiles.shape[1]
    gate, up, down = triples(slot_count)
    input_sum[...] = jnp.zeros_like(input_sum)

    def first(block):
        places = places_of(table, block, slot_count, tiles.shape[0] - 1)
        columns = [columns_of(table, block, index, tile) for index in range(3 * slot_count)]
        down_tiles = jnp.concatenate([tiles[places[index]] for index in down], axis=1)
        grad_in = jnp.concatenate([tokens_at(token_refs, columns[index]) for index in down], axis=1)
        return places, columns, grad_in, dot(grad_in, down_tiles, TURNED)

    def rest(block, places, columns, grad_in, hidden_grad):
        gate_grad = (hidden_grad * gate_slope[block]).astype(BF16)
        up_grad = (hidden_grad * gate_act[block]).astype(BF16)
        down_terms = dot(hidden_turned[block], grad_in, PLAIN) * grad_scale
        for at, index in enumerate(down):
            sums[places[index]] = down_terms[:, at * tile : (at + 1) * tile]
        for indices, grad in ((gate, gate_grad), (up, up_grad)):
            weights = jnp.concatenate([tiles[places[index]] for index in indices], axis=0)
            back = dot(grad, weights, TURNED)
            turned = jnp.concatenate([x_turned[columns[index], :] for index in indices], axis=0)
            terms = dot(turned, grad, PLAIN) * grad_scale
            for at, index in enumerate(indices):
                sums[places[index]] = terms[at * tile : (at + 1) * tile]
                input_sum[:, columns[index]] += back[:, at * tile : (at + 1) * tile]

    in_turn(first, rest, gate_slope.shape[0])
    store_parts(input_sum, input_own, input_other, parts)
    for ref, part in zip(grad_refs, weight_parts):
        share = ref.shape[2]
        for at in range(part[2]):
            offset = offset_of(table, part, at, near, share)
            ref[at] = sums[:, pl.ds(offset, share), :].astype(BF16)


def fold(table, part_1, part_2, got_1, got_2, out_1, out_2):
    half = got_1.shape[0]
    out_2[:half] = add(part_2[:half], got_1[...])
    out_2[half:] = part_2[half:]
    out_1[:half] = part_1[:half]
    out_1[half:] = add(part_1[half:], got_2[...])


def call(kernel, table, args, in_specs, out_specs, out_shape, grid=1, scratch=(), cost=0, vmem=40):
    return pl.pallas_call(
        kernel,
        grid_spec=pltpu.PrefetchScalarGridSpec(
            num_scalar_prefetch=1,
            grid=(grid,),
            in_specs=in_specs,
            out_specs=out_specs,
            scratch_shapes=scratch,
        ),
        out_shape=out_shape,
        compiler_params=pltpu.CompilerParams(vmem_limit_bytes=vmem * MIB),
        cost_estimate=pl.CostEstimate(flops=0, bytes_accessed=cost, transcendentals=0),
    )(table, *args)


def shards(tokens, out_grad, weight_tiles, tile_counts, tile_rows):
    row_share, _, blocks_dev, slot_count, tile = weight_tiles.shape
    own_rows, features = tokens.shape
    dp_size, tensor_size = lax.axis_size("dp"), lax.axis_size("tensor")
    far = math.gcd(4, math.gcd(dp_size, blocks_dev))
    near = dp_size // far
    blocks = blocks_dev // far
    terms = 3 * slot_count
    grad_scale = 1.0 / math.sqrt(own_rows * tensor_size * dp_size)
    me = lax.axis_index("dp")
    far_at, near_at = me // near, me % near
    far_strides, near_strides = strides_of(far, near), strides_of(near)
    tensor_strides = strides_of(tensor_size)
    shape = jax.ShapeDtypeStruct

    x_items, g_items = {0: tokens}, {0: out_grad}
    capacity = (terms * blocks_dev - 3 * blocks_dev + 3 * (slot_count - 1) * (far - 1)) // far
    slots = capacity + 1
    block_ids = jnp.arange(blocks_dev, dtype=jnp.int32)
    load = tile_counts[0] + tile_counts[1] + tile_counts[2]
    earlier = (load[:, None] > load[None, :]) | (
        (load[:, None] == load[None, :]) & (block_ids[:, None] < block_ids[None, :])
    )
    rank = jnp.sum(earlier.astype(jnp.int32), axis=0)
    home = rank % far
    before = (home[:, None] == home[None, :]) & (rank[:, None] < rank[None, :])
    start = jnp.sum(jnp.where(before, load[:, None], 0), axis=0)
    ranks_of = (
        jnp.arange(blocks, dtype=jnp.int32)[None, :] * far
        + (jnp.arange(far, dtype=jnp.int32)[:, None] ^ far_at)
    ).reshape(blocks_dev)
    columns = jnp.concatenate(
        [
            block_ids[None, :],
            start[None, :],
            (start + tile_counts[0])[None, :],
            (start + tile_counts[0] + tile_counts[1])[None, :],
            tile_counts,
            jnp.transpose(tile_rows, (0, 2, 1)).reshape(terms, blocks_dev),
        ]
    )
    table = jnp.sum(
        jnp.where(ranks_of[None, :, None] == rank[None, None, :], columns[:, None, :], 0), axis=2
    )
    place = jnp.where(block_ids == 0, far_at, near_at).astype(jnp.int32)
    table = jnp.concatenate([table, place[None, :]])

    tile_lines = jnp.transpose(weight_tiles, (0, 1, 3, 2, 4)).reshape(
        row_share, terms, blocks_dev, tile
    )
    packed_shape = (slots, row_share, tile)
    packed = call(
        functools.partial(pack, blocks=blocks, slot_count=slot_count),
        table,
        [tile_lines],
        [whole(tile_lines.shape)],
        [whole(packed_shape)] * far,
        [shape(packed_shape, BF16)] * far,
        scratch=[pltpu.VMEM((row_share * terms * blocks_dev, tile), F32)],
        cost=1_000_000,
        vmem=24,
    )
    staged = tensor_size == 2 and far == 4 and near == 4
    if far > 1:
        x_items[near] = swap(after(tokens, *packed), "dp", near)
    received = [swap(packed[at], "dp", at * near) for at in reversed(range(1, far))][::-1]
    held = jnp.stack([packed[0], *received])
    x_core, g_core = {}, {}
    if staged:
        x_core = {at: swap(x_items[at], "tensor", 1) for at in (0, near)}
        g_core = {0: swap(out_grad, "tensor", 1)}
        held = after(held, *x_core.values(), *g_core.values())

    half = far // 2
    split = near == 4 and far % 2 == 0
    if split:
        from_1, from_2 = swap(held, "dp", 1), swap(held, "dp", 2)
        pass_1, pass_2 = from_1[:half], from_2[half:]
        weight_list = [held, from_1, from_2, swap(pass_1, "dp", 2), swap(pass_2, "dp", 1)]
        weight_parts = [(0, 0, far), (1, 0, far), (2, 0, far), (3, 0, half), (3, half, half)]
    else:
        items = gather({0: held}, "dp", near_strides)
        pass_1 = pass_2 = held
        weight_list = [items[at] for at in range(near)]
        weight_parts = [(at, 0, far) for at in range(near)]

    if staged:
        x_source, g_source = after((tokens, out_grad), held)
        x_items[2 * near] = swap(x_source, "dp", 2 * near)
        g_items[near] = swap(g_source, "dp", near)
        x_source, g_source = after((x_items[2 * near], out_grad), x_items[2 * near], g_items[near])
        g_source = after(g_source, pass_1, pass_2)
        x_items[3 * near] = swap(x_source, "dp", near)
        g_items[2 * near] = swap(g_source, "dp", 2 * near)
        g_items[3 * near] = swap(g_items[2 * near], "dp", near)
        x_late = jnp.concatenate([x_items[2 * near], x_items[3 * near]])
        x_late = swap(after(x_late, *weight_list[3:], g_items[2 * near]), "tensor", 1)
        g_late = jnp.concatenate([g_items[at * near] for at in range(1, far)])
        g_late = swap(g_late, "tensor", 1)
    else:
        for items, value in ((x_items, tokens), (g_items, out_grad)):
            items.update(gather({0: value}, "dp", far_strides))

    far_order = [at * near for at in range(0, far, 2)] + [at * near for at in range(1, far, 2)]
    if staged:
        order = [at * near for at in range(far)]
        x_list = [x_items[at] for at in order] + [x_core[at] for at in order[:2]] + [x_late]
        g_list = [g_items[at] for at in order] + [g_core[0], g_late]
        parts = [(other, far_order.index(at)) for other in (False, True) for at in order]
        other_parts = [(at, 1) for at in far_order]
    else:
        x_list, g_list, parts, other_parts = [], [], [], []
        for place, at in enumerate(far_order):
            x_parts = gather({0: x_items[at]}, "tensor", tensor_strides)
            g_parts = gather({0: g_items[at]}, "tensor", tensor_strides)
            for other in x_parts:
                parts.append((other != 0, len(other_parts) if other else place))
                if other:
                    other_parts.append((at, other))
                x_list.append(x_parts[other])
                g_list.append(g_parts[other])

    group_rows = far * tensor_size * own_rows
    own_shape = (far, own_rows, features)
    other_shape = (len(other_parts), own_rows, features)
    steps = 2 if slots % 2 == 0 else 1
    tiles_shape = (slots, tile, tile)
    tiles = call(
        functools.partial(assemble, weight_parts=weight_parts, near=near),
        table,
        weight_list,
        [
            pl.BlockSpec((length, slots // steps, row_share, tile), lambda step, *_: (0, step, 0, 0))
            for _, _, length in weight_parts
        ],
        pl.BlockSpec((slots // steps, tile, tile), lambda step, *_: (step, 0, 0)),
        shape(tiles_shape, BF16),
        grid=steps,
        scratch=[pltpu.VMEM((slots // steps, tile, tile), F32)],
        cost=10_000_000,
        vmem=24,
    )
    def specs_of(*groups):
        return [whole(one.shape) for group in groups for one in group]

    middle_shapes = [
        shape((features, group_rows), BF16),
        shape((blocks, group_rows, tile), F32),
        shape((blocks, group_rows, tile), F32),
        shape((blocks, tile, group_rows), BF16),
    ]
    sum_shapes = [shape(own_shape, BF16), shape(other_shape, BF16)]
    outs = call(
        functools.partial(ahead, token_count=len(x_list), slot_count=slot_count, parts=parts),
        table,
        [*x_list, tiles],
        specs_of(x_list, [tiles]),
        specs_of(middle_shapes, sum_shapes),
        middle_shapes + sum_shapes,
        scratch=[pltpu.VMEM((group_rows, features), F32)],
        cost=30_000_000,
    )
    middle, (ffn_own, ffn_other) = outs[:4], outs[4:]

    def to_near(own_sums, other_sums):
        from_core = swap(other_sums, "tensor", 1)
        return from_core, add(own_sums[half:], from_core[half:])

    def to_far(own_sums, from_core, got):
        return add(own_sums[1], from_core[1], got[1])

    def generic(own_sums, other_sums):
        sums = {}
        for index, at in enumerate(far_order):
            items = {0: own_sums[index]}
            for other_index, (far_part, other) in enumerate(other_parts):
                if far_part == at:
                    items[other] = other_sums[other_index]
            sums[at] = scatter(items, "tensor", tensor_strides)[0]
        return scatter(sums, "dp", far_strides)[0]

    if staged:
        ffn_core, ffn_near = to_near(ffn_own, after(ffn_other, g_items[3 * near]))
        middle = after(tuple(middle), ffn_near)
    part_shapes = [shape((length,) + packed_shape, BF16) for _, _, length in weight_parts]
    outs = call(
        functools.partial(
            behind,
            token_count=len(g_list),
            weight_parts=weight_parts,
            slot_count=slot_count,
            grad_scale=grad_scale,
            near=near,
            parts=parts,
        ),
        table,
        [*g_list, tiles, *middle],
        specs_of(g_list, [tiles], middle),
        specs_of(sum_shapes, part_shapes),
        sum_shapes + part_shapes,
        scratch=[pltpu.VMEM((group_rows, features), F32), pltpu.VMEM(tiles_shape, F32)],
        cost=40_000_000,
    )
    (input_own, input_other), tile_terms = outs[:2], outs[2:]

    def halves(parts):
        return swap(parts[3], "dp", 1), swap(parts[4], "dp", 2)

    def folded(parts, got_1, got_2):
        args = [parts[1], parts[2], got_1, got_2]
        out_shapes = [shape(parts[1].shape, BF16)] * 2
        return call(
            fold, table, args, specs_of(args), specs_of(out_shapes), out_shapes, cost=40_000_000, vmem=16
        )

    def summed(parts, to_1, to_2):
        from_1, from_2 = swap(to_1, "dp", 1), swap(to_2, "dp", 2)
        return [add(parts[0][at], from_1[at], from_2[at]) for at in range(far)]

    def sent_back(sums):
        return [sums[0]] + [swap(sums[at], "dp", at * near) for at in range(1, far)]

    if staged:
        ffn_got = swap(ffn_near, "dp", near)
        input_other = after(input_other, ffn_got)
        got = halves(tile_terms)
        ffn_last = to_far(ffn_own, ffn_core, ffn_got)
        ffn_far = swap(ffn_last, "dp", 2 * near)
        input_core, input_near = to_near(input_own, input_other)
        input_got = swap(input_near, "dp", near)
        to_1, to_2 = folded(after(tile_terms, ffn_last, input_near), *got)
        input_last = after(to_far(input_own, input_core, input_got), ffn_far)
        input_far = swap(input_last, "dp", 2 * near)
        sums = after(tuple(summed(tile_terms, to_1, to_2)), input_last)
        back = list(after(tuple(sent_back(sums)), input_far))
        ffn_rows = add(ffn_own[0], ffn_core[0], ffn_got[0], ffn_far)
        input_rows = add(input_own[0], input_core[0], input_got[0], input_far)
    else:
        if split:
            sums = summed(tile_terms, *folded(tile_terms, *halves(tile_terms)))
        else:
            sums = scatter(dict(enumerate(tile_terms)), "dp", near_strides)[0]
        back = sent_back(sums)
        ffn_rows = generic(ffn_own, ffn_other)
        input_rows = generic(input_own, input_other)

    grads = call(
        functools.partial(
            unpack, blocks=blocks, slot_count=slot_count
        ),
        table,
        back,
        specs_of(back),
        whole(tile_lines.shape),
        shape(tile_lines.shape, BF16),
        scratch=[pltpu.VMEM((row_share * terms * blocks_dev, tile), F32)],
        cost=2_000_000,
        vmem=24,
    )
    tile_grad = jnp.transpose(
        grads.reshape(row_share, 3, slot_count, blocks_dev, tile), (0, 1, 3, 2, 4)
    )
    return ffn_rows, input_rows, tile_grad


def solution(mesh):
    return jax.shard_map(
        shards,
        mesh=mesh,
        in_specs=(
            P(("dp", "tensor"), None),
            P(("dp", "tensor"), None),
            P("dp", None, "tensor", None, None),
            P(None, "tensor"),
            P(None, "tensor", None),
        ),
        out_specs=(
            P(("dp", "tensor"), None),
            P(("dp", "tensor"), None),
            P("dp", None, "tensor", None, None),
        ),
        check_vma=False,
    )
```

```python
import functools
import math

import jax
import jax.numpy as jnp
from jax import lax
from jax.experimental import pallas as pl
from jax.experimental.pallas import tpu as pltpu
from jax.sharding import PartitionSpec as P

F32 = jnp.float32
BF16 = jnp.bfloat16
PLAIN = (((1,), (0,)), ((), ()))
TURNED = (((1,), (1,)), ((), ()))
MIB = 1024 * 1024
UNROLL = 7
dot = functools.partial(lax.dot_general, preferred_element_type=F32)


def swap(value, axis, stride):
    size = lax.axis_size(axis)
    return lax.ppermute(value, axis, [(at, at ^ stride) for at in range(size)])


def after(value, *others):
    return lax.optimization_barrier((value, *others))[0]


def add(first, *others):
    total = first.astype(F32)
    for other in others:
        total = total + other.astype(F32)
    return total.astype(BF16)


def strides_of(size, unit=1):
    found = []
    step = size // 2
    while step >= 1:
        found.append(step * unit)
        step //= 2
    return found


def gather(items, axis, strides):
    for stride in strides:
        items = {**items, **{at ^ stride: swap(one, axis, stride) for at, one in items.items()}}
    return items


def scatter(items, axis, strides):
    for stride in reversed(strides):
        kept = {}
        for at, one in items.items():
            if not at & stride:
                kept[at] = add(one, swap(items[at ^ stride], axis, stride))
        items = kept
    return items


def whole(shape):
    return pl.BlockSpec(shape, lambda *_: (0,) * len(shape), pipeline_mode=pl.Buffered(1))


def pack(table, tiles, *refs, blocks, slot_count):
    outs, lines = refs[:-1], refs[-1]
    spare = outs[0].shape[0] - 1
    share, terms, blocks_dev, _ = tiles.shape
    for row in range(share):
        for term in range(terms):
            at = (row * terms + term) * blocks_dev
            lines[at : at + blocks_dev, :] = tiles[row, term].astype(F32)
    for at, out in enumerate(outs):

        def one(place, _, at=at, out=out):
            column = at * blocks + place
            block = table[0, column]
            for matrix in range(3):
                first, count = table[1 + matrix, column], table[4 + matrix, column]
                for slot in range(slot_count):
                    to = jnp.where(slot < count, first + slot, spare)
                    source = (matrix * slot_count + slot) * blocks_dev + block
                    out[to] = lines[pl.ds(source, share, stride=terms * blocks_dev), :].astype(BF16)
            return _

        lax.fori_loop(0, blocks, one, 0, unroll=True)


def unpack(table, *refs, blocks, slot_count):
    out, lines, sources = refs[-2], refs[-1], refs[:-2]
    share, terms, blocks_dev, _ = out.shape
    for at, ref in enumerate(sources):

        def one(place, _, at=at, ref=ref):
            column = at * blocks + place
            block = table[0, column]
            for matrix in range(3):
                first, count = table[1 + matrix, column], table[4 + matrix, column]
                for slot in range(slot_count):
                    live = slot < count
                    value = ref[jnp.where(live, first + slot, 0)].astype(F32)
                    target = (matrix * slot_count + slot) * blocks_dev + block
                    lines[pl.ds(target, share, stride=terms * blocks_dev), :] = jnp.where(
                        live, value, 0.0
                    )
            return _

        lax.fori_loop(0, blocks, one, 0, unroll=True)
    for row in range(share):
        for term in range(terms):
            at = (row * terms + term) * blocks_dev
            out[row, term] = lines[at : at + blocks_dev, :].astype(BF16)


def offset_of(table, part, at, near, share):
    far_part = (part[1] + at) ^ table[16, 0]
    near_part = part[0] ^ table[16, 1]
    return pl.multiple_of((far_part * near + near_part) * share, share)


def assemble(table, *refs, weight_parts, near):
    weight_refs, out, tiles = refs[: len(weight_parts)], refs[-2], refs[-1]
    for ref, part in zip(weight_refs, weight_parts):
        share = ref.shape[2]
        for at in range(part[2]):
            offset = offset_of(table, part, at, near, share)
            tiles[:, pl.ds(offset, share), :] = ref[at].astype(F32)
    out[...] = tiles[...].astype(BF16)

    @pl.when(pl.program_id(0) == pl.num_programs(0) - 1)
    def _():
        out[out.shape[0] - 1] = jnp.zeros(out.shape[1:], BF16)


def places_of(table, block, slot_count, spare):
    places = []
    for matrix in range(3):
        first, count = table[1 + matrix, block], table[4 + matrix, block]
        places += [jnp.where(slot < count, first + slot, spare) for slot in range(slot_count)]
    return places


def store_parts(total, own, other, parts):
    own_rows = own.shape[1]
    for at, (is_other, place) in enumerate(parts):
        ref = other if is_other else own
        ref[place] = total[at * own_rows : (at + 1) * own_rows, :].astype(BF16)


def tokens_at(refs, columns):
    return jnp.concatenate([ref[:, columns] for ref in refs], axis=0)


def columns_of(table, block, index, tile):
    return pl.ds(pl.multiple_of(table[7 + index, block] * tile, tile), tile)


def triples(slot_count):
    return [range(at * slot_count, (at + 1) * slot_count) for at in range(3)]


def in_turn(first, rest, blocks):
    group = max(size for size in range(1, UNROLL + 1) if blocks % size == 0)

    def some(at, _):
        held = first(at * group)
        for block in range(group):
            following = first(at * group + block + 1) if block + 1 < group else None
            rest(at * group + block, *held)
            held = following
        return _

    lax.fori_loop(0, blocks // group, some, 0)


def ahead(table, *refs, token_count, slot_count, parts):
    token_refs, refs = refs[:token_count], refs[token_count:]
    tiles, x_turned, gate_slope, gate_act_out, hidden_turned, ffn_own, ffn_other, ffn_sum = refs
    tile = tiles.shape[1]
    gate, up, down = triples(slot_count)

    for at in range(x_turned.shape[0] // tile):
        here = slice(at * tile, (at + 1) * tile)
        x_turned[here, :] = tokens_at(token_refs, here).T
    ffn_sum[...] = jnp.zeros_like(ffn_sum)

    def first(block):
        places = places_of(table, block, slot_count, tiles.shape[0] - 1)
        sums = []
        for indices in (gate, up):
            columns = [columns_of(table, block, index, tile) for index in indices]
            values = jnp.concatenate([tokens_at(token_refs, column) for column in columns], axis=1)
            weights = jnp.concatenate([tiles[places[index]] for index in indices], axis=0)
            sums.append(dot(values, weights, PLAIN))
        return places, *sums

    def rest(block, places, gate_pre, up_pre):
        gate_sig = jax.nn.sigmoid(gate_pre)
        gate_act = gate_pre * gate_sig
        hidden = (gate_act * up_pre).astype(BF16)
        gate_slope[block] = up_pre * gate_sig * (1.0 + gate_pre * (1.0 - gate_sig))
        gate_act_out[block] = gate_act
        hidden_turned[block] = hidden.T
        down_tiles = jnp.concatenate([tiles[places[index]] for index in down], axis=1)
        ffn = dot(hidden, down_tiles, PLAIN)
        for at, index in enumerate(down):
            ffn_sum[:, columns_of(table, block, index, tile)] += ffn[:, at * tile : (at + 1) * tile]

    in_turn(first, rest, gate_slope.shape[0])
    store_parts(ffn_sum, ffn_own, ffn_other, parts)


def behind(table, *refs, token_count, weight_parts, slot_count, grad_scale, near, parts):
    token_refs, refs = refs[:token_count], refs[token_count:]
    tiles, x_turned, gate_slope, gate_act, hidden_turned, input_own, input_other = refs[:7]
    grad_refs, input_sum, sums = refs[7:-2], refs[-2], refs[-1]
    tile = tiles.shape[1]
    gate, up, down = triples(slot_count)
    input_sum[...] = jnp.zeros_like(input_sum)

    def first(block):
        places = places_of(table, block, slot_count, tiles.shape[0] - 1)
        columns = [columns_of(table, block, index, tile) for index in range(3 * slot_count)]
        down_tiles = jnp.concatenate([tiles[places[index]] for index in down], axis=1)
        grad_in = jnp.concatenate([tokens_at(token_refs, columns[index]) for index in down], axis=1)
        return places, columns, grad_in, dot(grad_in, down_tiles, TURNED)

    def rest(block, places, columns, grad_in, hidden_grad):
        gate_grad = (hidden_grad * gate_slope[block]).astype(BF16)
        up_grad = (hidden_grad * gate_act[block]).astype(BF16)
        down_terms = dot(hidden_turned[block], grad_in, PLAIN) * grad_scale
        for at, index in enumerate(down):
            sums[places[index]] = down_terms[:, at * tile : (at + 1) * tile]
        for indices, grad in ((gate, gate_grad), (up, up_grad)):
            weights = jnp.concatenate([tiles[places[index]] for index in indices], axis=0)
            back = dot(grad, weights, TURNED)
            turned = jnp.concatenate([x_turned[columns[index], :] for index in indices], axis=0)
            terms = dot(turned, grad, PLAIN) * grad_scale
            for at, index in enumerate(indices):
                sums[places[index]] = terms[at * tile : (at + 1) * tile]
                input_sum[:, columns[index]] += back[:, at * tile : (at + 1) * tile]

    in_turn(first, rest, gate_slope.shape[0])
    store_parts(input_sum, input_own, input_other, parts)
    for ref, part in zip(grad_refs, weight_parts):
        share = ref.shape[2]
        for at in range(part[2]):
            offset = offset_of(table, part, at, near, share)
            ref[at] = sums[:, pl.ds(offset, share), :].astype(BF16)


def fold(table, part_1, part_2, got_1, got_2, out_1, out_2):
    half = got_1.shape[0]
    out_2[:half] = add(part_2[:half], got_1[...])
    out_2[half:] = part_2[half:]
    out_1[:half] = part_1[:half]
    out_1[half:] = add(part_1[half:], got_2[...])


def call(kernel, table, args, in_specs, out_specs, out_shape, grid=1, scratch=(), cost=0, vmem=40):
    return pl.pallas_call(
        kernel,
        grid_spec=pltpu.PrefetchScalarGridSpec(
            num_scalar_prefetch=1,
            grid=(grid,),
            in_specs=in_specs,
            out_specs=out_specs,
            scratch_shapes=scratch,
        ),
        out_shape=out_shape,
        compiler_params=pltpu.CompilerParams(vmem_limit_bytes=vmem * MIB),
        cost_estimate=pl.CostEstimate(flops=0, bytes_accessed=cost, transcendentals=0),
    )(table, *args)


def shards(tokens, out_grad, weight_tiles, tile_counts, tile_rows):
    row_share, _, blocks_dev, slot_count, tile = weight_tiles.shape
    own_rows, features = tokens.shape
    dp_size, tensor_size = lax.axis_size("dp"), lax.axis_size("tensor")
    far = math.gcd(4, math.gcd(dp_size, blocks_dev))
    near = dp_size // far
    blocks = blocks_dev // far
    terms = 3 * slot_count
    grad_scale = 1.0 / math.sqrt(own_rows * tensor_size * dp_size)
    me = lax.axis_index("dp")
    far_at, near_at = me // near, me % near
    far_strides, near_strides = strides_of(far, near), strides_of(near)
    tensor_strides = strides_of(tensor_size)
    shape = jax.ShapeDtypeStruct

    x_items, g_items = {0: tokens}, {0: out_grad}
    capacity = (terms * blocks_dev - 3 * blocks_dev + 3 * (slot_count - 1) * (far - 1)) // far
    slots = capacity + 1
    block_ids = jnp.arange(blocks_dev, dtype=jnp.int32)
    load = tile_counts[0] + tile_counts[1] + tile_counts[2]
    earlier = (load[:, None] > load[None, :]) | (
        (load[:, None] == load[None, :]) & (block_ids[:, None] < block_ids[None, :])
    )
    rank = jnp.sum(earlier.astype(jnp.int32), axis=0)
    home = rank % far
    before = (home[:, None] == home[None, :]) & (rank[:, None] < rank[None, :])
    start = jnp.sum(jnp.where(before, load[:, None], 0), axis=0)
    ranks_of = (
        jnp.arange(blocks, dtype=jnp.int32)[None, :] * far
        + (jnp.arange(far, dtype=jnp.int32)[:, None] ^ far_at)
    ).reshape(blocks_dev)
    columns = jnp.concatenate(
        [
            block_ids[None, :],
            start[None, :],
            (start + tile_counts[0])[None, :],
            (start + tile_counts[0] + tile_counts[1])[None, :],
            tile_counts,
            jnp.transpose(tile_rows, (0, 2, 1)).reshape(terms, blocks_dev),
        ]
    )
    table = jnp.sum(
        jnp.where(ranks_of[None, :, None] == rank[None, None, :], columns[:, None, :], 0), axis=2
    )
    place = jnp.where(block_ids == 0, far_at, near_at).astype(jnp.int32)
    table = jnp.concatenate([table, place[None, :]])

    tile_lines = jnp.transpose(weight_tiles, (0, 1, 3, 2, 4)).reshape(
        row_share, terms, blocks_dev, tile
    )
    packed_shape = (slots, row_share, tile)
    packed = call(
        functools.partial(pack, blocks=blocks, slot_count=slot_count),
        table,
        [tile_lines],
        [whole(tile_lines.shape)],
        [whole(packed_shape)] * far,
        [shape(packed_shape, BF16)] * far,
        scratch=[pltpu.VMEM((row_share * terms * blocks_dev, tile), F32)],
        cost=1_000_000,
        vmem=24,
    )
    staged = tensor_size == 2 and far == 4 and near == 4
    received = [swap(packed[at], "dp", at * near) for at in reversed(range(1, far))][::-1]
    held = jnp.stack([packed[0], *received])
    if staged:
        x_items[near] = swap(after(tokens, received[0]), "dp", near)
        x_core, g_core = swap(tokens, "tensor", 1), swap(out_grad, "tensor", 1)
        held = after(held, x_core, g_core, x_items[near])

    half = far // 2
    split = near == 4 and far % 2 == 0
    if split:
        from_1, from_2 = swap(held, "dp", 1), swap(held, "dp", 2)
        pass_1, pass_2 = from_1[:half], from_2[half:]
        weight_list = [held, from_1, from_2, swap(pass_1, "dp", 2), swap(pass_2, "dp", 1)]
        weight_parts = [(0, 0, far), (1, 0, far), (2, 0, far), (3, 0, half), (3, half, half)]
    else:
        items = gather({0: held}, "dp", near_strides)
        pass_1 = pass_2 = held
        weight_list = [items[at] for at in range(near)]
        weight_parts = [(at, 0, far) for at in range(near)]

    if staged:
        x_source, g_source = after((tokens, out_grad), held)
        x_items[2 * near] = swap(x_source, "dp", 2 * near)
        g_items[near] = swap(g_source, "dp", near)
        x_source, g_source = after(
            (x_items[2 * near], out_grad), x_items[2 * near], x_items[near], g_items[near]
        )
        x_items[3 * near] = swap(x_source, "dp", near)
        g_items[2 * near] = swap(g_source, "dp", 2 * near)
        g_items[3 * near] = swap(g_items[2 * near], "dp", near)
        x_late = jnp.concatenate([x_items[at * near] for at in range(1, far)])
        x_late = swap(after(x_late, *weight_list[3:], g_items[2 * near]), "tensor", 1)
        g_late = jnp.concatenate([g_items[at * near] for at in range(1, far)])
        g_late = swap(g_late, "tensor", 1)
    else:
        for items, value in ((x_items, tokens), (g_items, out_grad)):
            items.update(gather({0: value}, "dp", far_strides))

    far_order = [at * near for at in range(0, far, 2)] + [at * near for at in range(1, far, 2)]
    if staged:
        order = [at * near for at in range(far)]
        x_list = [x_items[at] for at in order] + [x_core, x_late]
        g_list = [g_items[at] for at in order] + [g_core, g_late]
        parts = [(other, far_order.index(at)) for other in (False, True) for at in order]
        other_parts = [(at, 1) for at in far_order]
    else:
        x_list, g_list, parts, other_parts = [], [], [], []
        for place, at in enumerate(far_order):
            x_parts = gather({0: x_items[at]}, "tensor", tensor_strides)
            g_parts = gather({0: g_items[at]}, "tensor", tensor_strides)
            for other in x_parts:
                parts.append((other != 0, len(other_parts) if other else place))
                if other:
                    other_parts.append((at, other))
                x_list.append(x_parts[other])
                g_list.append(g_parts[other])

    group_rows = far * tensor_size * own_rows
    own_shape = (far, own_rows, features)
    other_shape = (len(other_parts), own_rows, features)
    steps = 2 if slots % 2 == 0 else 1
    tiles_shape = (slots, tile, tile)
    tiles = call(
        functools.partial(assemble, weight_parts=weight_parts, near=near),
        table,
        weight_list,
        [
            pl.BlockSpec((length, slots // steps, row_share, tile), lambda step, *_: (0, step, 0, 0))
            for _, _, length in weight_parts
        ],
        pl.BlockSpec((slots // steps, tile, tile), lambda step, *_: (step, 0, 0)),
        shape(tiles_shape, BF16),
        grid=steps,
        scratch=[pltpu.VMEM((slots // steps, tile, tile), F32)],
        cost=10_000_000,
        vmem=24,
    )
    def specs_of(*groups):
        return [whole(one.shape) for group in groups for one in group]

    middle_shapes = [
        shape((features, group_rows), BF16),
        shape((blocks, group_rows, tile), F32),
        shape((blocks, group_rows, tile), F32),
        shape((blocks, tile, group_rows), BF16),
    ]
    sum_shapes = [shape(own_shape, BF16), shape(other_shape, BF16)]
    outs = call(
        functools.partial(ahead, token_count=len(x_list), slot_count=slot_count, parts=parts),
        table,
        [*x_list, tiles],
        specs_of(x_list, [tiles]),
        specs_of(middle_shapes, sum_shapes),
        middle_shapes + sum_shapes,
        scratch=[pltpu.VMEM((group_rows, features), F32)],
        cost=30_000_000,
    )
    middle, (ffn_own, ffn_other) = outs[:4], outs[4:]

    def to_near(own_sums, other_sums):
        from_core = swap(other_sums, "tensor", 1)
        return from_core, add(own_sums[half:], from_core[half:])

    def to_far(own_sums, from_core, got):
        return add(own_sums[1], from_core[1], got[1])

    def generic(own_sums, other_sums):
        sums = {}
        for index, at in enumerate(far_order):
            items = {0: own_sums[index]}
            for other_index, (far_part, other) in enumerate(other_parts):
                if far_part == at:
                    items[other] = other_sums[other_index]
            sums[at] = scatter(items, "tensor", tensor_strides)[0]
        return scatter(sums, "dp", far_strides)[0]

    if staged:
        ffn_core, ffn_near = to_near(ffn_own, after(ffn_other, g_items[3 * near]))
        middle = after(tuple(middle), ffn_near)
    part_shapes = [shape((length,) + packed_shape, BF16) for _, _, length in weight_parts]
    outs = call(
        functools.partial(
            behind,
            token_count=len(g_list),
            weight_parts=weight_parts,
            slot_count=slot_count,
            grad_scale=grad_scale,
            near=near,
            parts=parts,
        ),
        table,
        [*g_list, tiles, *middle],
        specs_of(g_list, [tiles], middle),
        specs_of(sum_shapes, part_shapes),
        sum_shapes + part_shapes,
        scratch=[pltpu.VMEM((group_rows, features), F32), pltpu.VMEM(tiles_shape, F32)],
        cost=40_000_000,
    )
    (input_own, input_other), tile_terms = outs[:2], outs[2:]

    def halves(parts):
        return swap(parts[3], "dp", 1), swap(parts[4], "dp", 2)

    def folded(parts, got_1, got_2):
        args = [parts[1], parts[2], got_1, got_2]
        out_shapes = [shape(parts[1].shape, BF16)] * 2
        return call(
            fold, table, args, specs_of(args), specs_of(out_shapes), out_shapes, cost=40_000_000, vmem=16
        )

    def summed(parts, to_1, to_2):
        from_1, from_2 = swap(to_1, "dp", 1), swap(to_2, "dp", 2)
        return [add(parts[0][at], from_1[at], from_2[at]) for at in range(far)]

    def sent_back(sums):
        return [sums[0]] + [swap(sums[at], "dp", at * near) for at in range(1, far)]

    if staged:
        ffn_got = swap(ffn_near, "dp", near)
        input_other = after(input_other, ffn_got)
        got = halves(tile_terms)
        ffn_last = to_far(ffn_own, ffn_core, ffn_got)
        ffn_far = swap(ffn_last, "dp", 2 * near)
        input_core, input_near = to_near(input_own, input_other)
        input_got = swap(input_near, "dp", near)
        to_1, to_2 = folded(after(tile_terms, ffn_last, input_near), *got)
        input_last = after(to_far(input_own, input_core, input_got), ffn_far)
        input_far = swap(input_last, "dp", 2 * near)
        sums = after(tuple(summed(tile_terms, to_1, to_2)), input_last)
        back = list(after(tuple(sent_back(sums)), input_far))
        ffn_rows = add(ffn_own[0], ffn_core[0], ffn_got[0], ffn_far)
        input_rows = add(input_own[0], input_core[0], input_got[0], input_far)
    else:
        if split:
            sums = summed(tile_terms, *folded(tile_terms, *halves(tile_terms)))
        else:
            sums = scatter(dict(enumerate(tile_terms)), "dp", near_strides)[0]
        back = sent_back(sums)
        ffn_rows = generic(ffn_own, ffn_other)
        input_rows = generic(input_own, input_other)

    grads = call(
        functools.partial(
            unpack, blocks=blocks, slot_count=slot_count
        ),
        table,
        back,
        specs_of(back),
        whole(tile_lines.shape),
        shape(tile_lines.shape, BF16),
        scratch=[pltpu.VMEM((row_share * terms * blocks_dev, tile), F32)],
        cost=2_000_000,
        vmem=24,
    )
    tile_grad = jnp.transpose(
        grads.reshape(row_share, 3, slot_count, blocks_dev, tile), (0, 1, 3, 2, 4)
    )
    return ffn_rows, input_rows, tile_grad


def solution(mesh):
    return jax.shard_map(
        shards,
        mesh=mesh,
        in_specs=(
            P(("dp", "tensor"), None),
            P(("dp", "tensor"), None),
            P("dp", None, "tensor", None, None),
            P(None, "tensor"),
            P(None, "tensor", None),
        ),
        out_specs=(
            P(("dp", "tensor"), None),
            P(("dp", "tensor"), None),
            P("dp", None, "tensor", None, None),
        ),
        check_vma=False,
    )
```

```python
import functools
import math

import jax
import jax.numpy as jnp
from jax import lax
from jax.experimental import pallas as pl
from jax.experimental.pallas import tpu as pltpu
from jax.sharding import PartitionSpec as P

F32 = jnp.float32
BF16 = jnp.bfloat16
PLAIN = (((1,), (0,)), ((), ()))
TURNED = (((1,), (1,)), ((), ()))
MIB = 1024 * 1024
UNROLL = 14
dot = functools.partial(lax.dot_general, preferred_element_type=F32)


def swap(value, axis, stride):
    size = lax.axis_size(axis)
    return lax.ppermute(value, axis, [(at, at ^ stride) for at in range(size)])


def after(value, *others):
    return lax.optimization_barrier((value, *others))[0]


def add(first, *others):
    total = first.astype(F32)
    for other in others:
        total = total + other.astype(F32)
    return total.astype(BF16)


def strides_of(size, unit=1):
    found = []
    step = size // 2
    while step >= 1:
        found.append(step * unit)
        step //= 2
    return found


def gather(items, axis, strides):
    for stride in strides:
        items = {**items, **{at ^ stride: swap(one, axis, stride) for at, one in items.items()}}
    return items


def scatter(items, axis, strides):
    for stride in reversed(strides):
        kept = {}
        for at, one in items.items():
            if not at & stride:
                kept[at] = add(one, swap(items[at ^ stride], axis, stride))
        items = kept
    return items


def whole(shape):
    return pl.BlockSpec(shape, lambda *_: (0,) * len(shape), pipeline_mode=pl.Buffered(1))


def pack(table, tiles, *refs, blocks, slot_count):
    outs, lines = refs[:-1], refs[-1]
    spare = outs[0].shape[0] - 1
    share, terms, blocks_dev, _ = tiles.shape
    for row in range(share):
        for term in range(terms):
            at = (row * terms + term) * blocks_dev
            lines[at : at + blocks_dev, :] = tiles[row, term].astype(F32)
    for at, out in enumerate(outs):

        def one(place, _, at=at, out=out):
            column = at * blocks + place
            block = table[0, column]
            for matrix in range(3):
                first, count = table[1 + matrix, column], table[4 + matrix, column]
                for slot in range(slot_count):
                    to = jnp.where(slot < count, first + slot, spare)
                    source = (matrix * slot_count + slot) * blocks_dev + block
                    out[to] = lines[pl.ds(source, share, stride=terms * blocks_dev), :].astype(BF16)
            return _

        lax.fori_loop(0, blocks, one, 0, unroll=True)


def unpack(table, *refs, blocks, slot_count):
    out, lines, sources = refs[-2], refs[-1], refs[:-2]
    share, terms, blocks_dev, _ = out.shape
    for at, ref in enumerate(sources):

        def one(place, _, at=at, ref=ref):
            column = at * blocks + place
            block = table[0, column]
            for matrix in range(3):
                first, count = table[1 + matrix, column], table[4 + matrix, column]
                for slot in range(slot_count):
                    live = slot < count
                    value = ref[jnp.where(live, first + slot, 0)].astype(F32)
                    target = (matrix * slot_count + slot) * blocks_dev + block
                    lines[pl.ds(target, share, stride=terms * blocks_dev), :] = jnp.where(
                        live, value, 0.0
                    )
            return _

        lax.fori_loop(0, blocks, one, 0, unroll=True)
    for row in range(share):
        for term in range(terms):
            at = (row * terms + term) * blocks_dev
            out[row, term] = lines[at : at + blocks_dev, :].astype(BF16)


def offset_of(table, part, at, near, share):
    far_part = (part[1] + at) ^ table[16, 0]
    near_part = part[0] ^ table[16, 1]
    return pl.multiple_of((far_part * near + near_part) * share, share)


def assemble(table, *refs, weight_parts, near):
    weight_refs, out, tiles = refs[: len(weight_parts)], refs[-2], refs[-1]
    for ref, part in zip(weight_refs, weight_parts):
        share = ref.shape[2]
        for at in range(part[2]):
            offset = offset_of(table, part, at, near, share)
            tiles[:, pl.ds(offset, share), :] = ref[at].astype(F32)
    out[...] = tiles[...].astype(BF16)

    @pl.when(pl.program_id(0) == pl.num_programs(0) - 1)
    def _():
        out[out.shape[0] - 1] = jnp.zeros(out.shape[1:], BF16)


def places_of(table, block, slot_count, spare):
    places = []
    for matrix in range(3):
        first, count = table[1 + matrix, block], table[4 + matrix, block]
        places += [jnp.where(slot < count, first + slot, spare) for slot in range(slot_count)]
    return places


def store_parts(total, own, other, parts):
    own_rows = own.shape[1]
    for at, (is_other, place) in enumerate(parts):
        ref = other if is_other else own
        ref[place] = total[at * own_rows : (at + 1) * own_rows, :].astype(BF16)


def tokens_at(refs, columns):
    return jnp.concatenate([ref[:, columns] for ref in refs], axis=0)


def columns_of(table, block, index, tile):
    return pl.ds(pl.multiple_of(table[7 + index, block] * tile, tile), tile)


def triples(slot_count):
    return [range(at * slot_count, (at + 1) * slot_count) for at in range(3)]


def in_turn(first, rest, blocks):
    group = max(size for size in range(1, UNROLL + 1) if blocks % size == 0)

    def some(at, _):
        held = first(at * group)
        for block in range(group):
            following = first(at * group + block + 1) if block + 1 < group else None
            rest(at * group + block, *held)
            held = following
        return _

    lax.fori_loop(0, blocks // group, some, 0)


def ahead(table, *refs, token_count, slot_count, parts):
    token_refs, refs = refs[:token_count], refs[token_count:]
    tiles, x_turned, gate_slope, gate_act_out, hidden_turned, ffn_own, ffn_other, ffn_sum = refs
    tile = tiles.shape[1]
    gate, up, down = triples(slot_count)

    for at in range(x_turned.shape[0] // tile):
        here = slice(at * tile, (at + 1) * tile)
        x_turned[here, :] = tokens_at(token_refs, here).T
    ffn_sum[...] = jnp.zeros_like(ffn_sum)

    def first(block):
        places = places_of(table, block, slot_count, tiles.shape[0] - 1)
        sums = []
        for indices in (gate, up):
            columns = [columns_of(table, block, index, tile) for index in indices]
            values = jnp.concatenate([tokens_at(token_refs, column) for column in columns], axis=1)
            weights = jnp.concatenate([tiles[places[index]] for index in indices], axis=0)
            sums.append(dot(values, weights, PLAIN))
        return places, *sums

    def rest(block, places, gate_pre, up_pre):
        gate_sig = jax.nn.sigmoid(gate_pre)
        gate_act = gate_pre * gate_sig
        hidden = (gate_act * up_pre).astype(BF16)
        gate_slope[block] = up_pre * gate_sig * (1.0 + gate_pre * (1.0 - gate_sig))
        gate_act_out[block] = gate_act
        hidden_turned[block] = hidden.T
        down_tiles = jnp.concatenate([tiles[places[index]] for index in down], axis=1)
        ffn = dot(hidden, down_tiles, PLAIN)
        for at, index in enumerate(down):
            ffn_sum[:, columns_of(table, block, index, tile)] += ffn[:, at * tile : (at + 1) * tile]

    in_turn(first, rest, gate_slope.shape[0])
    store_parts(ffn_sum, ffn_own, ffn_other, parts)


def behind(table, *refs, token_count, weight_parts, slot_count, grad_scale, near, parts):
    token_refs, refs = refs[:token_count], refs[token_count:]
    tiles, x_turned, gate_slope, gate_act, hidden_turned, input_own, input_other = refs[:7]
    grad_refs, input_sum, sums = refs[7:-2], refs[-2], refs[-1]
    tile = tiles.shape[1]
    gate, up, down = triples(slot_count)
    input_sum[...] = jnp.zeros_like(input_sum)

    def first(block):
        places = places_of(table, block, slot_count, tiles.shape[0] - 1)
        columns = [columns_of(table, block, index, tile) for index in range(3 * slot_count)]
        down_tiles = jnp.concatenate([tiles[places[index]] for index in down], axis=1)
        grad_in = jnp.concatenate([tokens_at(token_refs, columns[index]) for index in down], axis=1)
        return places, columns, grad_in, dot(grad_in, down_tiles, TURNED)

    def rest(block, places, columns, grad_in, hidden_grad):
        gate_grad = (hidden_grad * gate_slope[block]).astype(BF16)
        up_grad = (hidden_grad * gate_act[block]).astype(BF16)
        down_terms = dot(hidden_turned[block], grad_in, PLAIN) * grad_scale
        for at, index in enumerate(down):
            sums[places[index]] = down_terms[:, at * tile : (at + 1) * tile]
        for indices, grad in ((gate, gate_grad), (up, up_grad)):
            weights = jnp.concatenate([tiles[places[index]] for index in indices], axis=0)
            back = dot(grad, weights, TURNED)
            turned = jnp.concatenate([x_turned[columns[index], :] for index in indices], axis=0)
            terms = dot(turned, grad, PLAIN) * grad_scale
            for at, index in enumerate(indices):
                sums[places[index]] = terms[at * tile : (at + 1) * tile]
                input_sum[:, columns[index]] += back[:, at * tile : (at + 1) * tile]

    in_turn(first, rest, gate_slope.shape[0])
    store_parts(input_sum, input_own, input_other, parts)
    for ref, part in zip(grad_refs, weight_parts):
        share = ref.shape[2]
        for at in range(part[2]):
            offset = offset_of(table, part, at, near, share)
            ref[at] = sums[:, pl.ds(offset, share), :].astype(BF16)


def fold(table, part_1, part_2, got_1, got_2, out_1, out_2):
    half = got_1.shape[0]
    out_2[:half] = add(part_2[:half], got_1[...])
    out_2[half:] = part_2[half:]
    out_1[:half] = part_1[:half]
    out_1[half:] = add(part_1[half:], got_2[...])


def call(kernel, table, args, in_specs, out_specs, out_shape, grid=1, scratch=(), cost=0, vmem=40):
    return pl.pallas_call(
        kernel,
        grid_spec=pltpu.PrefetchScalarGridSpec(
            num_scalar_prefetch=1,
            grid=(grid,),
            in_specs=in_specs,
            out_specs=out_specs,
            scratch_shapes=scratch,
        ),
        out_shape=out_shape,
        compiler_params=pltpu.CompilerParams(vmem_limit_bytes=vmem * MIB),
        cost_estimate=pl.CostEstimate(flops=0, bytes_accessed=cost, transcendentals=0),
    )(table, *args)


def shards(tokens, out_grad, weight_tiles, tile_counts, tile_rows):
    row_share, _, blocks_dev, slot_count, tile = weight_tiles.shape
    own_rows, features = tokens.shape
    dp_size, tensor_size = lax.axis_size("dp"), lax.axis_size("tensor")
    far = math.gcd(4, math.gcd(dp_size, blocks_dev))
    near = dp_size // far
    blocks = blocks_dev // far
    terms = 3 * slot_count
    grad_scale = 1.0 / math.sqrt(own_rows * tensor_size * dp_size)
    me = lax.axis_index("dp")
    far_at, near_at = me // near, me % near
    far_strides, near_strides = strides_of(far, near), strides_of(near)
    tensor_strides = strides_of(tensor_size)
    shape = jax.ShapeDtypeStruct

    x_items, g_items = {0: tokens}, {0: out_grad}
    capacity = (terms * blocks_dev - 3 * blocks_dev + 3 * (slot_count - 1) * (far - 1)) // far
    slots = capacity + 1
    block_ids = jnp.arange(blocks_dev, dtype=jnp.int32)
    load = tile_counts[0] + tile_counts[1] + tile_counts[2]
    earlier = (load[:, None] > load[None, :]) | (
        (load[:, None] == load[None, :]) & (block_ids[:, None] < block_ids[None, :])
    )
    rank = jnp.sum(earlier.astype(jnp.int32), axis=0)
    home = rank % far
    before = (home[:, None] == home[None, :]) & (rank[:, None] < rank[None, :])
    start = jnp.sum(jnp.where(before, load[:, None], 0), axis=0)
    ranks_of = (
        jnp.arange(blocks, dtype=jnp.int32)[None, :] * far
        + (jnp.arange(far, dtype=jnp.int32)[:, None] ^ far_at)
    ).reshape(blocks_dev)
    columns = jnp.concatenate(
        [
            block_ids[None, :],
            start[None, :],
            (start + tile_counts[0])[None, :],
            (start + tile_counts[0] + tile_counts[1])[None, :],
            tile_counts,
            jnp.transpose(tile_rows, (0, 2, 1)).reshape(terms, blocks_dev),
        ]
    )
    table = jnp.sum(
        jnp.where(ranks_of[None, :, None] == rank[None, None, :], columns[:, None, :], 0), axis=2
    )
    place = jnp.where(block_ids == 0, far_at, near_at).astype(jnp.int32)
    table = jnp.concatenate([table, place[None, :]])

    tile_lines = jnp.transpose(weight_tiles, (0, 1, 3, 2, 4)).reshape(
        row_share, terms, blocks_dev, tile
    )
    packed_shape = (slots, row_share, tile)
    packed = call(
        functools.partial(pack, blocks=blocks, slot_count=slot_count),
        table,
        [tile_lines],
        [whole(tile_lines.shape)],
        [whole(packed_shape)] * far,
        [shape(packed_shape, BF16)] * far,
        scratch=[pltpu.VMEM((row_share * terms * blocks_dev, tile), F32)],
        cost=1_000_000,
        vmem=24,
    )
    staged = tensor_size == 2 and far == 4 and near == 4
    received = [swap(packed[at], "dp", at * near) for at in reversed(range(1, far))][::-1]
    held = jnp.stack([packed[0], *received])
    if staged:
        x_items[near] = swap(after(tokens, received[-1]), "dp", near)
        x_core, g_core = swap(tokens, "tensor", 1), swap(out_grad, "tensor", 1)
        held = after(held, x_core, g_core, x_items[near])

    half = far // 2
    split = near == 4 and far % 2 == 0
    if split:
        from_1, from_2 = swap(held, "dp", 1), swap(held, "dp", 2)
        pass_1, pass_2 = from_1[:half], from_2[half:]
        weight_list = [held, from_1, from_2, swap(pass_1, "dp", 2), swap(pass_2, "dp", 1)]
        weight_parts = [(0, 0, far), (1, 0, far), (2, 0, far), (3, 0, half), (3, half, half)]
    else:
        items = gather({0: held}, "dp", near_strides)
        pass_1 = pass_2 = held
        weight_list = [items[at] for at in range(near)]
        weight_parts = [(at, 0, far) for at in range(near)]

    if staged:
        x_source, g_source = after((tokens, out_grad), held)
        x_items[2 * near] = swap(x_source, "dp", 2 * near)
        g_items[near] = swap(g_source, "dp", near)
        x_source, g_source = after(
            (x_items[2 * near], out_grad), x_items[2 * near], x_items[near], g_items[near]
        )
        x_items[3 * near] = swap(x_source, "dp", near)
        g_items[2 * near] = swap(g_source, "dp", 2 * near)
        g_items[3 * near] = swap(g_items[2 * near], "dp", near)
        x_late = jnp.concatenate([x_items[at * near] for at in range(1, far)])
        x_late = swap(after(x_late, *weight_list[3:], g_items[2 * near]), "tensor", 1)
        g_late = jnp.concatenate([g_items[at * near] for at in range(1, far)])
        g_late = swap(g_late, "tensor", 1)
    else:
        for items, value in ((x_items, tokens), (g_items, out_grad)):
            items.update(gather({0: value}, "dp", far_strides))

    far_order = [at * near for at in range(0, far, 2)] + [at * near for at in range(1, far, 2)]
    if staged:
        order = [at * near for at in range(far)]
        x_list = [x_items[at] for at in order] + [x_core, x_late]
        g_list = [g_items[at] for at in order] + [g_core, g_late]
        parts = [(other, far_order.index(at)) for other in (False, True) for at in order]
        other_parts = [(at, 1) for at in far_order]
    else:
        x_list, g_list, parts, other_parts = [], [], [], []
        for place, at in enumerate(far_order):
            x_parts = gather({0: x_items[at]}, "tensor", tensor_strides)
            g_parts = gather({0: g_items[at]}, "tensor", tensor_strides)
            for other in x_parts:
                parts.append((other != 0, len(other_parts) if other else place))
                if other:
                    other_parts.append((at, other))
                x_list.append(x_parts[other])
                g_list.append(g_parts[other])

    group_rows = far * tensor_size * own_rows
    own_shape = (far, own_rows, features)
    other_shape = (len(other_parts), own_rows, features)
    steps = 2 if slots % 2 == 0 else 1
    tiles_shape = (slots, tile, tile)
    tiles = call(
        functools.partial(assemble, weight_parts=weight_parts, near=near),
        table,
        weight_list,
        [
            pl.BlockSpec((length, slots // steps, row_share, tile), lambda step, *_: (0, step, 0, 0))
            for _, _, length in weight_parts
        ],
        pl.BlockSpec((slots // steps, tile, tile), lambda step, *_: (step, 0, 0)),
        shape(tiles_shape, BF16),
        grid=steps,
        scratch=[pltpu.VMEM((slots // steps, tile, tile), F32)],
        cost=10_000_000,
        vmem=24,
    )
    def specs_of(*groups):
        return [whole(one.shape) for group in groups for one in group]

    middle_shapes = [
        shape((features, group_rows), BF16),
        shape((blocks, group_rows, tile), F32),
        shape((blocks, group_rows, tile), F32),
        shape((blocks, tile, group_rows), BF16),
    ]
    sum_shapes = [shape(own_shape, BF16), shape(other_shape, BF16)]
    outs = call(
        functools.partial(ahead, token_count=len(x_list), slot_count=slot_count, parts=parts),
        table,
        [*x_list, tiles],
        specs_of(x_list, [tiles]),
        specs_of(middle_shapes, sum_shapes),
        middle_shapes + sum_shapes,
        scratch=[pltpu.VMEM((group_rows, features), F32)],
        cost=30_000_000,
    )
    middle, (ffn_own, ffn_other) = outs[:4], outs[4:]

    def to_near(own_sums, other_sums):
        from_core = swap(other_sums, "tensor", 1)
        return from_core, add(own_sums[half:], from_core[half:])

    def to_far(own_sums, from_core, got):
        return add(own_sums[1], from_core[1], got[1])

    def generic(own_sums, other_sums):
        sums = {}
        for index, at in enumerate(far_order):
            items = {0: own_sums[index]}
            for other_index, (far_part, other) in enumerate(other_parts):
                if far_part == at:
                    items[other] = other_sums[other_index]
            sums[at] = scatter(items, "tensor", tensor_strides)[0]
        return scatter(sums, "dp", far_strides)[0]

    if staged:
        ffn_core, ffn_near = to_near(ffn_own, after(ffn_other, g_items[3 * near]))
        middle = after(tuple(middle), ffn_near)
    part_shapes = [shape((length,) + packed_shape, BF16) for _, _, length in weight_parts]
    outs = call(
        functools.partial(
            behind,
            token_count=len(g_list),
            weight_parts=weight_parts,
            slot_count=slot_count,
            grad_scale=grad_scale,
            near=near,
            parts=parts,
        ),
        table,
        [*g_list, tiles, *middle],
        specs_of(g_list, [tiles], middle),
        specs_of(sum_shapes, part_shapes),
        sum_shapes + part_shapes,
        scratch=[pltpu.VMEM((group_rows, features), F32), pltpu.VMEM(tiles_shape, F32)],
        cost=40_000_000,
    )
    (input_own, input_other), tile_terms = outs[:2], outs[2:]

    def halves(parts):
        return swap(parts[3], "dp", 1), swap(parts[4], "dp", 2)

    def folded(parts, got_1, got_2):
        args = [parts[1], parts[2], got_1, got_2]
        out_shapes = [shape(parts[1].shape, BF16)] * 2
        return call(
            fold, table, args, specs_of(args), specs_of(out_shapes), out_shapes, cost=40_000_000, vmem=16
        )

    def summed(parts, to_1, to_2):
        from_1, from_2 = swap(to_1, "dp", 1), swap(to_2, "dp", 2)
        return [add(parts[0][at], from_1[at], from_2[at]) for at in range(far)]

    def sent_back(sums):
        return [sums[0]] + [swap(sums[at], "dp", at * near) for at in range(1, far)]

    if staged:
        ffn_got = swap(ffn_near, "dp", near)
        input_other = after(input_other, ffn_got)
        got = halves(tile_terms)
        ffn_last = to_far(ffn_own, ffn_core, ffn_got)
        ffn_far = swap(ffn_last, "dp", 2 * near)
        input_core, input_near = to_near(input_own, input_other)
        input_got = swap(input_near, "dp", near)
        to_1, to_2 = folded(after(tile_terms, ffn_last, input_near), *got)
        input_last = after(to_far(input_own, input_core, input_got), ffn_far)
        input_far = swap(input_last, "dp", 2 * near)
        sums = after(tuple(summed(tile_terms, to_1, to_2)), input_last)
        back = list(after(tuple(sent_back(sums)), input_far))
        ffn_rows = add(ffn_own[0], ffn_core[0], ffn_got[0], ffn_far)
        input_rows = add(input_own[0], input_core[0], input_got[0], input_far)
    else:
        if split:
            sums = summed(tile_terms, *folded(tile_terms, *halves(tile_terms)))
        else:
            sums = scatter(dict(enumerate(tile_terms)), "dp", near_strides)[0]
        back = sent_back(sums)
        ffn_rows = generic(ffn_own, ffn_other)
        input_rows = generic(input_own, input_other)

    grads = call(
        functools.partial(
            unpack, blocks=blocks, slot_count=slot_count
        ),
        table,
        back,
        specs_of(back),
        whole(tile_lines.shape),
        shape(tile_lines.shape, BF16),
        scratch=[pltpu.VMEM((row_share * terms * blocks_dev, tile), F32)],
        cost=2_000_000,
        vmem=24,
    )
    tile_grad = jnp.transpose(
        grads.reshape(row_share, 3, slot_count, blocks_dev, tile), (0, 1, 3, 2, 4)
    )
    return ffn_rows, input_rows, tile_grad


def solution(mesh):
    return jax.shard_map(
        shards,
        mesh=mesh,
        in_specs=(
            P(("dp", "tensor"), None),
            P(("dp", "tensor"), None),
            P("dp", None, "tensor", None, None),
            P(None, "tensor"),
            P(None, "tensor", None),
        ),
        out_specs=(
            P(("dp", "tensor"), None),
            P(("dp", "tensor"), None),
            P("dp", None, "tensor", None, None),
        ),
        check_vma=False,
    )
```

```python
import functools
import math

import jax
import jax.numpy as jnp
from jax import lax
from jax.experimental import pallas as pl
from jax.experimental.pallas import tpu as pltpu
from jax.sharding import PartitionSpec as P

F32 = jnp.float32
BF16 = jnp.bfloat16
PLAIN = (((1,), (0,)), ((), ()))
TURNED = (((1,), (1,)), ((), ()))
MIB = 1024 * 1024
UNROLL = 14
dot = functools.partial(lax.dot_general, preferred_element_type=F32)


def swap(value, axis, stride):
    size = lax.axis_size(axis)
    return lax.ppermute(value, axis, [(at, at ^ stride) for at in range(size)])


def after(value, *others):
    return lax.optimization_barrier((value, *others))[0]


def add(first, *others):
    total = first.astype(F32)
    for other in others:
        total = total + other.astype(F32)
    return total.astype(BF16)


def strides_of(size, unit=1):
    found = []
    step = size // 2
    while step >= 1:
        found.append(step * unit)
        step //= 2
    return found


def gather(items, axis, strides):
    for stride in strides:
        items = {**items, **{at ^ stride: swap(one, axis, stride) for at, one in items.items()}}
    return items


def scatter(items, axis, strides):
    for stride in reversed(strides):
        kept = {}
        for at, one in items.items():
            if not at & stride:
                kept[at] = add(one, swap(items[at ^ stride], axis, stride))
        items = kept
    return items


def whole(shape):
    return pl.BlockSpec(shape, lambda *_: (0,) * len(shape), pipeline_mode=pl.Buffered(1))


def pack(table, tiles, *refs, blocks, slot_count):
    outs, lines = refs[:-1], refs[-1]
    spare = outs[0].shape[0] - 1
    share, terms, blocks_dev, _ = tiles.shape
    for row in range(share):
        for term in range(terms):
            at = (row * terms + term) * blocks_dev
            lines[at : at + blocks_dev, :] = tiles[row, term].astype(F32)
    for at, out in enumerate(outs):

        def one(place, _, at=at, out=out):
            column = at * blocks + place
            block = table[0, column]
            for matrix in range(3):
                first, count = table[1 + matrix, column], table[4 + matrix, column]
                for slot in range(slot_count):
                    to = jnp.where(slot < count, first + slot, spare)
                    source = (matrix * slot_count + slot) * blocks_dev + block
                    out[to] = lines[pl.ds(source, share, stride=terms * blocks_dev), :].astype(BF16)
            return _

        lax.fori_loop(0, blocks, one, 0, unroll=True)


def unpack(table, *refs, blocks, slot_count):
    out, lines, sources = refs[-2], refs[-1], refs[:-2]
    share, terms, blocks_dev, _ = out.shape
    for at, ref in enumerate(sources):

        def one(place, _, at=at, ref=ref):
            column = at * blocks + place
            block = table[0, column]
            for matrix in range(3):
                first, count = table[1 + matrix, column], table[4 + matrix, column]
                for slot in range(slot_count):
                    live = slot < count
                    value = ref[jnp.where(live, first + slot, 0)].astype(F32)
                    target = (matrix * slot_count + slot) * blocks_dev + block
                    lines[pl.ds(target, share, stride=terms * blocks_dev), :] = jnp.where(
                        live, value, 0.0
                    )
            return _

        lax.fori_loop(0, blocks, one, 0, unroll=True)
    for row in range(share):
        for term in range(terms):
            at = (row * terms + term) * blocks_dev
            out[row, term] = lines[at : at + blocks_dev, :].astype(BF16)


def offset_of(table, part, at, near, share):
    far_part = (part[1] + at) ^ table[16, 0]
    near_part = part[0] ^ table[16, 1]
    return pl.multiple_of((far_part * near + near_part) * share, share)


def assemble(table, *refs, weight_parts, near):
    weight_refs, out, tiles = refs[: len(weight_parts)], refs[-2], refs[-1]
    for ref, part in zip(weight_refs, weight_parts):
        share = ref.shape[2]
        for at in range(part[2]):
            offset = offset_of(table, part, at, near, share)
            tiles[:, pl.ds(offset, share), :] = ref[at].astype(F32)
    out[...] = tiles[...].astype(BF16)

    @pl.when(pl.program_id(0) == pl.num_programs(0) - 1)
    def _():
        out[out.shape[0] - 1] = jnp.zeros(out.shape[1:], BF16)


def places_of(table, block, slot_count, spare):
    places = []
    for matrix in range(3):
        first, count = table[1 + matrix, block], table[4 + matrix, block]
        places += [jnp.where(slot < count, first + slot, spare) for slot in range(slot_count)]
    return places


def store_parts(total, own, other, parts):
    own_rows = own.shape[1]
    for at, (is_other, place) in enumerate(parts):
        ref = other if is_other else own
        ref[place] = total[at * own_rows : (at + 1) * own_rows, :].astype(BF16)


def tokens_at(refs, columns):
    return jnp.concatenate([ref[:, columns] for ref in refs], axis=0)


def columns_of(table, block, index, tile):
    return pl.ds(pl.multiple_of(table[7 + index, block] * tile, tile), tile)


def triples(slot_count):
    return [range(at * slot_count, (at + 1) * slot_count) for at in range(3)]


def in_turn(first, rest, blocks):
    group = max(size for size in range(1, UNROLL + 1) if blocks % size == 0)

    def some(at, _):
        held = first(at * group)
        for block in range(group):
            following = first(at * group + block + 1) if block + 1 < group else None
            rest(at * group + block, *held)
            held = following
        return _

    lax.fori_loop(0, blocks // group, some, 0)


def ahead(table, *refs, token_count, slot_count, parts):
    token_refs, refs = refs[:token_count], refs[token_count:]
    tiles, x_turned, gate_slope, gate_act_out, hidden_turned, ffn_own, ffn_other, ffn_sum = refs
    tile = tiles.shape[1]
    gate, up, down = triples(slot_count)

    for at in range(x_turned.shape[0] // tile):
        here = slice(at * tile, (at + 1) * tile)
        x_turned[here, :] = tokens_at(token_refs, here).T
    ffn_sum[...] = jnp.zeros_like(ffn_sum)

    def first(block):
        places = places_of(table, block, slot_count, tiles.shape[0] - 1)
        sums = []
        for indices in (gate, up):
            columns = [columns_of(table, block, index, tile) for index in indices]
            values = jnp.concatenate([tokens_at(token_refs, column) for column in columns], axis=1)
            weights = jnp.concatenate([tiles[places[index]] for index in indices], axis=0)
            sums.append(dot(values, weights, PLAIN))
        return places, *sums

    def rest(block, places, gate_pre, up_pre):
        gate_sig = jax.nn.sigmoid(gate_pre)
        gate_act = gate_pre * gate_sig
        hidden = (gate_act * up_pre).astype(BF16)
        gate_slope[block] = up_pre * gate_sig * (1.0 + gate_pre * (1.0 - gate_sig))
        gate_act_out[block] = gate_act
        hidden_turned[block] = hidden.T
        down_tiles = jnp.concatenate([tiles[places[index]] for index in down], axis=1)
        ffn = dot(hidden, down_tiles, PLAIN)
        for at, index in enumerate(down):
            ffn_sum[:, columns_of(table, block, index, tile)] += ffn[:, at * tile : (at + 1) * tile]

    in_turn(first, rest, gate_slope.shape[0])
    store_parts(ffn_sum, ffn_own, ffn_other, parts)


def behind(table, *refs, token_count, weight_parts, slot_count, grad_scale, near, parts):
    token_refs, refs = refs[:token_count], refs[token_count:]
    tiles, x_turned, gate_slope, gate_act, hidden_turned, input_own, input_other = refs[:7]
    grad_refs, input_sum, sums = refs[7:-2], refs[-2], refs[-1]
    tile = tiles.shape[1]
    gate, up, down = triples(slot_count)
    input_sum[...] = jnp.zeros_like(input_sum)

    def first(block):
        places = places_of(table, block, slot_count, tiles.shape[0] - 1)
        columns = [columns_of(table, block, index, tile) for index in range(3 * slot_count)]
        down_tiles = jnp.concatenate([tiles[places[index]] for index in down], axis=1)
        grad_in = jnp.concatenate([tokens_at(token_refs, columns[index]) for index in down], axis=1)
        return places, columns, grad_in, dot(grad_in, down_tiles, TURNED)

    def rest(block, places, columns, grad_in, hidden_grad):
        gate_grad = (hidden_grad * gate_slope[block]).astype(BF16)
        up_grad = (hidden_grad * gate_act[block]).astype(BF16)
        down_terms = dot(hidden_turned[block], grad_in, PLAIN) * grad_scale
        for at, index in enumerate(down):
            sums[places[index]] = down_terms[:, at * tile : (at + 1) * tile]
        for indices, grad in ((gate, gate_grad), (up, up_grad)):
            weights = jnp.concatenate([tiles[places[index]] for index in indices], axis=0)
            back = dot(grad, weights, TURNED)
            turned = jnp.concatenate([x_turned[columns[index], :] for index in indices], axis=0)
            terms = dot(turned, grad, PLAIN) * grad_scale
            for at, index in enumerate(indices):
                sums[places[index]] = terms[at * tile : (at + 1) * tile]
                input_sum[:, columns[index]] += back[:, at * tile : (at + 1) * tile]

    in_turn(first, rest, gate_slope.shape[0])
    store_parts(input_sum, input_own, input_other, parts)
    for ref, part in zip(grad_refs, weight_parts):
        share = ref.shape[2]
        for at in range(part[2]):
            offset = offset_of(table, part, at, near, share)
            ref[at] = sums[:, pl.ds(offset, share), :].astype(BF16)


def fold(table, part_1, part_2, got_1, got_2, out_1, out_2):
    half = got_1.shape[0]
    out_2[:half] = add(part_2[:half], got_1[...])
    out_2[half:] = part_2[half:]
    out_1[:half] = part_1[:half]
    out_1[half:] = add(part_1[half:], got_2[...])


def call(kernel, table, args, in_specs, out_specs, out_shape, grid=1, scratch=(), cost=0, vmem=40):
    return pl.pallas_call(
        kernel,
        grid_spec=pltpu.PrefetchScalarGridSpec(
            num_scalar_prefetch=1,
            grid=(grid,),
            in_specs=in_specs,
            out_specs=out_specs,
            scratch_shapes=scratch,
        ),
        out_shape=out_shape,
        compiler_params=pltpu.CompilerParams(vmem_limit_bytes=vmem * MIB),
        cost_estimate=pl.CostEstimate(flops=0, bytes_accessed=cost, transcendentals=0),
    )(table, *args)


def shards(tokens, out_grad, weight_tiles, tile_counts, tile_rows):
    row_share, _, blocks_dev, slot_count, tile = weight_tiles.shape
    own_rows, features = tokens.shape
    dp_size, tensor_size = lax.axis_size("dp"), lax.axis_size("tensor")
    far = math.gcd(4, math.gcd(dp_size, blocks_dev))
    near = dp_size // far
    blocks = blocks_dev // far
    terms = 3 * slot_count
    grad_scale = 1.0 / math.sqrt(own_rows * tensor_size * dp_size)
    me = lax.axis_index("dp")
    far_at, near_at = me // near, me % near
    far_strides, near_strides = strides_of(far, near), strides_of(near)
    tensor_strides = strides_of(tensor_size)
    shape = jax.ShapeDtypeStruct

    x_items, g_items = {0: tokens}, {0: out_grad}
    if far > 1:
        x_items[near] = swap(tokens, "dp", near)

    capacity = (terms * blocks_dev - 3 * blocks_dev + 3 * (slot_count - 1) * (far - 1)) // far
    slots = capacity + 1
    block_ids = jnp.arange(blocks_dev, dtype=jnp.int32)
    load = tile_counts[0] + tile_counts[1] + tile_counts[2]
    earlier = (load[:, None] > load[None, :]) | (
        (load[:, None] == load[None, :]) & (block_ids[:, None] < block_ids[None, :])
    )
    rank = jnp.sum(earlier.astype(jnp.int32), axis=0)
    home = rank % far
    before = (home[:, None] == home[None, :]) & (rank[:, None] < rank[None, :])
    start = jnp.sum(jnp.where(before, load[:, None], 0), axis=0)
    ranks_of = (
        jnp.arange(blocks, dtype=jnp.int32)[None, :] * far
        + (jnp.arange(far, dtype=jnp.int32)[:, None] ^ far_at)
    ).reshape(blocks_dev)
    columns = jnp.concatenate(
        [
            block_ids[None, :],
            start[None, :],
            (start + tile_counts[0])[None, :],
            (start + tile_counts[0] + tile_counts[1])[None, :],
            tile_counts,
            jnp.transpose(tile_rows, (0, 2, 1)).reshape(terms, blocks_dev),
        ]
    )
    table = jnp.sum(
        jnp.where(ranks_of[None, :, None] == rank[None, None, :], columns[:, None, :], 0), axis=2
    )
    place = jnp.where(block_ids == 0, far_at, near_at).astype(jnp.int32)
    table = jnp.concatenate([table, place[None, :]])

    tile_lines = jnp.transpose(weight_tiles, (0, 1, 3, 2, 4)).reshape(
        row_share, terms, blocks_dev, tile
    )
    packed_shape = (slots, row_share, tile)
    packed = call(
        functools.partial(pack, blocks=blocks, slot_count=slot_count),
        table,
        [tile_lines],
        [whole(tile_lines.shape)],
        [whole(packed_shape)] * far,
        [shape(packed_shape, BF16)] * far,
        scratch=[pltpu.VMEM((row_share * terms * blocks_dev, tile), F32)],
        cost=1_000_000,
        vmem=24,
    )
    staged = tensor_size == 2 and far == 4 and near == 4
    received = [swap(packed[at], "dp", at * near) for at in reversed(range(1, far))][::-1]
    held = jnp.stack([packed[0], *received])
    x_core, g_core = {}, {}
    if staged:
        x_core = {at: swap(x_items[at], "tensor", 1) for at in (0, near)}
        g_core = {0: swap(out_grad, "tensor", 1)}
        held = after(held, *x_core.values(), *g_core.values())

    half = far // 2
    split = near == 4 and far % 2 == 0
    if split:
        from_1, from_2 = swap(held, "dp", 1), swap(held, "dp", 2)
        pass_1, pass_2 = from_1[:half], from_2[half:]
        weight_list = [held, from_1, from_2, swap(pass_1, "dp", 2), swap(pass_2, "dp", 1)]
        weight_parts = [(0, 0, far), (1, 0, far), (2, 0, far), (3, 0, half), (3, half, half)]
    else:
        items = gather({0: held}, "dp", near_strides)
        pass_1 = pass_2 = held
        weight_list = [items[at] for at in range(near)]
        weight_parts = [(at, 0, far) for at in range(near)]

    if staged:
        x_source, g_source = after((tokens, out_grad), held)
        x_items[2 * near] = swap(x_source, "dp", 2 * near)
        g_items[near] = swap(g_source, "dp", near)
        x_source, g_source = after((x_items[2 * near], out_grad), x_items[2 * near], g_items[near])
        x_items[3 * near] = swap(x_source, "dp", near)
        g_items[2 * near] = swap(g_source, "dp", 2 * near)
        g_items[3 * near] = swap(g_items[2 * near], "dp", near)
        x_late = jnp.concatenate([x_items[2 * near], x_items[3 * near]])
        x_late = swap(after(x_late, *weight_list[3:], g_items[2 * near]), "tensor", 1)
        g_late = jnp.concatenate([g_items[at * near] for at in range(1, far)])
        g_late = swap(g_late, "tensor", 1)
    else:
        for items, value in ((x_items, tokens), (g_items, out_grad)):
            items.update(gather({0: value}, "dp", far_strides))

    far_order = [at * near for at in range(0, far, 2)] + [at * near for at in range(1, far, 2)]
    if staged:
        order = [at * near for at in range(far)]
        x_list = [x_items[at] for at in order] + [x_core[at] for at in order[:2]] + [x_late]
        g_list = [g_items[at] for at in order] + [g_core[0], g_late]
        parts = [(other, far_order.index(at)) for other in (False, True) for at in order]
        other_parts = [(at, 1) for at in far_order]
    else:
        x_list, g_list, parts, other_parts = [], [], [], []
        for place, at in enumerate(far_order):
            x_parts = gather({0: x_items[at]}, "tensor", tensor_strides)
            g_parts = gather({0: g_items[at]}, "tensor", tensor_strides)
            for other in x_parts:
                parts.append((other != 0, len(other_parts) if other else place))
                if other:
                    other_parts.append((at, other))
                x_list.append(x_parts[other])
                g_list.append(g_parts[other])

    group_rows = far * tensor_size * own_rows
    own_shape = (far, own_rows, features)
    other_shape = (len(other_parts), own_rows, features)
    steps = 2 if slots % 2 == 0 else 1
    tiles_shape = (slots, tile, tile)
    tiles = call(
        functools.partial(assemble, weight_parts=weight_parts, near=near),
        table,
        weight_list,
        [
            pl.BlockSpec((length, slots // steps, row_share, tile), lambda step, *_: (0, step, 0, 0))
            for _, _, length in weight_parts
        ],
        pl.BlockSpec((slots // steps, tile, tile), lambda step, *_: (step, 0, 0)),
        shape(tiles_shape, BF16),
        grid=steps,
        scratch=[pltpu.VMEM((slots // steps, tile, tile), F32)],
        cost=10_000_000,
        vmem=24,
    )
    def specs_of(*groups):
        return [whole(one.shape) for group in groups for one in group]

    middle_shapes = [
        shape((features, group_rows), BF16),
        shape((blocks, group_rows, tile), F32),
        shape((blocks, group_rows, tile), F32),
        shape((blocks, tile, group_rows), BF16),
    ]
    sum_shapes = [shape(own_shape, BF16), shape(other_shape, BF16)]
    outs = call(
        functools.partial(ahead, token_count=len(x_list), slot_count=slot_count, parts=parts),
        table,
        [*x_list, tiles],
        specs_of(x_list, [tiles]),
        specs_of(middle_shapes, sum_shapes),
        middle_shapes + sum_shapes,
        scratch=[pltpu.VMEM((group_rows, features), F32)],
        cost=30_000_000,
    )
    middle, (ffn_own, ffn_other) = outs[:4], outs[4:]

    def to_near(own_sums, other_sums):
        from_core = swap(other_sums, "tensor", 1)
        return from_core, add(own_sums[half:], from_core[half:])

    def to_far(own_sums, from_core, got):
        return add(own_sums[1], from_core[1], got[1])

    def generic(own_sums, other_sums):
        sums = {}
        for index, at in enumerate(far_order):
            items = {0: own_sums[index]}
            for other_index, (far_part, other) in enumerate(other_parts):
                if far_part == at:
                    items[other] = other_sums[other_index]
            sums[at] = scatter(items, "tensor", tensor_strides)[0]
        return scatter(sums, "dp", far_strides)[0]

    if staged:
        ffn_core, ffn_near = to_near(ffn_own, after(ffn_other, g_items[3 * near]))
        middle = after(tuple(middle), ffn_near)
    part_shapes = [shape((length,) + packed_shape, BF16) for _, _, length in weight_parts]
    outs = call(
        functools.partial(
            behind,
            token_count=len(g_list),
            weight_parts=weight_parts,
            slot_count=slot_count,
            grad_scale=grad_scale,
            near=near,
            parts=parts,
        ),
        table,
        [*g_list, tiles, *middle],
        specs_of(g_list, [tiles], middle),
        specs_of(sum_shapes, part_shapes),
        sum_shapes + part_shapes,
        scratch=[pltpu.VMEM((group_rows, features), F32), pltpu.VMEM(tiles_shape, F32)],
        cost=40_000_000,
    )
    (input_own, input_other), tile_terms = outs[:2], outs[2:]

    def halves(parts):
        return swap(parts[3], "dp", 1), swap(parts[4], "dp", 2)

    def folded(parts, got_1, got_2):
        args = [parts[1], parts[2], got_1, got_2]
        out_shapes = [shape(parts[1].shape, BF16)] * 2
        return call(
            fold, table, args, specs_of(args), specs_of(out_shapes), out_shapes, cost=40_000_000, vmem=16
        )

    def summed(parts, to_1, to_2):
        from_1, from_2 = swap(to_1, "dp", 1), swap(to_2, "dp", 2)
        return [add(parts[0][at], from_1[at], from_2[at]) for at in range(far)]

    def sent_back(sums):
        return [sums[0]] + [swap(sums[at], "dp", at * near) for at in range(1, far)]

    if staged:
        ffn_got = swap(ffn_near, "dp", near)
        input_other = after(input_other, ffn_got)
        got = halves(tile_terms)
        ffn_last = to_far(ffn_own, ffn_core, ffn_got)
        ffn_far = swap(ffn_last, "dp", 2 * near)
        input_core, input_near = to_near(input_own, input_other)
        input_got = swap(input_near, "dp", near)
        to_1, to_2 = folded(after(tile_terms, ffn_last, input_near), *got)
        input_last = after(to_far(input_own, input_core, input_got), ffn_far)
        input_far = swap(input_last, "dp", 2 * near)
        sums = after(tuple(summed(tile_terms, to_1, to_2)), input_last)
        back = list(after(tuple(sent_back(sums)), input_far))
        ffn_rows = add(ffn_own[0], ffn_core[0], ffn_got[0], ffn_far)
        input_rows = add(input_own[0], input_core[0], input_got[0], input_far)
    else:
        if split:
            sums = summed(tile_terms, *folded(tile_terms, *halves(tile_terms)))
        else:
            sums = scatter(dict(enumerate(tile_terms)), "dp", near_strides)[0]
        back = sent_back(sums)
        ffn_rows = generic(ffn_own, ffn_other)
        input_rows = generic(input_own, input_other)

    grads = call(
        functools.partial(
            unpack, blocks=blocks, slot_count=slot_count
        ),
        table,
        back,
        specs_of(back),
        whole(tile_lines.shape),
        shape(tile_lines.shape, BF16),
        scratch=[pltpu.VMEM((row_share * terms * blocks_dev, tile), F32)],
        cost=2_000_000,
        vmem=24,
    )
    tile_grad = jnp.transpose(
        grads.reshape(row_share, 3, slot_count, blocks_dev, tile), (0, 1, 3, 2, 4)
    )
    return ffn_rows, input_rows, tile_grad


def solution(mesh):
    return jax.shard_map(
        shards,
        mesh=mesh,
        in_specs=(
            P(("dp", "tensor"), None),
            P(("dp", "tensor"), None),
            P("dp", None, "tensor", None, None),
            P(None, "tensor"),
            P(None, "tensor", None),
        ),
        out_specs=(
            P(("dp", "tensor"), None),
            P(("dp", "tensor"), None),
            P("dp", None, "tensor", None, None),
        ),
        check_vma=False,
    )
```
